32 devices in a mesh: section: 2 (over x), seq: 4 (over y, core), dp: 4 (over z).
Axes of the slice: x: 2, y: 2, z: 4, core: 2. Of those that a mesh axis runs over, the one named last changes fastest.
Arguments:
- inputs: bfloat16 [16, 512, 768], P('dp', 'seq'), may hold values from -6 to 6
- cotangent: bfloat16 [16, 512, 768], P('dp', 'seq'), may hold values from -6 to 6
- lengths: int32 [16], P('dp'), may hold values from 60 to 512, as said below
- w_qkv: bfloat16 [2, 768, 2304], P('section'), may hold values from -0.21875 to 0.21875
- attn_bias: bfloat16 [2, 1536], P('section'), may hold values from -3 to 3
- w_out: bfloat16 [2, 768, 768], P('section'), may hold values from -0.875 to 0.875
- out_bias: bfloat16 [2, 1536], P('section'), may hold values from -2 to 2
- w_up: bfloat16 [2, 768, 3072], P('section'), may hold values from -0.21875 to 0.21875
- bias_up: bfloat16 [2, 3072], P('section'), may hold values from -3 to 3
- w_down: bfloat16 [2, 3072, 768], P('section'), may hold values from -0.109375 to 0.109375
- norm_gain: bfloat16 [2, 1536], P('section'), may hold values from 0.5 to 1.5
- norm_bias: bfloat16 [2, 1536], P('section'), may hold values from -2 to 2
Outputs:
- section_out: bfloat16 [2, 16, 512, 768], P('section', 'dp', 'seq')
- section_grad: float32 [2, 16, 512, 768], P('section', 'dp', 'seq')
- grad_w_qkv: float32 [2, 768, 2304], P('section', ('seq', 'dp'))
- grad_attn_bias: float32 [2, 1536], P('section', ('seq', 'dp'))
- grad_w_out: float32 [2, 768, 768], P('section', ('seq', 'dp'))
- grad_out_bias: float32 [2, 1536], P('section', ('seq', 'dp'))
- grad_w_up: float32 [2, 768, 3072], P('section', ('seq', 'dp'))
- grad_bias_up: float32 [2, 3072], P('section', ('seq', 'dp'))
- grad_w_down: float32 [2, 3072, 768], P('section', ('seq', 'dp'))
- grad_norm_gain: float32 [2, 1536], P('section', ('seq', 'dp'))
- grad_norm_bias: float32 [2, 1536], P('section', ('seq', 'dp'))
The draws below stay inside these ranges and needn't reach their ends.
Inputs may be any that keep to these rules, and one draw needn't show every extreme that they name: `lengths`: in each aligned group of 4 tables, one table drawn from the seed has length 512.
All inputs are finite; a program needn't handle non-finite values.
Results may differ from the reference program's by a relative error of at most 0.019.
Values may be sent and summed in bfloat16 or wider, within the bound.
A program may use at most 192 MiB of HBM per device.

```python
import jax
import jax.numpy as jnp
from jax import lax

D = 768
H = 12
FF = 3072
S = 512
MICRO = 2
SEQ_MB = 2
SEQS = 16


def draw_lengths(key, part):
    key = jax.random.fold_in(key, 11)
    shortest = S * 15 // 128
    seq_dev = MICRO * SEQ_MB
    groups = SEQS // seq_dev
    ragged = jax.random.randint(jax.random.fold_in(key, 1), (groups, seq_dev), shortest, S + 1, dtype=jnp.int32)
    chosen = jax.random.randint(jax.random.fold_in(key, 2), (groups, 1), 0, seq_dev, dtype=jnp.int32)
    is_full = jnp.arange(seq_dev, dtype=jnp.int32)[None, :] == chosen
    return jnp.where(is_full, S, ragged).reshape(SEQS).astype(jnp.int32)


def steps_of(stream_key, shape, pieces, smallest, high):
    loudness = 1.0
    for axis_at, blocks in pieces:
        heights = jax.random.uniform(jax.random.fold_in(jax.random.fold_in(stream_key, 6), axis_at), (blocks,), jnp.float32, smallest / len(pieces), high / len(pieces))
        loudness = loudness * jnp.repeat(jnp.exp(heights), shape[axis_at] // blocks).reshape((-1,) + (1,) * (len(shape) - 1 - axis_at))
    return loudness


def noise(stream_key, dims, scale, reach, pieces=(), kind=jnp.bfloat16):
    result = jax.random.normal(stream_key, dims, jnp.float32) * scale
    if len(pieces) > 0:
        result = steps_of(stream_key, dims, pieces, -0.22, 0.18) * result
    return jnp.clip(result, min=-reach, max=reach).astype(kind)


def setup_inputs(seed: int = 0) -> dict:
    keys = jax.random.split(jax.random.key(seed), 13)
    return {
        "inputs": noise(keys[0], (SEQS, S, D), 1.0, 6.0, ((0, 4), (1, 4))),
        "cotangent": noise(keys[1], (SEQS, S, D), 1.0, 6.0, ((0, 4), (1, 4))),
        "lengths": draw_lengths(jax.random.fold_in(keys[12], 71), 0),
        "w_qkv": noise(keys[3], (2, D, 3 * D), D ** -0.5, 0.21875, ((0, 2),)),
        "attn_bias": noise(keys[4], (2, 2 * D), 0.5, 3.0, ((0, 2),)),
        "w_out": noise(keys[5], (2, D, D), (D // 16) ** -0.5, 0.875, ((0, 2),)),
        "out_bias": noise(keys[6], (2, 2 * D), 0.3, 2.0, ((0, 2),)),
        "w_up": noise(keys[7], (2, D, FF), D ** -0.5, 0.21875, ((0, 2),)),
        "bias_up": noise(keys[8], (2, FF), 0.5, 3.0, ((0, 2),)),
        "w_down": noise(keys[9], (2, FF, D), FF ** -0.5, 0.109375, ((0, 2),)),
        "norm_gain": jnp.clip(1.0 + 0.1 * jax.random.normal(keys[10], (2, 2 * D), jnp.float32), 0.5, 1.5).astype(jnp.bfloat16),
        "norm_bias": noise(keys[11], (2, 2 * D), 0.3, 2.0, ((0, 2),)),
    }


EPS = 1e-12
HIGH = lax.Precision.HIGHEST

@jax.custom_vjp
def low(v):
    return lax.optimization_barrier(v.astype(jnp.bfloat16)).astype(jnp.float32)

@jax.custom_vjp
def low_back(v):
    return v

def low_keep(v):
    return (low(v), None)

def low_pass(kept, grad):
    return (grad,)

def back_keep(v):
    return (v, None)

def back_low(kept, grad):
    return (low(grad),)
low.defvjp(low_keep, low_pass)
low_back.defvjp(back_keep, back_low)

def round_both(argument):
    return low_back(low(argument))

def layer_norm(resid, gain, shift):
    average = lax.optimization_barrier(jnp.mean(resid, axis=-1, keepdims=True))
    centred = resid - average
    spread = lax.optimization_barrier(jnp.mean(centred * centred, axis=-1, keepdims=True))
    return centred * lax.rsqrt(spread + EPS) * gain + shift

def encoder_layer(section_in, weights, key_valid):
    w_qkv, attn_bias, w_out, out_bias, w_up, bias_up, w_down, norm_gain, norm_bias = weights
    count, length, width = section_in.shape
    head_dim = width // H
    projected = jnp.einsum('gsd,de->gse', section_in, w_qkv, precision=HIGH)
    queries = round_both(projected[..., :width] + attn_bias[:width])
    key_rows = round_both(projected[..., width:2 * width])
    value_rows = round_both(projected[..., 2 * width:] + attn_bias[width:])
    query_heads = queries.reshape(count, length, H, head_dim)
    key_heads = key_rows.reshape(count, length, H, head_dim)
    value_heads = value_rows.reshape(count, length, H, head_dim)
    scores = low_back(jnp.einsum('gqhe,gkhe->ghqk', query_heads, key_heads, precision=HIGH) * head_dim ** (-0.5))
    scores = jnp.where(key_valid[:, None, None, :], scores, -1e+30)
    row_top = lax.optimization_barrier(jnp.max(scores, axis=-1, keepdims=True))
    exp_scores = jnp.exp(scores - row_top)
    probs = exp_scores / lax.optimization_barrier(jnp.sum(exp_scores, axis=-1, keepdims=True))
    attended = jnp.einsum('ghqk,gkhe->gqhe', low(probs), value_heads, precision=HIGH)
    attended = round_both(attended.reshape(count, length, width))
    branch_one = low_back(jnp.einsum('gsd,de->gse', attended, w_out, precision=HIGH) + out_bias[:width])
    resid_one = section_in + branch_one
    normed_one = layer_norm(resid_one, norm_gain[:width], norm_bias[:width])
    pre_act = low_back(jnp.einsum('gsd,df->gsf', low(normed_one), w_up, precision=HIGH) + bias_up)
    hidden = low(jax.nn.gelu(pre_act, approximate=False))
    branch_two = low_back(jnp.einsum('gsf,fd->gsd', hidden, w_down, precision=HIGH) + out_bias[width:])
    resid_two = normed_one + branch_two
    return layer_norm(resid_two, norm_gain[width:], norm_bias[width:])

def reference(inputs, cotangent, lengths, w_qkv, attn_bias, w_out, out_bias, w_up, bias_up, w_down, norm_gain, norm_bias):
    weights = tuple((entry.astype(jnp.float32) for entry in (w_qkv, attn_bias, w_out, out_bias, w_up, bias_up, w_down, norm_gain, norm_bias)))
    seq_dev = MICRO * SEQ_MB
    groups = SEQS // seq_dev
    stacked_in = inputs.astype(jnp.float32).reshape(groups, seq_dev, S, D)
    stacked_cot = cotangent.astype(jnp.float32).reshape(groups, seq_dev, S, D)
    stacked_len = lengths.reshape(groups, seq_dev)
    positions = jnp.arange(S, dtype=jnp.int32)

    def one_group(totals, group_item):
        block_in, block_cot, block_len = group_item
        key_valid = positions[None, :] < block_len[:, None]

        def forward(first_in, zero_shift, params):
            lower_params = tuple((entry[0] for entry in params))
            upper_params = tuple((entry[1] for entry in params))
            middle = low_back(low(encoder_layer(first_in, lower_params, key_valid)) + zero_shift)
            return (encoder_layer(middle, upper_params, key_valid), middle)
        final, pullback, middle = jax.vjp(forward, block_in, jnp.zeros_like(block_in), weights, has_aux=True)
        masked_cot = block_cot * key_valid[..., None].astype(jnp.float32)
        grad_in, grad_mid, grad_params = pullback(masked_cot)
        totals = jax.tree.map(jnp.add, totals, grad_params)
        return (totals, (middle, final, grad_in, grad_mid))
    starting = tuple((jnp.zeros_like(entry) for entry in weights))
    totals, (middle, final, grad_in, grad_mid) = lax.scan(one_group, starting, (stacked_in, stacked_cot, stacked_len))
    section_out = jnp.stack([middle.reshape(SEQS, S, D), final.reshape(SEQS, S, D)]).astype(jnp.bfloat16)
    section_grad = jnp.stack([grad_in.reshape(SEQS, S, D), grad_mid.reshape(SEQS, S, D)]).astype(jnp.float32)
    return (section_out, section_grad, totals[0], totals[1], totals[2], totals[3], totals[4], totals[5], totals[6], totals[7], totals[8])
```

```python
import functools

import jax
import jax.numpy as jnp
from jax import lax
from jax.experimental import pallas as pl
from jax.experimental.pallas import tpu as pltpu
from jax.sharding import PartitionSpec as P

H = 12
MICRO = 2
EPS = 1e-12
MESH = pl.DeviceIdType.MESH
BF = jnp.bfloat16
F32 = jnp.float32
LANES = 128
INV_SQRT_2PI = 0.3989422804014327
INV_SQRT_2 = 0.7071067811865476


def dot_nn(a, b):
    return lax.dot_general(a, b, (((1,), (0,)), ((), ())), preferred_element_type=F32)


def dot_nt(a, b):
    return lax.dot_general(a, b, (((1,), (1,)), ((), ())), preferred_element_type=F32)


def dot_tn(a, b):
    return lax.dot_general(a, b, (((0,), (0,)), ((), ())), preferred_element_type=F32)


def layers_kernel(
    len_ref, in_hbm, cot_hbm, wqkv_hbm, wout_hbm, wup_hbm, wdown_hbm,
    abias_ref, obias_ref, bup_ref, gain_ref, shift_ref,
    sout_hbm, sgrad_hbm, xs, os_, n1s, fs, dps, das, dus, dzs, bg,
    ab, wqkv, wout, wup, wdown, q_s, kv, lse, ot, xh1, xh2, rs1, rs2, gp, dr1, acc, do_s,
    dkv_own, dkv_send, dkv_recv, yb, gb,
    w_sem, loc_sem, ex_send, ex_recv, hop_send, hop_recv, kv_send, kv_rsem, dk_ssem, dk_rsem,
    out_loc, out_send, out_recv,
):
    width = wqkv.shape[0]
    ff = wup.shape[1]
    span = in_hbm.shape[1]
    rows = 2 * span
    keys = 2 * rows
    hd = width // H
    pairs = H // 2
    nff = ff // width
    sec = lax.axis_index("section")
    seq = lax.axis_index("seq")
    dp = lax.axis_index("dp")
    hi = seq // 2
    lo = seq % 2
    core_dev = (sec, hi * 2 + 1 - lo, dp)
    y_dev = (sec, (1 - hi) * 2 + lo, dp)
    x_dev = (1 - sec, seq, dp)

    weight_copies = [
        pltpu.make_async_copy(src.at[0], dst, w_sem.at[i])
        for i, (src, dst) in enumerate(
            ((wqkv_hbm, wqkv), (wout_hbm, wout), (wup_hbm, wup), (wdown_hbm, wdown))
        )
    ]
    for copy in weight_copies:
        copy.start()

    barrier = pltpu.get_barrier_semaphore()
    for dev in (core_dev, y_dev, x_dev):
        pl.semaphore_signal(barrier, inc=1, device_id=dev, device_id_type=MESH)
    pl.semaphore_wait(barrier, 3)

    def own_copy(src, m):
        return pltpu.make_async_copy(
            src.at[2 * hi + m], ab.at[0, pl.ds(m * rows, span)], loc_sem.at[m]
        )

    def y_copy(src, m):
        return pltpu.make_async_remote_copy(
            src_ref=src.at[2 * (1 - hi) + m],
            dst_ref=ab.at[0, pl.ds(m * rows + span, span)],
            send_sem=ex_send.at[m], recv_sem=ex_recv.at[m],
            device_id=y_dev, device_id_type=MESH,
        )

    for is_sec, src in ((0, in_hbm), (1, cot_hbm)):
        @pl.when(sec == is_sec)
        def _(src=src):
            for m in range(MICRO):
                y_copy(src, m).start()
                own_copy(src, m).start()

    bg[...] = jnp.zeros_like(bg)

    def mrows(m):
        return pl.ds(pl.multiple_of(m * rows, rows), rows)

    def hop_copy(src, m):
        return pltpu.make_async_remote_copy(
            src_ref=src.at[mrows(m)], dst_ref=ab.at[1, mrows(m)],
            send_sem=hop_send.at[m], recv_sem=hop_recv.at[m],
            device_id=x_dev, device_id_type=MESH,
        )

    def kv_copy(m):
        return pltpu.make_async_remote_copy(
            src_ref=kv.at[m, pl.ds(0, rows)], dst_ref=kv.at[m, pl.ds(rows, rows)],
            send_sem=kv_send.at[m], recv_sem=kv_rsem.at[m],
            device_id=core_dev, device_id_type=MESH,
        )

    def dkv_copy(m):
        return pltpu.make_async_remote_copy(
            src_ref=dkv_send.at[m], dst_ref=dkv_recv.at[m],
            send_sem=dk_ssem.at[m], recv_sem=dk_rsem.at[m],
            device_id=core_dev, device_id_type=MESH,
        )

    def out_copies(kind, src, dst, m):
        table = 2 * hi + m
        base = m * rows
        return (
            pltpu.make_async_copy(
                src.at[pl.ds(base, span)], dst.at[table], out_loc.at[kind, m]
            ),
            pltpu.make_async_remote_copy(
                src_ref=src.at[pl.ds(base + span, span)], dst_ref=dst.at[table],
                send_sem=out_send.at[kind, m], recv_sem=out_recv.at[kind, m],
                device_id=y_dev, device_id_type=MESH,
            ),
        )

    def wait_slot(which, m):
        @pl.when(which == 0)
        def _():
            own_copy(in_hbm, m).wait()
            y_copy(in_hbm, m).wait_recv()

        @pl.when(which == 1)
        def _():
            hop_copy(yb, m).wait_recv()

    def positions(shape):
        row = lax.broadcasted_iota(jnp.int32, shape, 0)
        block = row // span
        within = row % span
        half = jnp.where(block % 2 == 0, hi, 1 - hi)
        core = jnp.where(block < 2, lo, 1 - lo)
        return (half * 2 + core) * span + within

    def lane_masks():
        lane = lax.broadcasted_iota(jnp.int32, (1, LANES), 1)
        left = (lane < hd).astype(F32).astype(BF)
        right = (lane >= hd).astype(F32).astype(BF)
        return left, right

    def split_heads(value):
        left, right = lane_masks()
        return jnp.concatenate([value * left, value * right], axis=0)

    def norm(resid, gain, shift):
        average = jnp.mean(resid, axis=-1, keepdims=True)
        centred = resid - average
        spread = jnp.mean(centred * centred, axis=-1, keepdims=True)
        scale = lax.rsqrt(spread + EPS)
        hat = centred * scale
        return hat, scale, hat * gain + shift

    def norm_back(grad, hat, scale, gain):
        dh = grad * gain
        return scale * (
            dh
            - jnp.mean(dh, axis=-1, keepdims=True)
            - hat * jnp.mean(dh * hat, axis=-1, keepdims=True)
        )

    def vec(ref, part):
        return ref[0:1, part * width:(part + 1) * width].astype(F32)

    def add_bias_grad(row, value):
        bg[row] += jnp.sum(value, axis=0, keepdims=True)

    def forward(step, m):
        r = mrows(m)
        wait_slot(sec, m)
        xs[r] = ab[sec, r]

        @pl.when(step == 0)
        def _():
            weight_copies[0].wait()

        x = xs[r]
        kv[m, pl.ds(0, rows), 0:width] = dot_nn(x, wqkv[:, width:2 * width]).astype(BF)
        kv[m, pl.ds(0, rows), width:2 * width] = (
            dot_nn(x, wqkv[:, 2 * width:3 * width]) + vec(abias_ref, 1)
        ).astype(BF)
        kv_copy(m).start()
        queries = (dot_nn(x, wqkv[:, 0:width]) + vec(abias_ref, 0)).astype(BF)
        q_s[r] = queries * (hd ** -0.5)

        @pl.when(step == 0)
        def _():
            for copy in weight_copies[1:]:
                copy.wait()

        kv_copy(m).wait_recv()
        key_bias = jnp.where(positions((keys, 1)) < len_ref[2 * hi + m], 0.0, -1e30)

        def head_pair(p, carry):
            cols = pl.ds(pl.multiple_of(p * LANES, LANES), LANES)
            vcols = pl.ds(pl.multiple_of(width + p * LANES, LANES), LANES)
            qq = split_heads(q_s[r, cols])
            st = dot_nt(kv[m, :, cols], qq) + key_bias
            top = jnp.max(st, axis=0, keepdims=True)
            e = jnp.exp(st - top)
            total = jnp.sum(e, axis=0, keepdims=True)
            lse[m, p] = top + jnp.log(total)
            o_t = dot_tn(kv[m, :, vcols], e.astype(BF)) * (1.0 / total)
            o_pair = jnp.concatenate([o_t[0:hd, 0:rows], o_t[hd:2 * hd, rows:2 * rows]], axis=0)
            os_[r, cols] = o_pair.T.astype(BF)
            return carry

        lax.fori_loop(0, pairs, head_pair, 0)

        r1 = x.astype(F32) + dot_nn(os_[r], wout[...]) + vec(obias_ref, 0)
        hat, scale, n1 = norm(r1, vec(gain_ref, 0), vec(shift_ref, 0))
        xh1[r] = hat
        rs1[r] = jnp.broadcast_to(scale, (rows, LANES))
        n1s[r] = n1.astype(BF)
        acc[...] = n1 + vec(obias_ref, 1)

        def ff_chunk(j, carry):
            cols = pl.ds(pl.multiple_of(j * width, width), width)
            u = dot_nn(n1s[r], wup[:, cols]) + bup_ref[0:1, cols].astype(F32)
            phi = 0.5 + 0.5 * lax.erf(u * INV_SQRT_2)
            f = (u * phi).astype(BF)
            fs[r, cols] = f
            gp[r, cols] = (phi + u * (jnp.exp(-0.5 * u * u) * INV_SQRT_2PI)).astype(BF)
            acc[...] += dot_nn(f, wdown[cols, :])
            return carry

        lax.fori_loop(0, nff, ff_chunk, 0)
        hat, scale, result = norm(acc[...], vec(gain_ref, 1), vec(shift_ref, 1))
        xh2[r] = hat
        rs2[r] = jnp.broadcast_to(scale, (rows, LANES))
        yb[r] = result.astype(BF)

        @pl.when(sec == 0)
        def _():
            hop_copy(yb, m).start()

        for copy in out_copies(0, yb, sout_hbm, m):
            copy.start()

    def backward(step, m):
        r = mrows(m)
        wait_slot(1 - sec, m)
        length = len_ref[2 * hi + m]
        row_pos = positions((rows, 1))
        row_scale = jnp.where((sec == 0) | (row_pos < length), 1.0, 0.0)
        dy = ab[1 - sec, r].astype(F32) * row_scale
        hat = xh2[r]
        add_bias_grad(9, dy * hat)
        add_bias_grad(11, dy)
        dr2 = norm_back(dy, hat, rs2[r, 0:1], vec(gain_ref, 1))
        dz = dr2.astype(BF)
        dzs[r] = dz
        add_bias_grad(3, dz.astype(F32))
        acc[...] = dr2

        def ff_chunk(j, carry):
            cols = pl.ds(pl.multiple_of(j * width, width), width)
            du = (dot_nt(dzs[r], wdown[cols, :]) * gp[r, cols].astype(F32)).astype(BF)
            dus[r, cols] = du
            bg[4 + j] += jnp.sum(du.astype(F32), axis=0, keepdims=True)
            acc[...] += dot_nt(du, wup[:, cols])
            return carry

        lax.fori_loop(0, nff, ff_chunk, 0)
        dn1 = acc[...]
        hat = xh1[r]
        add_bias_grad(8, dn1 * hat)
        add_bias_grad(10, dn1)
        grad1 = norm_back(dn1, hat, rs1[r, 0:1], vec(gain_ref, 0))
        dr1[...] = grad1
        da = grad1.astype(BF)
        das[r] = da
        add_bias_grad(2, da.astype(F32))
        do_s[...] = dot_nt(da, wout[...]).astype(BF)
        key_bias = jnp.where(positions((keys, 1)) < length, 0.0, -1e30)

        def head_pair(p, carry):
            cols = pl.ds(pl.multiple_of(p * LANES, LANES), LANES)
            vcols = pl.ds(pl.multiple_of(width + p * LANES, LANES), LANES)
            qq = split_heads(q_s[r, cols])
            dd = split_heads(do_s[:, cols])
            kp = kv[m, :, cols]
            pt = jnp.exp(dot_nt(kp, qq) + key_bias - lse[m, p])
            dv = dot_nn(pt.astype(BF), dd)
            dpt = dot_nt(kv[m, :, vcols], dd)
            inner = jnp.sum(pt * dpt, axis=0, keepdims=True)
            ds = (pt * (dpt - inner)).astype(BF)
            dk = dot_nn(ds, qq)
            dq_t = dot_tn(kp, ds)
            dq_pair = jnp.concatenate([dq_t[0:hd, 0:rows], dq_t[hd:2 * hd, rows:2 * rows]], axis=0)
            dps[r, cols] = (dq_pair.T * (hd ** -0.5)).astype(BF)
            dkv_own[:, cols] = dk[0:rows]
            dkv_own[:, vcols] = dv[0:rows]
            dkv_send[m, :, cols] = dk[rows:keys].astype(BF)
            dkv_send[m, :, vcols] = dv[rows:keys].astype(BF)
            return carry

        lax.fori_loop(0, pairs, head_pair, 0)
        dkv_copy(m).start()
        dq = dps[r, 0:width]
        add_bias_grad(0, dq.astype(F32))
        dr1[...] += dot_nt(dq, wqkv[:, 0:width])
        dkv_copy(m).wait_recv()
        dk = (dkv_own[:, 0:width] + dkv_recv[m, :, 0:width].astype(F32)).astype(BF)
        dv = (dkv_own[:, width:2 * width] + dkv_recv[m, :, width:2 * width].astype(F32)).astype(BF)
        dps[r, width:2 * width] = dk
        dps[r, 2 * width:3 * width] = dv
        add_bias_grad(1, dv.astype(F32))
        dx = dr1[...] + dot_nt(dk, wqkv[:, width:2 * width]) + dot_nt(dv, wqkv[:, 2 * width:3 * width])
        gb[r] = dx.astype(BF)

        @pl.when(sec == 1)
        def _():
            hop_copy(gb, m).start()

        for copy in out_copies(1, gb, sgrad_hbm, m):
            copy.start()

    def one_step(step, carry):
        is_forward = (step == 0) | ((step == 1) & (sec == 0)) | ((step == 2) & (sec == 1))
        m = jnp.where(sec == 0, step % 2, step // 2)

        @pl.when(is_forward)
        def _():
            forward(step, m)

        @pl.when(jnp.logical_not(is_forward))
        def _():
            backward(step, m)

        return carry

    lax.fori_loop(0, 2 * MICRO, one_step, 0)

    for m in range(MICRO):
        y_copy(in_hbm, m).wait_send()
        hop_copy(yb, m).wait_send()
        kv_copy(m).wait_send()
        dkv_copy(m).wait_send()
        for kind, src, dst in ((0, yb, sout_hbm), (1, gb, sgrad_hbm)):
            local_out, remote_out = out_copies(kind, src, dst, m)
            local_out.wait()
            remote_out.wait()


def run_layers(args, shapes):
    (inputs, cotangent, lengths, w_qkv, attn_bias, w_out, out_bias, w_up, bias_up, w_down,
     norm_gain, norm_bias) = args
    tables, span, width = inputs.shape
    ff = w_up.shape[2]
    rows = 2 * span
    total = MICRO * rows
    keys = 2 * rows
    any_spec = pl.BlockSpec(memory_space=pl.ANY)
    vmem = pl.BlockSpec(memory_space=pltpu.VMEM)
    smem = pl.BlockSpec(memory_space=pltpu.SMEM)
    dma = pltpu.SemaphoreType.DMA
    return pl.pallas_call(
        layers_kernel,
        name="layers",
        out_shape=(
            jax.ShapeDtypeStruct((tables, span, width), BF),
            jax.ShapeDtypeStruct((tables, span, width), BF),
            jax.ShapeDtypeStruct((total, width), BF),
            jax.ShapeDtypeStruct((total, width), BF),
            jax.ShapeDtypeStruct((total, width), BF),
            jax.ShapeDtypeStruct((total, ff), BF),
            jax.ShapeDtypeStruct((total, 3 * width), BF),
            jax.ShapeDtypeStruct((total, width), BF),
            jax.ShapeDtypeStruct((total, ff), BF),
            jax.ShapeDtypeStruct((total, width), BF),
            jax.ShapeDtypeStruct((12, 1, width), F32),
        ),
        in_specs=[smem] + [any_spec] * 6 + [vmem] * 5,
        out_specs=(any_spec, any_spec) + (vmem,) * 9,
        scratch_shapes=[
            pltpu.VMEM((2, total, width), BF),
            pltpu.VMEM((width, 3 * width), BF),
            pltpu.VMEM((width, width), BF),
            pltpu.VMEM((width, ff), BF),
            pltpu.VMEM((ff, width), BF),
            pltpu.VMEM((total, width), BF),
            pltpu.VMEM((MICRO, keys, 2 * width), BF),
            pltpu.VMEM((MICRO, H // 2, 1, 2 * rows), F32),
            pltpu.VMEM((8, LANES), BF),
            pltpu.VMEM((total, width), F32),
            pltpu.VMEM((total, width), F32),
            pltpu.VMEM((total, LANES), F32),
            pltpu.VMEM((total, LANES), F32),
            pltpu.VMEM((total, ff), BF),
            pltpu.VMEM((rows, width), F32),
            pltpu.VMEM((rows, width), F32),
            pltpu.VMEM((rows, width), BF),
            pltpu.VMEM((rows, 2 * width), F32),
            pltpu.VMEM((MICRO, rows, 2 * width), BF),
            pltpu.VMEM((MICRO, rows, 2 * width), BF),
            pltpu.VMEM((total, width), BF),
            pltpu.VMEM((total, width), BF),
            dma((4,)), dma((MICRO,)), dma((MICRO,)), dma((MICRO,)), dma((MICRO,)), dma((MICRO,)),
            dma((MICRO,)), dma((MICRO,)), dma((MICRO,)), dma((MICRO,)),
            dma((2, MICRO)), dma((2, MICRO)), dma((2, MICRO)),
        ],
        compiler_params=pltpu.CompilerParams(
            collective_id=0, has_side_effects=True, vmem_limit_bytes=60 * 2 ** 20
        ),
    )(lengths, inputs, cotangent, w_qkv, w_out, w_up, w_down,
      attn_bias, out_bias, bias_up, norm_gain, norm_bias)


def local(*args):
    (sout, sgrad, xs, os_, n1s, fs, dps, das, dus, dzs, bg) = run_layers(args, None)
    width = xs.shape[1]
    index = lax.axis_index("seq") * lax.axis_size("dp") + lax.axis_index("dp")
    count = lax.axis_size("seq") * lax.axis_size("dp")

    def weight_grad(a, b):
        full = dot_tn(a, b).astype(BF)
        return lax.psum_scatter(full, ("seq", "dp"), scatter_dimension=0, tiled=True).astype(F32)

    sums = lax.psum(bg.reshape(12 * width), ("seq", "dp"))

    def piece(start, rows):
        part = sums[start * width:(start + rows) * width]
        size = rows * width // count
        return lax.dynamic_slice_in_dim(part, index * size, size, 0)[None]

    return (
        sout[None],
        sgrad.astype(F32)[None],
        weight_grad(xs, dps)[None],
        piece(0, 2),
        weight_grad(os_, das)[None],
        piece(2, 2),
        weight_grad(n1s, dus)[None],
        piece(4, 4),
        weight_grad(fs, dzs)[None],
        piece(8, 2),
        piece(10, 2),
    )


def solution(mesh):
    return jax.shard_map(
        local,
        mesh=mesh,
        in_specs=(
            P("dp", "seq", None),
            P("dp", "seq", None),
            P("dp"),
            P("section", None, None),
            P("section", None),
            P("section", None, None),
            P("section", None),
            P("section", None, None),
            P("section", None),
            P("section", None, None),
            P("section", None),
            P("section", None),
        ),
        out_specs=(
            P("section", "dp", "seq", None),
            P("section", "dp", "seq", None),
            P("section", ("seq", "dp"), None),
            P("section", ("seq", "dp")),
            P("section", ("seq", "dp"), None),
            P("section", ("seq", "dp")),
            P("section", ("seq", "dp"), None),
            P("section", ("seq", "dp")),
            P("section", ("seq", "dp"), None),
            P("section", ("seq", "dp")),
            P("section", ("seq", "dp")),
        ),
        check_vma=False,
    )
```

```python
import functools

import jax
import jax.numpy as jnp
from jax import lax
from jax.experimental import pallas as pl
from jax.experimental.pallas import tpu as pltpu
from jax.sharding import PartitionSpec as P

H = 12
MICRO = 2
EPS = 1e-12
MESH = pl.DeviceIdType.MESH
BF = jnp.bfloat16
F32 = jnp.float32
LANES = 128
INV_SQRT_2PI = 0.3989422804014327
INV_SQRT_2 = 0.7071067811865476
L_F, L_N, L_O, L_X, L_COUNT = 0, 4, 5, 6, 7
R_P, R_A, R_U, R_Z, R_COUNT = 0, 3, 4, 8, 9
CHUNKS = 12
Z_FIRST = 2


def dot_nn(a, b):
    return lax.dot_general(a, b, (((1,), (0,)), ((), ())), preferred_element_type=F32)


def dot_nt(a, b):
    return lax.dot_general(a, b, (((1,), (1,)), ((), ())), preferred_element_type=F32)


def dot_tn(a, b):
    return lax.dot_general(a, b, (((0,), (0,)), ((), ())), preferred_element_type=F32)


def layers_kernel(
    len_ref, in_hbm, cot_hbm, wqkv_hbm, wout_hbm, wup_hbm, wdown_hbm,
    abias_ref, obias_ref, bup_ref, gain_ref, shift_ref,
    sout_hbm, sgrad_hbm, lt, rt, bg,
    ab, wqkv, wout, wup, wdown, q_s, kv, lse, o_s, n_s, xh1, xh2, rs1, rs2, gp, dr1, acc, do_s,
    dkv_own, dkv_send, dkv_recv, yb, gb,
    w_sem, loc_sem, ex_send, ex_recv, hop_send, hop_recv, kv_send, kv_rsem, dk_ssem, dk_rsem,
    out_loc, out_send, out_recv,
):
    width = wqkv.shape[0]
    ff = wup.shape[1]
    span = in_hbm.shape[1]
    rows = 2 * span
    keys = 2 * rows
    hd = width // H
    pairs = H // 2
    nff = ff // width
    dp_size = 4
    unit = width // 16
    sec = lax.axis_index("section")
    seq = lax.axis_index("seq")
    dp = lax.axis_index("dp")
    hi = seq // 2
    lo = seq % 2
    core_dev = (sec, hi * 2 + 1 - lo, dp)
    y_dev = (sec, (1 - hi) * 2 + lo, dp)
    x_dev = (1 - sec, seq, dp)

    weight_copies = [
        pltpu.make_async_copy(src.at[0], dst, w_sem.at[i])
        for i, (src, dst) in enumerate(
            ((wqkv_hbm, wqkv), (wout_hbm, wout), (wup_hbm, wup), (wdown_hbm, wdown))
        )
    ]
    for copy in weight_copies:
        copy.start()

    barrier = pltpu.get_barrier_semaphore()
    for dev in (core_dev, y_dev, x_dev):
        pl.semaphore_signal(barrier, inc=1, device_id=dev, device_id_type=MESH)
    pl.semaphore_wait(barrier, 3)

    def own_copy(src, m):
        return pltpu.make_async_copy(
            src.at[2 * hi + m], ab.at[0, pl.ds(m * rows, span)], loc_sem.at[m]
        )

    def y_copy(src, m):
        return pltpu.make_async_remote_copy(
            src_ref=src.at[2 * (1 - hi) + m],
            dst_ref=ab.at[0, pl.ds(m * rows + span, span)],
            send_sem=ex_send.at[m], recv_sem=ex_recv.at[m],
            device_id=y_dev, device_id_type=MESH,
        )

    for is_sec, src in ((0, in_hbm), (1, cot_hbm)):
        @pl.when(sec == is_sec)
        def _(src=src):
            for m in range(MICRO):
                y_copy(src, m).start()
                own_copy(src, m).start()

    bg[...] = jnp.zeros_like(bg)

    def mrows(m):
        return pl.ds(pl.multiple_of(m * rows, rows), rows)

    def hop_copy(src, m):
        return pltpu.make_async_remote_copy(
            src_ref=src.at[mrows(m)], dst_ref=ab.at[1, mrows(m)],
            send_sem=hop_send.at[m], recv_sem=hop_recv.at[m],
            device_id=x_dev, device_id_type=MESH,
        )

    def kv_copy(m):
        return pltpu.make_async_remote_copy(
            src_ref=kv.at[m, pl.ds(0, rows)], dst_ref=kv.at[m, pl.ds(rows, rows)],
            send_sem=kv_send.at[m], recv_sem=kv_rsem.at[m],
            device_id=core_dev, device_id_type=MESH,
        )

    def dkv_copy(m):
        return pltpu.make_async_remote_copy(
            src_ref=dkv_send.at[m], dst_ref=dkv_recv.at[m],
            send_sem=dk_ssem.at[m], recv_sem=dk_rsem.at[m],
            device_id=core_dev, device_id_type=MESH,
        )

    def out_copies(kind, src, dst, m):
        table = 2 * hi + m
        base = m * rows
        return (
            pltpu.make_async_copy(
                src.at[pl.ds(base, span)], dst.at[table], out_loc.at[kind, m]
            ),
            pltpu.make_async_remote_copy(
                src_ref=src.at[pl.ds(base + span, span)], dst_ref=dst.at[table],
                send_sem=out_send.at[kind, m], recv_sem=out_recv.at[kind, m],
                device_id=y_dev, device_id_type=MESH,
            ),
        )

    def wait_slot(which, m):
        @pl.when(which == 0)
        def _():
            own_copy(in_hbm, m).wait()
            y_copy(in_hbm, m).wait_recv()

        @pl.when(which == 1)
        def _():
            hop_copy(yb, m).wait_recv()

    def positions(shape):
        row = lax.broadcasted_iota(jnp.int32, shape, 0)
        block = row // span
        within = row % span
        half = jnp.where(block % 2 == 0, hi, 1 - hi)
        core = jnp.where(block < 2, lo, 1 - lo)
        return (half * 2 + core) * span + within

    def lane_masks():
        lane = lax.broadcasted_iota(jnp.int32, (1, LANES), 1)
        left = (lane < hd).astype(F32).astype(BF)
        right = (lane >= hd).astype(F32).astype(BF)
        return left, right

    def split_heads(value):
        left, right = lane_masks()
        return jnp.concatenate([value * left, value * right], axis=0)

    def norm(resid, gain, shift):
        average = jnp.mean(resid, axis=-1, keepdims=True)
        centred = resid - average
        spread = jnp.mean(centred * centred, axis=-1, keepdims=True)
        scale = lax.rsqrt(spread + EPS)
        hat = centred * scale
        return hat, scale, hat * gain + shift

    def norm_back(grad, hat, scale, gain):
        dh = grad * gain
        return scale * (
            dh
            - jnp.mean(dh, axis=-1, keepdims=True)
            - hat * jnp.mean(dh * hat, axis=-1, keepdims=True)
        )

    def vec(ref, part):
        return ref[0:1, part * width:(part + 1) * width].astype(F32)

    def add_bias_grad(row, value):
        bg[row] += jnp.sum(value, axis=0, keepdims=True)

    def forward(step, m):
        r = mrows(m)
        wait_slot(sec, m)

        @pl.when(step == 0)
        def _():
            weight_copies[0].wait()

        x = ab[sec, r]
        kv[m, pl.ds(0, rows), 0:width] = dot_nn(x, wqkv[:, width:2 * width]).astype(BF)
        kv[m, pl.ds(0, rows), width:2 * width] = (
            dot_nn(x, wqkv[:, 2 * width:3 * width]) + vec(abias_ref, 1)
        ).astype(BF)
        kv_copy(m).start()
        queries = (dot_nn(x, wqkv[:, 0:width]) + vec(abias_ref, 0)).astype(BF)
        q_s[r] = queries * (hd ** -0.5)

        @pl.when(step == 0)
        def _():
            for copy in weight_copies[1:]:
                copy.wait()

        kv_copy(m).wait_recv()
        key_bias = jnp.where(positions((keys, 1)) < len_ref[2 * hi + m], 0.0, -1e30)

        def head_pair(p, carry):
            cols = pl.ds(pl.multiple_of(p * LANES, LANES), LANES)
            vcols = pl.ds(pl.multiple_of(width + p * LANES, LANES), LANES)
            qq = split_heads(q_s[r, cols])
            st = dot_nt(kv[m, :, cols], qq) + key_bias
            top = jnp.max(st, axis=0, keepdims=True)
            e = jnp.exp(st - top)
            total = jnp.sum(e, axis=0, keepdims=True)
            lse[m, p] = top + jnp.log(total)
            o_t = dot_tn(kv[m, :, vcols], e.astype(BF)) * (1.0 / total)
            o_pair = jnp.concatenate([o_t[0:hd, 0:rows], o_t[hd:2 * hd, rows:2 * rows]], axis=0)
            lt[L_O, cols, r] = o_pair.astype(BF)
            o_s[:, cols] = o_pair.T.astype(BF)
            return carry

        lax.fori_loop(0, pairs, head_pair, 0)

        r1 = x.astype(F32) + dot_nn(o_s[...], wout[...]) + vec(obias_ref, 0)
        hat, scale, n1 = norm(r1, vec(gain_ref, 0), vec(shift_ref, 0))
        xh1[r] = hat
        rs1[r] = jnp.broadcast_to(scale, (rows, LANES))
        n_s[...] = n1.astype(BF)
        acc[...] = n1 + vec(obias_ref, 1)

        def ff_chunk(j, carry):
            cols = pl.ds(pl.multiple_of(j * width, width), width)
            u = dot_nn(n_s[...], wup[:, cols]) + bup_ref[0:1, cols].astype(F32)
            phi = 0.5 + 0.5 * lax.erf(u * INV_SQRT_2)
            f = (u * phi).astype(BF)
            f_t = f.T
            for z in range(dp_size):
                for part in range(nff):
                    lt[part, pl.ds((j * dp_size + z) * unit, unit), r] = f_t[
                        (z * nff + part) * unit:(z * nff + part + 1) * unit
                    ]
            gp[r, cols] = (phi + u * (jnp.exp(-0.5 * u * u) * INV_SQRT_2PI)).astype(BF)
            acc[...] += dot_nn(f, wdown[cols, :])
            return carry

        lax.fori_loop(0, nff, ff_chunk, 0)
        hat, scale, result = norm(acc[...], vec(gain_ref, 1), vec(shift_ref, 1))
        xh2[r] = hat
        rs2[r] = jnp.broadcast_to(scale, (rows, LANES))
        yb[r] = result.astype(BF)

        @pl.when(sec == 0)
        def _():
            hop_copy(yb, m).start()

        for copy in out_copies(0, yb, sout_hbm, m):
            copy.start()
        lt[L_X, :, r] = ab[sec, r].T
        lt[L_N, :, r] = n_s[...].T

    def backward(step, m):
        r = mrows(m)
        wait_slot(1 - sec, m)
        length = len_ref[2 * hi + m]
        row_pos = positions((rows, 1))
        row_scale = jnp.where((sec == 0) | (row_pos < length), 1.0, 0.0)
        dy = ab[1 - sec, r].astype(F32) * row_scale
        hat = xh2[r]
        add_bias_grad(9, dy * hat)
        add_bias_grad(11, dy)
        dr2 = norm_back(dy, hat, rs2[r, 0:1], vec(gain_ref, 1))
        dz = dr2.astype(BF)
        rt[R_Z, r] = dz
        add_bias_grad(3, dz.astype(F32))
        acc[...] = dr2

        def ff_chunk(j, carry):
            cols = pl.ds(pl.multiple_of(j * width, width), width)
            du = (dot_nt(rt[R_Z, r], wdown[cols, :]) * gp[r, cols].astype(F32)).astype(BF)
            rt[R_U + j, r] = du
            bg[4 + j] += jnp.sum(du.astype(F32), axis=0, keepdims=True)
            acc[...] += dot_nt(du, wup[:, cols])
            return carry

        lax.fori_loop(0, nff, ff_chunk, 0)
        dn1 = acc[...]
        hat = xh1[r]
        add_bias_grad(8, dn1 * hat)
        add_bias_grad(10, dn1)
        grad1 = norm_back(dn1, hat, rs1[r, 0:1], vec(gain_ref, 0))
        dr1[...] = grad1
        da = grad1.astype(BF)
        rt[R_A, r] = da
        add_bias_grad(2, da.astype(F32))
        do_s[...] = dot_nt(da, wout[...]).astype(BF)
        key_bias = jnp.where(positions((keys, 1)) < length, 0.0, -1e30)

        def head_pair(p, carry):
            cols = pl.ds(pl.multiple_of(p * LANES, LANES), LANES)
            vcols = pl.ds(pl.multiple_of(width + p * LANES, LANES), LANES)
            qq = split_heads(q_s[r, cols])
            dd = split_heads(do_s[:, cols])
            kp = kv[m, :, cols]
            pt = jnp.exp(dot_nt(kp, qq) + key_bias - lse[m, p])
            dv = dot_nn(pt.astype(BF), dd)
            dpt = dot_nt(kv[m, :, vcols], dd)
            inner = jnp.sum(pt * dpt, axis=0, keepdims=True)
            ds = (pt * (dpt - inner)).astype(BF)
            dk = dot_nn(ds, qq)
            dq_t = dot_tn(kp, ds)
            dq_pair = jnp.concatenate([dq_t[0:hd, 0:rows], dq_t[hd:2 * hd, rows:2 * rows]], axis=0)
            rt[R_P, r, cols] = (dq_pair.T * (hd ** -0.5)).astype(BF)
            dkv_own[:, cols] = dk[0:rows]
            dkv_own[:, vcols] = dv[0:rows]
            dkv_send[m, :, cols] = dk[rows:keys].astype(BF)
            dkv_send[m, :, vcols] = dv[rows:keys].astype(BF)
            return carry

        lax.fori_loop(0, pairs, head_pair, 0)
        dkv_copy(m).start()
        dq = rt[R_P, r]
        add_bias_grad(0, dq.astype(F32))
        dr1[...] += dot_nt(dq, wqkv[:, 0:width])
        dkv_copy(m).wait_recv()
        dk = (dkv_own[:, 0:width] + dkv_recv[m, :, 0:width].astype(F32)).astype(BF)
        dv = (dkv_own[:, width:2 * width] + dkv_recv[m, :, width:2 * width].astype(F32)).astype(BF)
        rt[R_P + 1, r] = dk
        rt[R_P + 2, r] = dv
        add_bias_grad(1, dv.astype(F32))
        dx = dr1[...] + dot_nt(dk, wqkv[:, width:2 * width]) + dot_nt(dv, wqkv[:, 2 * width:3 * width])
        gb[r] = dx.astype(BF)

        @pl.when(sec == 1)
        def _():
            hop_copy(gb, m).start()

        for copy in out_copies(1, gb, sgrad_hbm, m):
            copy.start()

    def one_step(step, carry):
        is_forward = (step == 0) | ((step == 1) & (sec == 0)) | ((step == 2) & (sec == 1))
        m = jnp.where(sec == 0, step % 2, step // 2)

        @pl.when(is_forward)
        def _():
            forward(step, m)

        @pl.when(jnp.logical_not(is_forward))
        def _():
            backward(step, m)

        return carry

    lax.fori_loop(0, 2 * MICRO, one_step, 0)

    for m in range(MICRO):
        y_copy(in_hbm, m).wait_send()
        hop_copy(yb, m).wait_send()
        kv_copy(m).wait_send()
        dkv_copy(m).wait_send()
        for kind, src, dst in ((0, yb, sout_hbm), (1, gb, sgrad_hbm)):
            local_out, remote_out = out_copies(kind, src, dst, m)
            local_out.wait()
            remote_out.wait()


def run_layers(args, shapes):
    (inputs, cotangent, lengths, w_qkv, attn_bias, w_out, out_bias, w_up, bias_up, w_down,
     norm_gain, norm_bias) = args
    tables, span, width = inputs.shape
    ff = w_up.shape[2]
    rows = 2 * span
    total = MICRO * rows
    keys = 2 * rows
    any_spec = pl.BlockSpec(memory_space=pl.ANY)
    vmem = pl.BlockSpec(memory_space=pltpu.VMEM)
    smem = pl.BlockSpec(memory_space=pltpu.SMEM)
    dma = pltpu.SemaphoreType.DMA
    return pl.pallas_call(
        layers_kernel,
        name="layers",
        out_shape=(
            jax.ShapeDtypeStruct((tables, span, width), BF),
            jax.ShapeDtypeStruct((tables, span, width), BF),
            jax.ShapeDtypeStruct((L_COUNT, width, total), BF),
            jax.ShapeDtypeStruct((R_COUNT, total, width), BF),
            jax.ShapeDtypeStruct((12, 1, width), F32),
        ),
        in_specs=[smem] + [any_spec] * 6 + [vmem] * 5,
        out_specs=(any_spec, any_spec) + (vmem,) * 3,
        scratch_shapes=[
            pltpu.VMEM((2, total, width), BF),
            pltpu.VMEM((width, 3 * width), BF),
            pltpu.VMEM((width, width), BF),
            pltpu.VMEM((width, ff), BF),
            pltpu.VMEM((ff, width), BF),
            pltpu.VMEM((total, width), BF),
            pltpu.VMEM((MICRO, keys, 2 * width), BF),
            pltpu.VMEM((MICRO, H // 2, 1, 2 * rows), F32),
            pltpu.VMEM((rows, width), BF),
            pltpu.VMEM((rows, width), BF),
            pltpu.VMEM((total, width), F32),
            pltpu.VMEM((total, width), F32),
            pltpu.VMEM((total, LANES), F32),
            pltpu.VMEM((total, LANES), F32),
            pltpu.VMEM((total, ff), BF),
            pltpu.VMEM((rows, width), F32),
            pltpu.VMEM((rows, width), F32),
            pltpu.VMEM((rows, width), BF),
            pltpu.VMEM((rows, 2 * width), F32),
            pltpu.VMEM((MICRO, rows, 2 * width), BF),
            pltpu.VMEM((MICRO, rows, 2 * width), BF),
            pltpu.VMEM((total, width), BF),
            pltpu.VMEM((total, width), BF),
            dma((4,)), dma((MICRO,)), dma((MICRO,)), dma((MICRO,)), dma((MICRO,)), dma((MICRO,)),
            dma((MICRO,)), dma((MICRO,)), dma((MICRO,)), dma((MICRO,)),
            dma((2, MICRO)), dma((2, MICRO)), dma((2, MICRO)),
        ],
        compiler_params=pltpu.CompilerParams(
            collective_id=0, has_side_effects=True, vmem_limit_bytes=60 * 2 ** 20
        ),
    )(lengths, inputs, cotangent, w_qkv, w_out, w_up, w_down,
      attn_bias, out_bias, bias_up, norm_gain, norm_bias)


def grads_kernel(
    lt, rt, bg,
    out, bg_out,
    core_src, chip, own, y_buf, up, down, turn_src, turn_buf, b_src, b_core, b_y, b_z,
    core_ss, core_rs, y_ss, y_rs, up_ss, up_rs, down_ss, down_rs, turn_ss, turn_rs,
    bc_ss, bc_rs, bz_ss, bz_rs,
):
    count = b_z.shape[0]
    unit = out.shape[1]
    block = count * unit
    sec = lax.axis_index("section")
    seq = lax.axis_index("seq")
    z = lax.axis_index("dp")
    hi = seq // 2
    lo = seq % 2
    core_dev = (sec, hi * 2 + 1 - lo, z)
    y_dev = (sec, (1 - hi) * 2 + lo, z)

    def z_dev(index):
        return (sec, seq, index)

    barrier = pltpu.get_barrier_semaphore()
    for dev in (core_dev, y_dev):
        pl.semaphore_signal(barrier, inc=1, device_id=dev, device_id_type=MESH)
    for by in range(1, count):
        pl.semaphore_signal(
            barrier, inc=1, device_id=z_dev((z + by) % count), device_id_type=MESH
        )
    pl.semaphore_wait(barrier, 1 + count)

    def remote(src, dst, send, recv, dev):
        return pltpu.make_async_remote_copy(
            src_ref=src, dst_ref=dst, send_sem=send, recv_sem=recv,
            device_id=dev, device_id_type=MESH,
        )

    def core_copy(k, half):
        return remote(
            core_src.at[k, half], chip.at[k, half], core_ss.at[k, half], core_rs.at[k, half], core_dev
        )

    def y_copy(k):
        return remote(chip.at[k, 1 - hi], y_buf.at[k], y_ss.at[k], y_rs.at[k], y_dev)

    def turn_copy(k):
        return remote(turn_src.at[k], turn_buf.at[k], turn_ss.at[k], turn_rs.at[k], y_dev)

    def piece(k, half, target):
        return chip.at[k, half, pl.ds(pl.multiple_of(target * unit, unit), unit)]

    def up_copy(job, k, half, target):
        return remote(
            piece(k, half, target), up.at[job, target], up_ss.at[job, target],
            up_rs.at[job, target], z_dev(jnp.minimum(z + 1, count - 1)),
        )

    def down_copy(job, k, half, target):
        return remote(
            piece(k, half, target), down.at[job, target], down_ss.at[job, target],
            down_rs.at[job, target], z_dev(jnp.maximum(z - 1, 0)),
        )

    def add_piece(k, half, target, landed):
        ref = piece(k, half, target)
        ref[...] = (ref[...].astype(F32) + landed[...].astype(F32)).astype(BF)

    def hop(number, job, k, half):
        @pl.when(z == number - 1)
        def _():
            for target in range(count - 1, number - 1, -1):
                if number > 1:
                    up_copy(job, k, half, target).wait_recv()
                    add_piece(k, half, target, up.at[job, target])
                up_copy(job, k, half, target).start()

        @pl.when(z == count - number)
        def _():
            for target in range(0, count - number):
                if number > 1:
                    down_copy(job, k, half, target).wait_recv()
                    add_piece(k, half, target, down.at[job, target])
                down_copy(job, k, half, target).start()

    def arrive(job, k, half, dst):
        dst[...] = piece(k, half, z)[...].astype(F32)

        @pl.when(z > 0)
        def _():
            up_copy(job, k, half, z).wait_recv()
            dst[...] += up[job, z].astype(F32)

        @pl.when(z < count - 1)
        def _():
            down_copy(job, k, half, z).wait_recv()
            dst[...] += down[job, z].astype(F32)

    def product(k):
        left = jnp.where(k < 8, jnp.minimum(k, L_N), jnp.where(k == 8, L_O, L_X))
        right = jnp.where(k < 4, R_Z, jnp.where(k < 8, k, jnp.where(k == 8, R_A, k - 9)))
        for half in range(2):
            base = pl.multiple_of((half * 2 + 1 - lo) * block, block)
            core_src[k, half] = dot_nn(lt[left, pl.ds(base, block), :], rt[right]).astype(BF)
            core_copy(k, half).start()
        for half in range(2):
            base = pl.multiple_of((half * 2 + lo) * block, block)
            own[k % 2, half] = dot_nn(lt[left, pl.ds(base, block), :], rt[right])

    def chip_sum(k):
        for half in range(2):
            core_copy(k, half).wait_recv()
            chip[k, half] = (own[k % 2, half] + chip[k, half].astype(F32)).astype(BF)

    def bias_core():
        return remote(b_src.at[0], b_core, bc_ss.at[0], bc_rs.at[0], core_dev)

    def bias_y():
        return remote(b_src.at[1], b_y, bc_ss.at[1], bc_rs.at[1], y_dev)

    def bias_z(by):
        return remote(
            b_src.at[2], b_z.at[by], bz_ss.at[by], bz_rs.at[by], z_dev((z + by) % count)
        )

    def step(t, carry):
        def at(first, last):
            return (t >= first) & (t <= last)

        @pl.when(t == 0)
        def _():
            b_src[0] = bg[...]
            bias_core().start()

        @pl.when(t < CHUNKS)
        def _():
            product(t)

        @pl.when(at(1, CHUNKS))
        def _():
            chip_sum(t - 1)

        @pl.when(at(1, Z_FIRST))
        def _():
            for half in range(2):
                hop(1, 2 * (t - 1) + half, t - 1, half)

        @pl.when(at(Z_FIRST + 1, CHUNKS))
        def _():
            y_copy(t - 1).start()

        @pl.when(t == 2)
        def _():
            bias_core().wait_recv()
            b_src[1] = b_src[0] + b_core[...]
            bias_y().start()

        @pl.when(t == 4)
        def _():
            bias_y().wait_recv()
            b_src[2] = b_src[1] + b_y[...]
            for by in range(1, count):
                bias_z(by).start()

        @pl.when(at(Z_FIRST + 3, CHUNKS + 2))
        def _():
            k = t - 3
            y_copy(k).wait_recv()
            chip[k, hi] = (chip[k, hi].astype(F32) + y_buf[k].astype(F32)).astype(BF)
            hop(1, k + Z_FIRST, k, hi)

        for number in range(2, count):
            @pl.when(at(Z_FIRST + 2 + number, CHUNKS + 1 + number))
            def _(number=number):
                k = t - 2 - number
                hop(number, k + Z_FIRST, k, hi)

            @pl.when(at(2 * number, 2 * number + Z_FIRST - 1))
            def _(number=number):
                k = t - 2 * number
                for half in range(2):
                    hop(number, 2 * k + half, k, half)

        @pl.when(at(Z_FIRST + 2 + count, CHUNKS + 1 + count))
        def _():
            k = t - 2 - count
            arrive(k + Z_FIRST, k, hi, out.at[k])

        @pl.when(at(2 * count, 2 * count + Z_FIRST - 1))
        def _():
            k = t - 2 * count
            arrive(2 * k + 1 - hi, k, 1 - hi, out.at[k])
            turn_src[k] = out[k].astype(BF)
            turn_copy(k).start()
            arrive(2 * k + hi, k, hi, out.at[k])

        @pl.when(at(2 * count + 2, 2 * count + 1 + Z_FIRST))
        def _():
            k = t - 2 * count - 2
            turn_copy(k).wait_recv()
            out[k] += turn_buf[k].astype(F32)

        return carry

    lax.fori_loop(0, CHUNKS + 2 + count, step, 0)

    for by in range(1, count):
        bias_z(by).wait_recv()
    total = b_src[2]
    for by in range(1, count):
        total = total + b_z[by]
    bg_out[...] = total
    bias_core().wait_send()
    bias_y().wait_send()
    for by in range(1, count):
        bias_z(by).wait_send()

    def sent(job, k, half):
        for target in range(count):
            @pl.when(target > z)
            def _(target=target):
                up_copy(job, k, half, target).wait_send()

            @pl.when(target < z)
            def _(target=target):
                down_copy(job, k, half, target).wait_send()

    def drain(k, carry):
        for half in range(2):
            core_copy(k, half).wait_send()

        @pl.when(k < Z_FIRST)
        def _():
            turn_copy(k).wait_send()
            for half in range(2):
                sent(2 * k + half, k, half)

        @pl.when(k >= Z_FIRST)
        def _():
            y_copy(k).wait_send()
            sent(k + Z_FIRST, k, hi)

        return carry

    lax.fori_loop(0, CHUNKS, drain, 0)


def run_grads(lt, rt, bg):
    count = lax.axis_size("dp")
    width = lt.shape[1]
    unit = width // (4 * count)
    block = count * unit
    jobs = CHUNKS + Z_FIRST
    vmem = pl.BlockSpec(memory_space=pltpu.VMEM)
    dma = pltpu.SemaphoreType.DMA
    return pl.pallas_call(
        grads_kernel,
        name="grads",
        out_shape=(
            jax.ShapeDtypeStruct((CHUNKS, unit, width), F32),
            jax.ShapeDtypeStruct((12, 1, width), F32),
        ),
        in_specs=[vmem] * 3,
        out_specs=(vmem,) * 2,
        scratch_shapes=[
            pltpu.VMEM((CHUNKS, 2, block, width), BF),
            pltpu.VMEM((CHUNKS, 2, block, width), BF),
            pltpu.VMEM((2, 2, block, width), F32),
            pltpu.VMEM((CHUNKS, block, width), BF),
            pltpu.VMEM((jobs, count, unit, width), BF),
            pltpu.VMEM((jobs, count, unit, width), BF),
            pltpu.VMEM((Z_FIRST, unit, width), BF),
            pltpu.VMEM((Z_FIRST, unit, width), BF),
            pltpu.VMEM((3, 12, 1, width), F32),
            pltpu.VMEM((12, 1, width), F32),
            pltpu.VMEM((12, 1, width), F32),
            pltpu.VMEM((count, 12, 1, width), F32),
            dma((CHUNKS, 2)), dma((CHUNKS, 2)), dma((CHUNKS,)), dma((CHUNKS,)),
            dma((jobs, count)), dma((jobs, count)), dma((jobs, count)), dma((jobs, count)),
            dma((Z_FIRST,)), dma((Z_FIRST,)), dma((2,)), dma((2,)), dma((count,)), dma((count,)),
        ],
        compiler_params=pltpu.CompilerParams(
            collective_id=1, has_side_effects=True, vmem_limit_bytes=60 * 2 ** 20
        ),
    )(lt, rt, bg)


def grads_by_scatter(lt, rt, bg, ff):
    width = lt.shape[1]
    parts = ff // width

    def scatter(full):
        return lax.psum_scatter(
            full.astype(BF), ("seq", "dp"), scatter_dimension=0, tiled=True
        ).astype(F32)

    left_f = lt[:parts].reshape(parts, 4, 4, width // 16, -1).transpose(1, 2, 0, 3, 4)
    down = scatter(dot_nn(left_f.reshape(ff, -1), rt[R_Z]))
    up = scatter(jnp.concatenate([dot_nn(lt[L_N], rt[R_U + j]) for j in range(parts)], axis=1))
    wout = scatter(dot_nn(lt[L_O], rt[R_A]))
    qkv = scatter(jnp.concatenate([dot_nn(lt[L_X], rt[R_P + j]) for j in range(3)], axis=1))
    return qkv, wout, up, down, lax.psum(bg, ("seq", "dp"))


def local(*args):
    sout, sgrad, lt, rt, bg = run_layers(args, None)
    width = lt.shape[1]
    ff = args[7].shape[2]
    index = lax.axis_index("seq") * lax.axis_size("dp") + lax.axis_index("dp")
    count = lax.axis_size("seq") * lax.axis_size("dp")
    if lax.axis_size("dp") == 4:
        out, sums = run_grads(lt, rt, bg)
        down = out[0:4].reshape(-1, width)
        up = jnp.concatenate([out[4], out[5], out[6], out[7]], axis=1)
        wout = out[8]
        qkv = jnp.concatenate([out[9], out[10], out[11]], axis=1)
    else:
        qkv, wout, up, down, sums = grads_by_scatter(lt, rt, bg, ff)
    sums = sums.reshape(-1)

    def piece(start, rows):
        part = sums[start * width:(start + rows) * width]
        size = rows * width // count
        return lax.dynamic_slice_in_dim(part, index * size, size, 0)[None]

    return (
        sout[None],
        sgrad.astype(F32)[None],
        qkv[None],
        piece(0, 2),
        wout[None],
        piece(2, 2),
        up[None],
        piece(4, 4),
        down[None],
        piece(8, 2),
        piece(10, 2),
    )


def solution(mesh):
    return jax.shard_map(
        local,
        mesh=mesh,
        in_specs=(
            P("dp", "seq", None),
            P("dp", "seq", None),
            P("dp"),
            P("section", None, None),
            P("section", None),
            P("section", None, None),
            P("section", None),
            P("section", None, None),
            P("section", None),
            P("section", None, None),
            P("section", None),
            P("section", None),
        ),
        out_specs=(
            P("section", "dp", "seq", None),
            P("section", "dp", "seq", None),
            P("section", ("seq", "dp"), None),
            P("section", ("seq", "dp")),
            P("section", ("seq", "dp"), None),
            P("section", ("seq", "dp")),
            P("section", ("seq", "dp"), None),
            P("section", ("seq", "dp")),
            P("section", ("seq", "dp"), None),
            P("section", ("seq", "dp")),
            P("section", ("seq", "dp")),
        ),
        check_vma=False,
    )
```

```python
import functools

import jax
import jax.numpy as jnp
from jax import lax
from jax.experimental import pallas as pl
from jax.experimental.pallas import tpu as pltpu
from jax.sharding import PartitionSpec as P

H = 12
MICRO = 2
EPS = 1e-12
MESH = pl.DeviceIdType.MESH
BF = jnp.bfloat16
F32 = jnp.float32
LANES = 128
INV_SQRT_2PI = 0.3989422804014327
INV_SQRT_2 = 0.7071067811865476
L_F, L_N, L_O, L_X, L_COUNT = 0, 4, 5, 6, 7
R_P, R_A, R_U, R_Z, R_COUNT = 0, 3, 4, 8, 9
CHUNKS = 12
Z_FIRST = 2


def dot_nn(a, b):
    return lax.dot_general(a, b, (((1,), (0,)), ((), ())), preferred_element_type=F32)


def dot_nt(a, b):
    return lax.dot_general(a, b, (((1,), (1,)), ((), ())), preferred_element_type=F32)


def dot_tn(a, b):
    return lax.dot_general(a, b, (((0,), (0,)), ((), ())), preferred_element_type=F32)


def layers_kernel(
    len_ref, in_hbm, cot_hbm, wqkv_hbm, wout_hbm, wup_hbm, wdown_hbm,
    abias_ref, obias_ref, bup_ref, gain_ref, shift_ref,
    sout_hbm, sgrad_hbm, lt, rt, bg,
    ab, wqkv, wout, wup, wdown, q_s, kv, lse, o_s, n_s, xh1, xh2, rs1, rs2, gp, dr1, acc, do_s,
    dkv_own, dkv_send, dkv_recv, yb, gb,
    w_sem, loc_sem, ex_send, ex_recv, hop_send, hop_recv, kv_send, kv_rsem, dk_ssem, dk_rsem,
    out_loc, out_send, out_recv,
):
    width = wqkv.shape[0]
    ff = wup.shape[1]
    span = in_hbm.shape[1]
    rows = 2 * span
    keys = 2 * rows
    hd = width // H
    pairs = H // 2
    half_pairs = H // 4
    nff = ff // width
    dp_size = 4
    unit = width // 16
    sec = lax.axis_index("section")
    seq = lax.axis_index("seq")
    dp = lax.axis_index("dp")
    hi = seq // 2
    lo = seq % 2
    core_dev = (sec, hi * 2 + 1 - lo, dp)
    y_dev = (sec, (1 - hi) * 2 + lo, dp)
    x_dev = (1 - sec, seq, dp)

    weight_copies = [
        pltpu.make_async_copy(src.at[0], dst, w_sem.at[i])
        for i, (src, dst) in enumerate(
            ((wqkv_hbm, wqkv), (wout_hbm, wout), (wup_hbm, wup), (wdown_hbm, wdown))
        )
    ]
    for copy in weight_copies:
        copy.start()

    barrier = pltpu.get_barrier_semaphore()
    for dev in (core_dev, y_dev, x_dev):
        pl.semaphore_signal(barrier, inc=1, device_id=dev, device_id_type=MESH)
    pl.semaphore_wait(barrier, 3)

    def own_copy(src, m):
        return pltpu.make_async_copy(
            src.at[2 * hi + m], ab.at[0, pl.ds(m * rows, span)], loc_sem.at[m]
        )

    def y_copy(src, m):
        return pltpu.make_async_remote_copy(
            src_ref=src.at[2 * (1 - hi) + m],
            dst_ref=ab.at[0, pl.ds(m * rows + span, span)],
            send_sem=ex_send.at[m], recv_sem=ex_recv.at[m],
            device_id=y_dev, device_id_type=MESH,
        )

    for is_sec, src in ((0, in_hbm), (1, cot_hbm)):
        @pl.when(sec == is_sec)
        def _(src=src):
            for m in range(MICRO):
                y_copy(src, m).start()
                own_copy(src, m).start()

    bg[...] = jnp.zeros_like(bg)

    def mrows(m):
        return pl.ds(pl.multiple_of(m * rows, rows), rows)

    def hop_copy(src, m):
        return pltpu.make_async_remote_copy(
            src_ref=src.at[mrows(m)], dst_ref=ab.at[1, mrows(m)],
            send_sem=hop_send.at[m], recv_sem=hop_recv.at[m],
            device_id=x_dev, device_id_type=MESH,
        )

    def kv_copy(m, part):
        return pltpu.make_async_remote_copy(
            src_ref=kv.at[m, part, pl.ds(0, rows)], dst_ref=kv.at[m, part, pl.ds(rows, rows)],
            send_sem=kv_send.at[m, part], recv_sem=kv_rsem.at[m, part],
            device_id=core_dev, device_id_type=MESH,
        )

    def dkv_copy(m, group):
        return pltpu.make_async_remote_copy(
            src_ref=dkv_send.at[m, group], dst_ref=dkv_recv.at[m, group],
            send_sem=dk_ssem.at[m, group], recv_sem=dk_rsem.at[m, group],
            device_id=core_dev, device_id_type=MESH,
        )

    def out_copies(kind, src, dst, m):
        table = 2 * hi + m
        base = m * rows
        return (
            pltpu.make_async_copy(
                src.at[pl.ds(base, span)], dst.at[table], out_loc.at[kind, m]
            ),
            pltpu.make_async_remote_copy(
                src_ref=src.at[pl.ds(base + span, span)], dst_ref=dst.at[table],
                send_sem=out_send.at[kind, m], recv_sem=out_recv.at[kind, m],
                device_id=y_dev, device_id_type=MESH,
            ),
        )

    def wait_slot(which, m):
        @pl.when(which == 0)
        def _():
            own_copy(in_hbm, m).wait()
            y_copy(in_hbm, m).wait_recv()

        @pl.when(which == 1)
        def _():
            hop_copy(yb, m).wait_recv()

    def positions(shape):
        row = lax.broadcasted_iota(jnp.int32, shape, 0)
        block = row // span
        within = row % span
        half = jnp.where(block % 2 == 0, hi, 1 - hi)
        core = jnp.where(block < 2, lo, 1 - lo)
        return (half * 2 + core) * span + within

    def lane_masks():
        lane = lax.broadcasted_iota(jnp.int32, (1, LANES), 1)
        left = (lane < hd).astype(F32).astype(BF)
        right = (lane >= hd).astype(F32).astype(BF)
        return left, right

    def split_heads(value):
        left, right = lane_masks()
        return jnp.concatenate([value * left, value * right], axis=0)

    def norm(resid, gain, shift):
        average = jnp.mean(resid, axis=-1, keepdims=True)
        centred = resid - average
        spread = jnp.mean(centred * centred, axis=-1, keepdims=True)
        scale = lax.rsqrt(spread + EPS)
        hat = centred * scale
        return hat, scale, hat * gain + shift

    def norm_back(grad, hat, scale, gain):
        dh = grad * gain
        return scale * (
            dh
            - jnp.mean(dh, axis=-1, keepdims=True)
            - hat * jnp.mean(dh * hat, axis=-1, keepdims=True)
        )

    def vec(ref, part):
        return ref[0:1, part * width:(part + 1) * width].astype(F32)

    def add_bias_grad(row, value):
        bg[row] += jnp.sum(value, axis=0, keepdims=True)

    def forward(step, m):
        r = mrows(m)
        wait_slot(sec, m)

        @pl.when(step == 0)
        def _():
            weight_copies[0].wait()

        x = ab[sec, r]
        kv[m, 0, pl.ds(0, rows)] = dot_nn(x, wqkv[:, width:2 * width]).astype(BF)
        kv_copy(m, 0).start()
        kv[m, 1, pl.ds(0, rows)] = (
            dot_nn(x, wqkv[:, 2 * width:3 * width]) + vec(abias_ref, 1)
        ).astype(BF)
        kv_copy(m, 1).start()
        queries = (dot_nn(x, wqkv[:, 0:width]) + vec(abias_ref, 0)).astype(BF)
        q_s[r] = queries * (hd ** -0.5)

        @pl.when(step == 0)
        def _():
            for copy in weight_copies[1:]:
                copy.wait()

        lt[L_X, :, r] = x.T
        kv_copy(m, 0).wait_recv()
        kv_copy(m, 1).wait_recv()
        key_bias = jnp.where(positions((keys, 1)) < len_ref[2 * hi + m], 0.0, -1e30)

        def head_pair(p, carry):
            cols = pl.ds(pl.multiple_of(p * LANES, LANES), LANES)
            qq = split_heads(q_s[r, cols])
            st = dot_nt(kv[m, 0, :, cols], qq) + key_bias
            top = jnp.max(st, axis=0, keepdims=True)
            e = jnp.exp(st - top)
            total = jnp.sum(e, axis=0, keepdims=True)
            lse[m, p] = top + jnp.log(total)
            o_t = dot_tn(kv[m, 1, :, cols], e.astype(BF)) * (1.0 / total)
            o_pair = jnp.concatenate([o_t[0:hd, 0:rows], o_t[hd:2 * hd, rows:2 * rows]], axis=0)
            lt[L_O, cols, r] = o_pair.astype(BF)
            o_s[:, cols] = o_pair.T.astype(BF)
            return carry

        lax.fori_loop(0, pairs, head_pair, 0, unroll=True)

        r1 = x.astype(F32) + dot_nn(o_s[...], wout[...]) + vec(obias_ref, 0)
        hat, scale, n1 = norm(r1, vec(gain_ref, 0), vec(shift_ref, 0))
        xh1[r] = hat
        rs1[r] = jnp.broadcast_to(scale, (rows, LANES))
        n_s[...] = n1.astype(BF)
        acc[...] = n1 + vec(obias_ref, 1)

        def ff_chunk(j, carry):
            cols = pl.ds(pl.multiple_of(j * width, width), width)
            u = dot_nn(n_s[...], wup[:, cols]) + bup_ref[0:1, cols].astype(F32)
            phi = 0.5 + 0.5 * lax.erf(u * INV_SQRT_2)
            f = (u * phi).astype(BF)
            f_t = f.T
            for z in range(dp_size):
                for part in range(nff):
                    lt[part, pl.ds((j * dp_size + z) * unit, unit), r] = f_t[
                        (z * nff + part) * unit:(z * nff + part + 1) * unit
                    ]
            gp[r, cols] = (phi + u * (jnp.exp(-0.5 * u * u) * INV_SQRT_2PI)).astype(BF)
            acc[...] += dot_nn(f, wdown[cols, :])
            return carry

        lax.fori_loop(0, nff, ff_chunk, 0, unroll=True)
        hat, scale, result = norm(acc[...], vec(gain_ref, 1), vec(shift_ref, 1))
        xh2[r] = hat
        rs2[r] = jnp.broadcast_to(scale, (rows, LANES))
        yb[r] = result.astype(BF)

        @pl.when(sec == 0)
        def _():
            hop_copy(yb, m).start()

        for copy in out_copies(0, yb, sout_hbm, m):
            copy.start()
        lt[L_N, :, r] = n_s[...].T

    def backward(step, m):
        r = mrows(m)
        wait_slot(1 - sec, m)
        length = len_ref[2 * hi + m]
        row_pos = positions((rows, 1))
        row_scale = jnp.where((sec == 0) | (row_pos < length), 1.0, 0.0)
        dy = ab[1 - sec, r].astype(F32) * row_scale
        hat = xh2[r]
        add_bias_grad(9, dy * hat)
        add_bias_grad(11, dy)
        dr2 = norm_back(dy, hat, rs2[r, 0:1], vec(gain_ref, 1))
        dz = dr2.astype(BF)
        rt[R_Z, r] = dz
        add_bias_grad(3, dz.astype(F32))
        acc[...] = dr2

        def ff_chunk(j, carry):
            cols = pl.ds(pl.multiple_of(j * width, width), width)
            du = (dot_nt(rt[R_Z, r], wdown[cols, :]) * gp[r, cols].astype(F32)).astype(BF)
            rt[R_U + j, r] = du
            bg[4 + j] += jnp.sum(du.astype(F32), axis=0, keepdims=True)
            acc[...] += dot_nt(du, wup[:, cols])
            return carry

        lax.fori_loop(0, nff, ff_chunk, 0, unroll=True)
        dn1 = acc[...]
        hat = xh1[r]
        add_bias_grad(8, dn1 * hat)
        add_bias_grad(10, dn1)
        grad1 = norm_back(dn1, hat, rs1[r, 0:1], vec(gain_ref, 0))
        dr1[...] = grad1
        da = grad1.astype(BF)
        rt[R_A, r] = da
        add_bias_grad(2, da.astype(F32))
        do_s[...] = dot_nt(da, wout[...]).astype(BF)
        key_bias = jnp.where(positions((keys, 1)) < length, 0.0, -1e30)

        def head_pair(group, index):
            p = group * half_pairs + index
            cols = pl.ds(p * LANES, LANES)
            kcols = pl.ds(index * LANES, LANES)
            vcols = pl.ds((half_pairs + index) * LANES, LANES)
            qq = split_heads(q_s[r, cols])
            dd = split_heads(do_s[:, cols])
            kp = kv[m, 0, :, cols]
            pt = jnp.exp(dot_nt(kp, qq) + key_bias - lse[m, p])
            dv = dot_nn(pt.astype(BF), dd)
            dpt = dot_nt(kv[m, 1, :, cols], dd)
            inner = jnp.sum(pt * dpt, axis=0, keepdims=True)
            ds = (pt * (dpt - inner)).astype(BF)
            dk = dot_nn(ds, qq)
            dq_t = dot_tn(kp, ds)
            dq_pair = jnp.concatenate([dq_t[0:hd, 0:rows], dq_t[hd:2 * hd, rows:2 * rows]], axis=0)
            rt[R_P, r, cols] = (dq_pair.T * (hd ** -0.5)).astype(BF)
            dkv_own[group, :, kcols] = dk[0:rows]
            dkv_own[group, :, vcols] = dv[0:rows]
            dkv_send[m, group, :, kcols] = dk[rows:keys].astype(BF)
            dkv_send[m, group, :, vcols] = dv[rows:keys].astype(BF)

        for group in range(2):
            for index in range(half_pairs):
                head_pair(group, index)
            dkv_copy(m, group).start()
        dq = rt[R_P, r]
        add_bias_grad(0, dq.astype(F32))
        dx = dr1[...] + dot_nt(dq, wqkv[:, 0:width])
        part = width // 2
        for group in range(2):
            dkv_copy(m, group).wait_recv()
            both = (dkv_own[group] + dkv_recv[m, group].astype(F32)).astype(BF)
            for which in range(2):
                at = (1 + which) * width + group * part
                piece = both[:, which * part:(which + 1) * part]
                rt[R_P + 1 + which, r, group * part:(group + 1) * part] = piece
                dx = dx + dot_nt(piece, wqkv[:, at:at + part])
        add_bias_grad(1, rt[R_P + 2, r].astype(F32))
        gb[r] = dx.astype(BF)

        @pl.when(sec == 1)
        def _():
            hop_copy(gb, m).start()

        for copy in out_copies(1, gb, sgrad_hbm, m):
            copy.start()

    def one_step(step, carry):
        is_forward = (step == 0) | ((step == 1) & (sec == 0)) | ((step == 2) & (sec == 1))
        m = jnp.where(sec == 0, step % 2, step // 2)

        @pl.when(is_forward)
        def _():
            forward(step, m)

        @pl.when(jnp.logical_not(is_forward))
        def _():
            backward(step, m)

        return carry

    lax.fori_loop(0, 2 * MICRO, one_step, 0)

    for m in range(MICRO):
        y_copy(in_hbm, m).wait_send()
        hop_copy(yb, m).wait_send()
        for part in range(2):
            kv_copy(m, part).wait_send()
            dkv_copy(m, part).wait_send()
        for kind, src, dst in ((0, yb, sout_hbm), (1, gb, sgrad_hbm)):
            local_out, remote_out = out_copies(kind, src, dst, m)
            local_out.wait()
            remote_out.wait()


def run_layers(args, shapes):
    (inputs, cotangent, lengths, w_qkv, attn_bias, w_out, out_bias, w_up, bias_up, w_down,
     norm_gain, norm_bias) = args
    tables, span, width = inputs.shape
    ff = w_up.shape[2]
    rows = 2 * span
    total = MICRO * rows
    keys = 2 * rows
    any_spec = pl.BlockSpec(memory_space=pl.ANY)
    vmem = pl.BlockSpec(memory_space=pltpu.VMEM)
    smem = pl.BlockSpec(memory_space=pltpu.SMEM)
    dma = pltpu.SemaphoreType.DMA
    return pl.pallas_call(
        layers_kernel,
        name="layers",
        out_shape=(
            jax.ShapeDtypeStruct((tables, span, width), BF),
            jax.ShapeDtypeStruct((tables, span, width), BF),
            jax.ShapeDtypeStruct((L_COUNT, width, total), BF),
            jax.ShapeDtypeStruct((R_COUNT, total, width), BF),
            jax.ShapeDtypeStruct((12, 1, width), F32),
        ),
        in_specs=[smem] + [any_spec] * 6 + [vmem] * 5,
        out_specs=(any_spec, any_spec) + (vmem,) * 3,
        scratch_shapes=[
            pltpu.VMEM((2, total, width), BF),
            pltpu.VMEM((width, 3 * width), BF),
            pltpu.VMEM((width, width), BF),
            pltpu.VMEM((width, ff), BF),
            pltpu.VMEM((ff, width), BF),
            pltpu.VMEM((total, width), BF),
            pltpu.VMEM((MICRO, 2, keys, width), BF),
            pltpu.VMEM((MICRO, H // 2, 1, 2 * rows), F32),
            pltpu.VMEM((rows, width), BF),
            pltpu.VMEM((rows, width), BF),
            pltpu.VMEM((total, width), F32),
            pltpu.VMEM((total, width), F32),
            pltpu.VMEM((total, LANES), F32),
            pltpu.VMEM((total, LANES), F32),
            pltpu.VMEM((total, ff), BF),
            pltpu.VMEM((rows, width), F32),
            pltpu.VMEM((rows, width), F32),
            pltpu.VMEM((rows, width), BF),
            pltpu.VMEM((2, rows, width), F32),
            pltpu.VMEM((MICRO, 2, rows, width), BF),
            pltpu.VMEM((MICRO, 2, rows, width), BF),
            pltpu.VMEM((total, width), BF),
            pltpu.VMEM((total, width), BF),
            dma((4,)), dma((MICRO,)), dma((MICRO,)), dma((MICRO,)), dma((MICRO,)), dma((MICRO,)),
            dma((MICRO, 2)), dma((MICRO, 2)), dma((MICRO, 2)), dma((MICRO, 2)),
            dma((2, MICRO)), dma((2, MICRO)), dma((2, MICRO)),
        ],
        compiler_params=pltpu.CompilerParams(
            collective_id=0, has_side_effects=True, vmem_limit_bytes=60 * 2 ** 20
        ),
    )(lengths, inputs, cotangent, w_qkv, w_out, w_up, w_down,
      attn_bias, out_bias, bias_up, norm_gain, norm_bias)


def grads_kernel(
    lt, rt, bg,
    out, bg_out,
    core_src, chip, own, y_buf, up, down, turn_src, turn_buf, b_src, b_core, b_y, b_z,
    core_ss, core_rs, y_ss, y_rs, up_ss, up_rs, down_ss, down_rs, turn_ss, turn_rs,
    bc_ss, bc_rs, bz_ss, bz_rs,
):
    count = b_z.shape[0]
    unit = out.shape[1]
    block = count * unit
    sec = lax.axis_index("section")
    seq = lax.axis_index("seq")
    z = lax.axis_index("dp")
    hi = seq // 2
    lo = seq % 2
    core_dev = (sec, hi * 2 + 1 - lo, z)
    y_dev = (sec, (1 - hi) * 2 + lo, z)

    def z_dev(index):
        return (sec, seq, index)

    barrier = pltpu.get_barrier_semaphore()
    for dev in (core_dev, y_dev):
        pl.semaphore_signal(barrier, inc=1, device_id=dev, device_id_type=MESH)
    for by in range(1, count):
        pl.semaphore_signal(
            barrier, inc=1, device_id=z_dev((z + by) % count), device_id_type=MESH
        )
    pl.semaphore_wait(barrier, 1 + count)

    def remote(src, dst, send, recv, dev):
        return pltpu.make_async_remote_copy(
            src_ref=src, dst_ref=dst, send_sem=send, recv_sem=recv,
            device_id=dev, device_id_type=MESH,
        )

    def core_copy(k, half):
        return remote(
            core_src.at[k, half], chip.at[k, half], core_ss.at[k, half], core_rs.at[k, half], core_dev
        )

    def y_copy(k):
        return remote(chip.at[k, 1 - hi], y_buf.at[k], y_ss.at[k], y_rs.at[k], y_dev)

    def turn_copy(k):
        return remote(turn_src.at[k], turn_buf.at[k], turn_ss.at[k], turn_rs.at[k], y_dev)

    def piece(k, half, target):
        return chip.at[k, half, pl.ds(pl.multiple_of(target * unit, unit), unit)]

    def up_copy(job, k, half, target):
        return remote(
            piece(k, half, target), up.at[job, target], up_ss.at[job, target],
            up_rs.at[job, target], z_dev(jnp.minimum(z + 1, count - 1)),
        )

    def down_copy(job, k, half, target):
        return remote(
            piece(k, half, target), down.at[job, target], down_ss.at[job, target],
            down_rs.at[job, target], z_dev(jnp.maximum(z - 1, 0)),
        )

    def add_piece(k, half, target, landed):
        ref = piece(k, half, target)
        ref[...] = (ref[...].astype(F32) + landed[...].astype(F32)).astype(BF)

    def hop(number, job, k, half):
        @pl.when(z == number - 1)
        def _():
            for target in range(count - 1, number - 1, -1):
                if number > 1:
                    up_copy(job, k, half, target).wait_recv()
                    add_piece(k, half, target, up.at[job, target])
                up_copy(job, k, half, target).start()

        @pl.when(z == count - number)
        def _():
            for target in range(0, count - number):
                if number > 1:
                    down_copy(job, k, half, target).wait_recv()
                    add_piece(k, half, target, down.at[job, target])
                down_copy(job, k, half, target).start()

    def arrive(job, k, half, dst):
        dst[...] = piece(k, half, z)[...].astype(F32)

        @pl.when(z > 0)
        def _():
            up_copy(job, k, half, z).wait_recv()
            dst[...] += up[job, z].astype(F32)

        @pl.when(z < count - 1)
        def _():
            down_copy(job, k, half, z).wait_recv()
            dst[...] += down[job, z].astype(F32)

    def product(k):
        left = jnp.where(k < 8, jnp.minimum(k, L_N), jnp.where(k == 8, L_O, L_X))
        right = jnp.where(k < 4, R_Z, jnp.where(k < 8, k, jnp.where(k == 8, R_A, k - 9)))
        for half in range(2):
            base = pl.multiple_of((half * 2 + 1 - lo) * block, block)
            core_src[k, half] = dot_nn(lt[left, pl.ds(base, block), :], rt[right]).astype(BF)
            core_copy(k, half).start()
        for half in range(2):
            base = pl.multiple_of((half * 2 + lo) * block, block)
            own[k % 2, half] = dot_nn(lt[left, pl.ds(base, block), :], rt[right])

    def chip_sum(k):
        for half in range(2):
            core_copy(k, half).wait_recv()
            chip[k, half] = (own[k % 2, half] + chip[k, half].astype(F32)).astype(BF)

    def bias_core():
        return remote(b_src.at[0], b_core, bc_ss.at[0], bc_rs.at[0], core_dev)

    def bias_y():
        return remote(b_src.at[1], b_y, bc_ss.at[1], bc_rs.at[1], y_dev)

    def bias_z(by):
        return remote(
            b_src.at[2], b_z.at[by], bz_ss.at[by], bz_rs.at[by], z_dev((z + by) % count)
        )

    def step(t, carry):
        def at(first, last):
            return (t >= first) & (t <= last)

        @pl.when(t == 0)
        def _():
            b_src[0] = bg[...]
            bias_core().start()

        @pl.when(t < CHUNKS)
        def _():
            product(t)

        @pl.when(at(1, CHUNKS))
        def _():
            chip_sum(t - 1)

        @pl.when(at(1, Z_FIRST))
        def _():
            for half in range(2):
                hop(1, 2 * (t - 1) + half, t - 1, half)

        @pl.when(at(Z_FIRST + 1, CHUNKS))
        def _():
            y_copy(t - 1).start()

        @pl.when(t == 2)
        def _():
            bias_core().wait_recv()
            b_src[1] = b_src[0] + b_core[...]
            bias_y().start()

        @pl.when(t == 4)
        def _():
            bias_y().wait_recv()
            b_src[2] = b_src[1] + b_y[...]
            for by in range(1, count):
                bias_z(by).start()

        @pl.when(at(Z_FIRST + 3, CHUNKS + 2))
        def _():
            k = t - 3
            y_copy(k).wait_recv()
            chip[k, hi] = (chip[k, hi].astype(F32) + y_buf[k].astype(F32)).astype(BF)
            hop(1, k + Z_FIRST, k, hi)

        for number in range(2, count):
            @pl.when(at(Z_FIRST + 2 + number, CHUNKS + 1 + number))
            def _(number=number):
                k = t - 2 - number
                hop(number, k + Z_FIRST, k, hi)

            @pl.when(at(2 * number, 2 * number + Z_FIRST - 1))
            def _(number=number):
                k = t - 2 * number
                for half in range(2):
                    hop(number, 2 * k + half, k, half)

        @pl.when(at(Z_FIRST + 2 + count, CHUNKS + 1 + count))
        def _():
            k = t - 2 - count
            arrive(k + Z_FIRST, k, hi, out.at[k])

        @pl.when(at(2 * count, 2 * count + Z_FIRST - 1))
        def _():
            k = t - 2 * count
            arrive(2 * k + 1 - hi, k, 1 - hi, out.at[k])
            turn_src[k] = out[k].astype(BF)
            turn_copy(k).start()
            arrive(2 * k + hi, k, hi, out.at[k])

        @pl.when(at(2 * count + 2, 2 * count + 1 + Z_FIRST))
        def _():
            k = t - 2 * count - 2
            turn_copy(k).wait_recv()
            out[k] += turn_buf[k].astype(F32)

        return carry

    lax.fori_loop(0, CHUNKS + 2 + count, step, 0)

    for by in range(1, count):
        bias_z(by).wait_recv()
    total = b_src[2]
    for by in range(1, count):
        total = total + b_z[by]
    bg_out[...] = total
    bias_core().wait_send()
    bias_y().wait_send()
    for by in range(1, count):
        bias_z(by).wait_send()

    def sent(job, k, half):
        for target in range(count):
            @pl.when(target > z)
            def _(target=target):
                up_copy(job, k, half, target).wait_send()

            @pl.when(target < z)
            def _(target=target):
                down_copy(job, k, half, target).wait_send()

    def drain(k, carry):
        for half in range(2):
            core_copy(k, half).wait_send()

        @pl.when(k < Z_FIRST)
        def _():
            turn_copy(k).wait_send()
            for half in range(2):
                sent(2 * k + half, k, half)

        @pl.when(k >= Z_FIRST)
        def _():
            y_copy(k).wait_send()
            sent(k + Z_FIRST, k, hi)

        return carry

    lax.fori_loop(0, CHUNKS, drain, 0)


def run_grads(lt, rt, bg):
    count = lax.axis_size("dp")
    width = lt.shape[1]
    unit = width // (4 * count)
    block = count * unit
    jobs = CHUNKS + Z_FIRST
    vmem = pl.BlockSpec(memory_space=pltpu.VMEM)
    dma = pltpu.SemaphoreType.DMA
    return pl.pallas_call(
        grads_kernel,
        name="grads",
        out_shape=(
            jax.ShapeDtypeStruct((CHUNKS, unit, width), F32),
            jax.ShapeDtypeStruct((12, 1, width), F32),
        ),
        in_specs=[vmem] * 3,
        out_specs=(vmem,) * 2,
        scratch_shapes=[
            pltpu.VMEM((CHUNKS, 2, block, width), BF),
            pltpu.VMEM((CHUNKS, 2, block, width), BF),
            pltpu.VMEM((2, 2, block, width), F32),
            pltpu.VMEM((CHUNKS, block, width), BF),
            pltpu.VMEM((jobs, count, unit, width), BF),
            pltpu.VMEM((jobs, count, unit, width), BF),
            pltpu.VMEM((Z_FIRST, unit, width), BF),
            pltpu.VMEM((Z_FIRST, unit, width), BF),
            pltpu.VMEM((3, 12, 1, width), F32),
            pltpu.VMEM((12, 1, width), F32),
            pltpu.VMEM((12, 1, width), F32),
            pltpu.VMEM((count, 12, 1, width), F32),
            dma((CHUNKS, 2)), dma((CHUNKS, 2)), dma((CHUNKS,)), dma((CHUNKS,)),
            dma((jobs, count)), dma((jobs, count)), dma((jobs, count)), dma((jobs, count)),
            dma((Z_FIRST,)), dma((Z_FIRST,)), dma((2,)), dma((2,)), dma((count,)), dma((count,)),
        ],
        compiler_params=pltpu.CompilerParams(
            collective_id=1, has_side_effects=True, vmem_limit_bytes=60 * 2 ** 20
        ),
    )(lt, rt, bg)


def grads_by_scatter(lt, rt, bg, ff):
    width = lt.shape[1]
    parts = ff // width

    def scatter(full):
        return lax.psum_scatter(
            full.astype(BF), ("seq", "dp"), scatter_dimension=0, tiled=True
        ).astype(F32)

    left_f = lt[:parts].reshape(parts, 4, 4, width // 16, -1).transpose(1, 2, 0, 3, 4)
    down = scatter(dot_nn(left_f.reshape(ff, -1), rt[R_Z]))
    up = scatter(jnp.concatenate([dot_nn(lt[L_N], rt[R_U + j]) for j in range(parts)], axis=1))
    wout = scatter(dot_nn(lt[L_O], rt[R_A]))
    qkv = scatter(jnp.concatenate([dot_nn(lt[L_X], rt[R_P + j]) for j in range(3)], axis=1))
    return qkv, wout, up, down, lax.psum(bg, ("seq", "dp"))


def finish_kernel(
    sout, sgrad, grads, sums,
    sout_ref, sgrad_ref, qkv_ref, abias_ref, wout_ref, obias_ref, up_ref, bup_ref, down_ref,
    gain_ref, shift_ref, sem,
):
    copy = pltpu.make_async_copy(sout, sout_ref.at[0], sem)
    copy.start()
    width = grads.shape[2]
    unit = grads.shape[1]
    size = abias_ref.shape[1]
    index = lax.axis_index("seq") * lax.axis_size("dp") + lax.axis_index("dp")
    for k in range(CHUNKS):
        if k < 4:
            down_ref[0, k * unit:(k + 1) * unit, :] = grads[k]
        elif k < 8:
            up_ref[0, :, (k - 4) * width:(k - 3) * width] = grads[k]
        elif k == 8:
            wout_ref[0] = grads[k]
        else:
            qkv_ref[0, :, (k - 9) * width:(k - 8) * width] = grads[k]
    sgrad_ref[0] = sgrad[...].astype(F32)
    whole = width // size
    low = index < whole
    pairs = [jnp.where(low, sums[row], sums[row + 1]) for row in (0, 2, 8, 10)]
    block = jnp.concatenate(pairs + pairs, axis=0)
    block = pltpu.roll(block, (width - (index % whole) * size) % width, axis=1)
    for row, ref in enumerate((abias_ref, obias_ref, gain_ref, shift_ref)):
        ref[...] = block[row:row + 1, 0:size]
    wide = 2 * size
    per = width // wide
    rows = sums[4]
    for row in range(1, 4):
        rows = jnp.where(index // per == row, sums[4 + row], rows)
    rows = pltpu.roll(
        jnp.concatenate([rows] * 8, axis=0), (width - (index % per) * wide) % width, axis=1
    )
    bup_ref[...] = rows[0:1, 0:wide]
    copy.wait()


def run_finish(sout, sgrad, grads, sums):
    unit, width = grads.shape[1:]
    size = width // 8
    vmem = pl.BlockSpec(memory_space=pltpu.VMEM)
    any_spec = pl.BlockSpec(memory_space=pl.ANY)
    shape = jax.ShapeDtypeStruct
    return pl.pallas_call(
        finish_kernel,
        name="finish",
        out_shape=(
            shape((1,) + sout.shape, BF),
            shape((1,) + sgrad.shape, F32),
            shape((1, unit, 3 * width), F32),
            shape((1, size), F32),
            shape((1, unit, width), F32),
            shape((1, size), F32),
            shape((1, unit, 4 * width), F32),
            shape((1, 2 * size), F32),
            shape((1, 4 * unit, width), F32),
            shape((1, size), F32),
            shape((1, size), F32),
        ),
        in_specs=[any_spec] + [vmem] * 3,
        out_specs=(any_spec,) + (vmem,) * 10,
        scratch_shapes=[pltpu.SemaphoreType.DMA],
        compiler_params=pltpu.CompilerParams(vmem_limit_bytes=32 * 2 ** 20),
    )(sout, sgrad, grads, sums)


def local(*args):
    sout, sgrad, lt, rt, bg = run_layers(args, None)
    width = lt.shape[1]
    ff = args[7].shape[2]
    index = lax.axis_index("seq") * lax.axis_size("dp") + lax.axis_index("dp")
    count = lax.axis_size("seq") * lax.axis_size("dp")
    if lax.axis_size("dp") == 4:
        out, sums = run_grads(lt, rt, bg)
        return run_finish(sout, sgrad, out, sums)
    qkv, wout, up, down, sums = grads_by_scatter(lt, rt, bg, ff)
    sums = sums.reshape(-1)

    def piece(start, rows):
        part = sums[start * width:(start + rows) * width]
        size = rows * width // count
        return lax.dynamic_slice_in_dim(part, index * size, size, 0)[None]

    return (
        sout[None],
        sgrad.astype(F32)[None],
        qkv[None],
        piece(0, 2),
        wout[None],
        piece(2, 2),
        up[None],
        piece(4, 4),
        down[None],
        piece(8, 2),
        piece(10, 2),
    )


def solution(mesh):
    return jax.shard_map(
        local,
        mesh=mesh,
        in_specs=(
            P("dp", "seq", None),
            P("dp", "seq", None),
            P("dp"),
            P("section", None, None),
            P("section", None),
            P("section", None, None),
            P("section", None),
            P("section", None, None),
            P("section", None),
            P("section", None, None),
            P("section", None),
            P("section", None),
        ),
        out_specs=(
            P("section", "dp", "seq", None),
            P("section", "dp", "seq", None),
            P("section", ("seq", "dp"), None),
            P("section", ("seq", "dp")),
            P("section", ("seq", "dp"), None),
            P("section", ("seq", "dp")),
            P("section", ("seq", "dp"), None),
            P("section", ("seq", "dp")),
            P("section", ("seq", "dp"), None),
            P("section", ("seq", "dp")),
            P("section", ("seq", "dp")),
        ),
        check_vma=False,
    )
```

```python
import functools

import jax
import jax.numpy as jnp
from jax import lax
from jax.experimental import pallas as pl
from jax.experimental.pallas import tpu as pltpu
from jax.sharding import PartitionSpec as P

H = 12
MICRO = 2
EPS = 1e-12
MESH = pl.DeviceIdType.MESH
BF = jnp.bfloat16
F32 = jnp.float32
LANES = 128
INV_SQRT_2PI = 0.3989422804014327
INV_SQRT_2 = 0.7071067811865476
L_F, L_N, L_O, L_X, L_COUNT = 0, 4, 5, 6, 7
R_P, R_A, R_U, R_Z, R_COUNT = 0, 3, 4, 8, 9
CHUNKS = 12
Z_FIRST = (1, 3)
EARLY = 6
DEDICATED = 6
Y_SLOTS = 8
STEPS = 20
VMEM_LIMIT = 63 * 2 ** 20


def dot_nn(a, b):
    return lax.dot_general(a, b, (((1,), (0,)), ((), ())), preferred_element_type=F32)


def dot_nt(a, b):
    return lax.dot_general(a, b, (((1,), (1,)), ((), ())), preferred_element_type=F32)


def dot_tn(a, b):
    return lax.dot_general(a, b, (((0,), (0,)), ((), ())), preferred_element_type=F32)


def train_kernel(with_sums, *refs):
    refs = iter(refs)

    def take(number):
        return [next(refs) for _ in range(number)]

    (len_ref, in_hbm, cot_hbm, wqkv_hbm, wout_hbm, wup_hbm, wdown_hbm,
     abias_ref, obias_ref, bup_ref, gain_ref, shift_ref) = take(12)
    sout_hbm, sgrad_hbm = take(2)
    if with_sums:
        out, bg_out = take(2)
    else:
        lt, rt, bg = take(3)
    (ab, wqkv, wout, pool, wdown, q_s, kv, lse, o_s, n_s, xh1, xh2, rs1, rs2, dr1, acc, do_s,
     dkv_own, dkv_send, dkv_recv, yb) = take(21)
    (w_sem, loc_sem, ex_send, ex_recv, hop_send, hop_recv, kv_ss, kv_rs, dk_ss, dk_rs,
     out_loc, out_ss, out_rs) = take(13)
    if with_sums:
        (lt, rt, bg, core_src, y_buf, up, down, turn_src, turn_buf,
         b_src, b_core, b_y, b_z) = take(13)
        (core_ss, core_rs, y_ss, y_rs, up_ss, up_rs, down_ss, down_rs, turn_ss, turn_rs,
         bc_ss, bc_rs, bz_ss, bz_rs) = take(14)

    width = wqkv.shape[0]
    ff = wdown.shape[0]
    span = in_hbm.shape[1]
    rows = 2 * span
    keys = 2 * rows
    hd = width // H
    pairs = H // 2
    half_pairs = H // 4
    nff = ff // width
    quarter = 4
    unit = width // 16
    sec = lax.axis_index("section")
    seq = lax.axis_index("seq")
    z = lax.axis_index("dp")
    count = lax.axis_size("dp")
    hi = seq // 2
    lo = seq % 2
    core_dev = (sec, hi * 2 + 1 - lo, z)
    y_dev = (sec, (1 - hi) * 2 + lo, z)
    x_dev = (1 - sec, seq, z)

    def z_dev(index):
        return (sec, seq, index)

    def remote(src, dst, send, recv, dev):
        return pltpu.make_async_remote_copy(
            src_ref=src, dst_ref=dst, send_sem=send, recv_sem=recv,
            device_id=dev, device_id_type=MESH,
        )

    weight_copies = [
        pltpu.make_async_copy(src.at[0], dst, w_sem.at[i])
        for i, (src, dst) in enumerate(((wqkv_hbm, wqkv), (wout_hbm, wout), (wdown_hbm, wdown)))
    ]
    tall = width // 4
    for j in range(nff):
        for part in range(4):
            weight_copies.append(
                pltpu.make_async_copy(
                    wup_hbm.at[0, pl.ds(part * tall, tall), pl.ds(j * width, width)],
                    pool.at[j * 4 + part],
                    w_sem.at[3 + j * 4 + part],
                )
            )
    for copy in weight_copies:
        copy.start()

    partners = [core_dev, y_dev, x_dev]
    if with_sums:
        partners += [z_dev((z + by) % count) for by in range(1, count)]
    barrier = pltpu.get_barrier_semaphore()
    for dev in partners:
        pl.semaphore_signal(barrier, inc=1, device_id=dev, device_id_type=MESH)
    pl.semaphore_wait(barrier, len(partners))

    def mrows(m):
        return pl.ds(pl.multiple_of(m * rows, rows), rows)

    def own_copy(src, m):
        return pltpu.make_async_copy(
            src.at[2 * hi + m], ab.at[0, pl.ds(m * rows, span)], loc_sem.at[m]
        )

    def seq_copy(src, m):
        return remote(
            src.at[2 * (1 - hi) + m], ab.at[0, pl.ds(m * rows + span, span)],
            ex_send.at[m], ex_recv.at[m], y_dev,
        )

    for is_sec, src in ((0, in_hbm), (1, cot_hbm)):
        @pl.when(sec == is_sec)
        def _(src=src):
            for m in range(MICRO):
                seq_copy(src, m).start()
                own_copy(src, m).start()

    bg[...] = jnp.zeros_like(bg)

    def hop_copy(src, m):
        return remote(src.at[mrows(m)], ab.at[1, mrows(m)], hop_send.at[m], hop_recv.at[m], x_dev)

    def kv_copy(m, part):
        return remote(
            kv.at[m, part, pl.ds(0, rows)], kv.at[m, part, pl.ds(rows, rows)],
            kv_ss.at[m, part], kv_rs.at[m, part], core_dev,
        )

    def dkv_copy(m, group):
        return remote(
            dkv_send.at[group], dkv_recv.at[m, group],
            dk_ss.at[m, group], dk_rs.at[m, group], core_dev,
        )

    def out_copies(kind, src, dst, m):
        table = 2 * hi + m
        base = m * rows
        return (
            pltpu.make_async_copy(src.at[pl.ds(base, span)], dst.at[table], out_loc.at[kind, m]),
            remote(
                src.at[pl.ds(base + span, span)], dst.at[table],
                out_ss.at[kind, m], out_rs.at[kind, m], y_dev,
            ),
        )

    def wait_slot(which, m):
        @pl.when(which == 0)
        def _():
            own_copy(in_hbm, m).wait()
            seq_copy(in_hbm, m).wait_recv()

        @pl.when(which == 1)
        def _():
            hop_copy(yb, m).wait_recv()

    def positions(shape, dim):
        row = lax.broadcasted_iota(jnp.int32, shape, dim)
        block = row // span
        within = row % span
        half = jnp.where(block % 2 == 0, hi, 1 - hi)
        core = jnp.where(block < 2, lo, 1 - lo)
        return (half * 2 + core) * span + within

    def left_lanes():
        return lax.broadcasted_iota(jnp.int32, (1, LANES), 1) < hd

    def split_heads(value):
        left = left_lanes().astype(F32)
        return jnp.concatenate([value * left.astype(BF), value * (1.0 - left).astype(BF)], axis=0)

    def norm(resid, gain, shift):
        average = jnp.mean(resid, axis=-1, keepdims=True)
        centred = resid - average
        spread = jnp.mean(centred * centred, axis=-1, keepdims=True)
        scale = lax.rsqrt(spread + EPS)
        hat = centred * scale
        return hat, scale, hat * gain + shift

    def norm_back(grad, hat, scale, gain):
        dh = grad * gain
        return scale * (
            dh
            - jnp.mean(dh, axis=-1, keepdims=True)
            - hat * jnp.mean(dh * hat, axis=-1, keepdims=True)
        )

    def wup(j):
        return pool[4 * j:4 * j + 4].reshape(width, width)

    def vec(ref, part):
        return ref[0:1, part * width:(part + 1) * width].astype(F32)

    def add_bias_grad(row, value):
        bg[row] += jnp.sum(value, axis=0, keepdims=True)


    def project(step, m):
        r = mrows(m)
        wait_slot(sec, m)

        @pl.when(step == 0)
        def _():
            weight_copies[0].wait()

        x = ab[sec, r]
        kv[m, 0, pl.ds(0, rows)] = dot_nn(x, wqkv[:, width:2 * width]).astype(BF)
        kv_copy(m, 0).start()
        kv[m, 1, pl.ds(0, rows)] = (
            dot_nn(x, wqkv[:, 2 * width:3 * width]) + vec(abias_ref, 1)
        ).astype(BF)
        kv_copy(m, 1).start()
        queries = (dot_nn(x, wqkv[:, 0:width]) + vec(abias_ref, 0)).astype(BF)
        q_s[r] = queries * (hd ** -0.5)
        lt[L_X, :, r] = x.T

        @pl.when(step == 0)
        def _():
            for copy in weight_copies[1:]:
                copy.wait()

    def forward(m):
        r = mrows(m)
        kv_copy(m, 0).wait_recv()
        kv_copy(m, 1).wait_recv()
        key_bias = jnp.where(positions((1, keys), 1) < len_ref[2 * hi + m], 0.0, -1e30)
        lane = lax.broadcasted_iota(jnp.int32, (1, LANES), 1)
        stats = jnp.zeros((keys, LANES), F32)
        for p in range(pairs):
            cols = pl.ds(p * LANES, LANES)
            scores = dot_nt(split_heads(q_s[r, cols]), kv[m, 0, :, cols]) + key_bias
            top = jnp.max(scores, axis=1, keepdims=True)
            e = jnp.exp(scores - top)
            total = jnp.sum(e, axis=1, keepdims=True)
            stats = jnp.where(lane == p, top + jnp.log(total), stats)
            o = dot_nn(e.astype(BF), kv[m, 1, :, cols]) * (1.0 / total)
            o_s[r, cols] = jnp.where(left_lanes(), o[0:rows], o[rows:2 * rows]).astype(BF)
        lse[m] = stats.T[0:8]

        r1 = ab[sec, r].astype(F32) + dot_nn(o_s[r], wout[...]) + vec(obias_ref, 0)
        hat, scale, n1 = norm(r1, vec(gain_ref, 0), vec(shift_ref, 0))
        xh1[r] = hat.astype(BF)
        rs1[r] = jnp.broadcast_to(scale, (rows, LANES))
        n_s[...] = n1.astype(BF)
        acc[...] = n1 + vec(obias_ref, 1)
        for j in range(nff):
            cols = pl.ds(j * width, width)
            u = dot_nn(n_s[...], wup(j)) + bup_ref[0:1, cols].astype(F32)
            phi = 0.5 + 0.5 * lax.erf(u * INV_SQRT_2)
            f = (u * phi).astype(BF)
            f_t = f.T
            for owner in range(quarter):
                for part in range(nff):
                    at = (owner * nff + part) * unit
                    lt[part, pl.ds((j * quarter + owner) * unit, unit), r] = f_t[at:at + unit]
            rt[R_U + j, r] = (phi + u * (jnp.exp(-0.5 * u * u) * INV_SQRT_2PI)).astype(BF)
            acc[...] += dot_nn(f, wdown[cols, :])
        hat, scale, result = norm(acc[...], vec(gain_ref, 1), vec(shift_ref, 1))
        xh2[r] = hat.astype(BF)
        rs2[r] = jnp.broadcast_to(scale, (rows, LANES))
        yb[r] = result.astype(BF)

        @pl.when(sec == 0)
        def _():
            hop_copy(yb, m).start()

        for copy in out_copies(0, yb, sout_hbm, m):
            copy.start()
        lt[L_N, :, r] = n_s[...].T
        lt[L_O, :, r] = o_s[r].T

    def backward(m, serve):
        r = mrows(m)
        wait_slot(1 - sec, m)
        length = len_ref[2 * hi + m]
        row_scale = jnp.where((sec == 0) | (positions((rows, 1), 0) < length), 1.0, 0.0)
        dy = ab[1 - sec, r].astype(F32) * row_scale
        hat = xh2[r].astype(F32)
        add_bias_grad(9, dy * hat)
        add_bias_grad(11, dy)
        dr2 = norm_back(dy, hat, rs2[r, 0:1], vec(gain_ref, 1))
        dz = dr2.astype(BF)
        rt[R_Z, r] = dz
        add_bias_grad(3, dz.astype(F32))
        acc[...] = dr2
        serve(0, 3)
        for j in range(nff):
            cols = pl.ds(j * width, width)
            du = (dot_nt(rt[R_Z, r], wdown[cols, :]) * rt[R_U + j, r].astype(F32)).astype(BF)
            rt[R_U + j, r] = du
            bg[4 + j] += jnp.sum(du.astype(F32), axis=0, keepdims=True)
            acc[...] += dot_nt(du, wup(j))
        serve(3, 4)
        dn1 = acc[...]
        hat = xh1[r].astype(F32)
        add_bias_grad(8, dn1 * hat)
        add_bias_grad(10, dn1)
        grad1 = norm_back(dn1, hat, rs1[r, 0:1], vec(gain_ref, 0))
        dr1[...] = grad1
        da = grad1.astype(BF)
        rt[R_A, r] = da
        add_bias_grad(2, da.astype(F32))
        do_s[...] = dot_nt(da, wout[...]).astype(BF)
        serve(4, 5)
        key_bias = jnp.where(positions((keys, 1), 0) < length, 0.0, -1e30)

        def head_pair(group, index):
            p = group * half_pairs + index
            cols = pl.ds(p * LANES, LANES)
            kcols = pl.ds(index * LANES, LANES)
            vcols = pl.ds((half_pairs + index) * LANES, LANES)
            qq = split_heads(q_s[r, cols])
            dd = split_heads(do_s[:, cols])
            kp = kv[m, 0, :, cols]
            pt = jnp.exp(dot_nt(kp, qq) + key_bias - lse[m, p:p + 1])
            dv = dot_nn(pt.astype(BF), dd)
            dpt = dot_nt(kv[m, 1, :, cols], dd)
            sums = jnp.sum(pt * dpt, axis=0, keepdims=True)
            ds = (pt * (dpt - sums)).astype(BF)
            dk = dot_nn(ds, qq)
            dq_t = dot_tn(kp, ds)
            dq_pair = jnp.concatenate([dq_t[0:hd, 0:rows], dq_t[hd:2 * hd, rows:2 * rows]], axis=0)
            rt[R_P, r, cols] = (dq_pair.T * (hd ** -0.5)).astype(BF)
            dkv_own[group, :, kcols] = dk[0:rows]
            dkv_own[group, :, vcols] = dv[0:rows]
            dkv_send[group, :, kcols] = dk[rows:keys].astype(BF)
            dkv_send[group, :, vcols] = dv[rows:keys].astype(BF)

        for group in range(2):
            for index in range(half_pairs):
                head_pair(group, index)
            dkv_copy(m, group).start()
            if group == 0:
                serve(5, EARLY)
        dq = rt[R_P, r]
        add_bias_grad(0, dq.astype(F32))
        dr1[...] += dot_nt(dq, wqkv[:, 0:width])

    def input_grad(m):
        r = mrows(m)
        dx = dr1[...]
        part = width // 2
        for group in range(2):
            dkv_copy(m, group).wait_recv()
            both = (dkv_own[group] + dkv_recv[m, group].astype(F32)).astype(BF)
            for which in range(2):
                at = (1 + which) * width + group * part
                piece = both[:, which * part:(which + 1) * part]
                rt[R_P + 1 + which, r, group * part:(group + 1) * part] = piece
                dx = dx + dot_nt(piece, wqkv[:, at:at + part])
        local_out, remote_out = out_copies(0, yb, sout_hbm, m)
        local_out.wait()
        remote_out.wait_send()

        @pl.when(sec == 0)
        def _():
            hop_copy(yb, m).wait_send()

        yb[r] = dx.astype(BF)

        @pl.when(sec == 1)
        def _():
            hop_copy(yb, m).start()

        for copy in out_copies(1, yb, sgrad_hbm, m):
            copy.start()
        for group in range(2):
            dkv_copy(m, group).wait_send()
        add_bias_grad(1, rt[R_P + 2, r].astype(F32))


    if with_sums:
        block = count * unit

        def slot_of(k, half):
            blocks = ff // tall
            return jnp.where(k < DEDICATED, blocks + 2 * k, 2 * (k - DEDICATED)) + half

        def core_copy(k, half):
            return remote(
                core_src.at[k % 2, half], pool.at[slot_of(k, half)],
                core_ss.at[k, half], core_rs.at[k, half], core_dev,
            )

        def y_copy(k):
            return remote(
                pool.at[slot_of(k, 1 - hi)], y_buf.at[k % Y_SLOTS], y_ss.at[k], y_rs.at[k], y_dev
            )

        def turn_copy(k):
            i = k // 2
            return remote(turn_src.at[i], turn_buf.at[i], turn_ss.at[i], turn_rs.at[i], y_dev)

        def piece(k, half, target):
            return pool.at[slot_of(k, half), pl.ds(pl.multiple_of(target * unit, unit), unit)]

        def up_copy(job, k, half, target):
            i = target - 1
            return remote(
                piece(k, half, target), up.at[job, i], up_ss.at[job, i], up_rs.at[job, i],
                z_dev(jnp.minimum(z + 1, count - 1)),
            )

        def down_copy(job, k, half, target):
            return remote(
                piece(k, half, target), down.at[job, target], down_ss.at[job, target],
                down_rs.at[job, target], z_dev(jnp.maximum(z - 1, 0)),
            )

        def add_piece(k, half, target, landed):
            ref = piece(k, half, target)
            ref[...] = (ref[...].astype(F32) + landed[...].astype(F32)).astype(BF)

        def hop(number, job, k, half):
            @pl.when(z == number - 1)
            def _():
                for target in range(count - 1, number - 1, -1):
                    if number > 1:
                        up_copy(job, k, half, target).wait_recv()
                        add_piece(k, half, target, up.at[job, target - 1])
                    up_copy(job, k, half, target).start()

            @pl.when(z == count - number)
            def _():
                for target in range(0, count - number):
                    if number > 1:
                        down_copy(job, k, half, target).wait_recv()
                        add_piece(k, half, target, down.at[job, target])
                    down_copy(job, k, half, target).start()

        def arrive(job, k, half):
            out[k] = piece(k, half, z)[...].astype(F32)

            @pl.when(z > 0)
            def _():
                up_copy(job, k, half, z).wait_recv()
                out[k] += up[job, jnp.maximum(z - 1, 0)].astype(F32)

            @pl.when(z < count - 1)
            def _():
                down_copy(job, k, half, z).wait_recv()
                out[k] += down[job, jnp.minimum(z, count - 2)].astype(F32)

        def along_z_first(k):
            return (k == Z_FIRST[0]) | (k == Z_FIRST[1])

        def jobs_of(k):
            return ((k, hi), (CHUNKS + k // 2, 1 - hi))

        def product(k, half):
            left = jnp.where(k < 8, jnp.minimum(k, L_N), jnp.where(k == 8, L_O, L_X))
            right = jnp.where(k < 4, R_Z, jnp.where(k < 8, k, jnp.where(k == 8, R_A, k - 9)))
            base = pl.multiple_of(half * block, block)
            return dot_nn(lt[left, pl.ds(base, block), :], rt[right])

        def for_core(k):
            @pl.when(k >= 2)
            def _():
                for half in range(2):
                    core_copy(k - 2, half).wait_send()

            for half in range(2):
                core_src[k % 2, half] = product(k, half * 2 + 1 - lo).astype(BF)
                core_copy(k, half).start()

        def chip_sum(k):
            for half in range(2):
                core_copy(k, half).wait_recv()
                slot = slot_of(k, half)
                pool[slot] = (product(k, half * 2 + lo) + pool[slot].astype(F32)).astype(BF)

            @pl.when(along_z_first(k))
            def _():
                for job, half in jobs_of(k):
                    hop(1, job, k, half)

            @pl.when(jnp.logical_not(along_z_first(k)))
            def _():
                y_copy(k).start()

        def bias_core():
            return remote(b_src.at[0], b_core, bc_ss.at[0], bc_rs.at[0], core_dev)

        def bias_y():
            return remote(b_src.at[1], b_y, bc_ss.at[1], bc_rs.at[1], y_dev)

        def bias_z(by):
            return remote(
                b_src.at[2], b_z.at[by - 1], bz_ss.at[by - 1], bz_rs.at[by - 1],
                z_dev((z + by) % count),
            )

        def sum_step(t):
            @pl.when(t < CHUNKS)
            def _():
                for_core(t)

            @pl.when((t >= 1) & (t <= CHUNKS))
            def _():
                chip_sum(t - 1)

            def y_first_at(lag, action):
                k = t - lag

                @pl.when((k >= 0) & (k < CHUNKS) & jnp.logical_not(along_z_first(k)))
                def _():
                    action(k)

            def z_first_at(lag, action):
                k = t - lag

                @pl.when(along_z_first(k))
                def _():
                    action(k)

            def from_y(k):
                y_copy(k).wait_recv()
                slot = slot_of(k, hi)
                pool[slot] = (pool[slot].astype(F32) + y_buf[k % Y_SLOTS].astype(F32)).astype(BF)
                hop(1, k, k, hi)

            y_first_at(4, from_y)
            for number in range(2, count):
                y_first_at(3 + number, lambda k, number=number: hop(number, k, k, hi))

                def both_halves(k, number=number):
                    for job, half in jobs_of(k):
                        hop(number, job, k, half)

                z_first_at(1 + 2 * number, both_halves)

            def turn(k):
                stays, goes = jobs_of(k)
                arrive(goes[0], k, goes[1])
                turn_src[k // 2] = out[k].astype(BF)
                turn_copy(k).start()
                arrive(stays[0], k, stays[1])

            def turned(k):
                turn_copy(k).wait_recv()
                out[k] += turn_buf[k // 2].astype(F32)

            y_first_at(4 + count, lambda k: arrive(k, k, hi))
            z_first_at(1 + 2 * count, turn)
            z_first_at(3 + 2 * count, turned)

            @pl.when(t == 7)
            def _():
                b_src[0] = bg[...]
                bias_core().start()

            @pl.when(t == 9)
            def _():
                bias_core().wait_recv()
                b_src[1] = b_src[0] + b_core[...]
                bias_y().start()

            @pl.when(t == 11)
            def _():
                bias_y().wait_recv()
                b_src[2] = b_src[1] + b_y[...]
                for by in range(1, count):
                    bias_z(by).start()

    def one_step(step, carry):
        first = sec == 0

        def among(*steps):
            hit = step == steps[0]
            for value in steps[1:]:
                hit = hit | (step == value)
            return hit

        late_forward = ((step == 3) & first) | ((step == 4) & jnp.logical_not(first))
        early_backward = ((step == 4) & first) | ((step == 3) & jnp.logical_not(first))
        m = jnp.where(among(2, 6, 7) | late_forward, 1, 0)

        def serve(start, stop):
            if with_sums:
                @pl.when((step == 6) & first)
                def _():
                    def body(t, c):
                        sum_step(t)
                        return c

                    lax.fori_loop(start, stop, body, 0)

        @pl.when(among(0, 2))
        def _():
            project(step, m)

        @pl.when((step == 1) | late_forward)
        def _():
            forward(m)

        @pl.when((step == 6) | early_backward)
        def _():
            backward(m, serve)

        @pl.when(among(5, 7))
        def _():
            input_grad(m)

        return carry

    lax.fori_loop(0, 8, one_step, 0)

    if with_sums:
        def rest(t, carry):
            sum_step(t)
            return carry

        lax.fori_loop(jnp.where(sec == 0, EARLY, 0), STEPS, rest, 0)

        total = b_src[2]
        for by in range(1, count):
            bias_z(by).wait_recv()
            total = total + b_z[by - 1]
        bg_out[...] = total
        bias_core().wait_send()
        bias_y().wait_send()
        for by in range(1, count):
            bias_z(by).wait_send()

        def sent(job, k, half):
            for target in range(count):
                if target > 0:
                    @pl.when(target > z)
                    def _(target=target):
                        up_copy(job, k, half, target).wait_send()

                if target < count - 1:
                    @pl.when(target < z)
                    def _(target=target):
                        down_copy(job, k, half, target).wait_send()

        def drain(k, carry):
            @pl.when(k >= CHUNKS - 2)
            def _():
                for half in range(2):
                    core_copy(k, half).wait_send()

            sent(k, k, hi)

            @pl.when(along_z_first(k))
            def _():
                turn_copy(k).wait_send()
                sent(CHUNKS + k // 2, k, 1 - hi)

            @pl.when(jnp.logical_not(along_z_first(k)))
            def _():
                y_copy(k).wait_send()

            return carry

        lax.fori_loop(0, CHUNKS, drain, 0)

    for m in range(MICRO):
        seq_copy(in_hbm, m).wait_send()
        for part in range(2):
            kv_copy(m, part).wait_send()
        out_copies(0, yb, sout_hbm, m)[1].wait_recv()
        local_out, remote_out = out_copies(1, yb, sgrad_hbm, m)
        local_out.wait()
        remote_out.wait()

        @pl.when(sec == 1)
        def _():
            hop_copy(yb, m).wait_send()


def run_train(args, with_sums):
    (inputs, cotangent, lengths, w_qkv, attn_bias, w_out, out_bias, w_up, bias_up, w_down,
     norm_gain, norm_bias) = args
    tables, span, width = inputs.shape
    ff = w_up.shape[2]
    rows = 2 * span
    total = MICRO * rows
    keys = 2 * rows
    count = lax.axis_size("dp")
    unit = width // 16
    block = count * unit
    tall = width // 4
    jobs = CHUNKS + len(Z_FIRST)
    any_spec = pl.BlockSpec(memory_space=pl.ANY)
    vmem = pl.BlockSpec(memory_space=pltpu.VMEM)
    smem = pl.BlockSpec(memory_space=pltpu.SMEM)
    dma = pltpu.SemaphoreType.DMA
    shape = jax.ShapeDtypeStruct
    stacks = (
        ((L_COUNT, width, total), BF),
        ((R_COUNT, total, width), BF),
        ((12, 1, width), F32),
    )
    if with_sums:
        results = (((CHUNKS, unit, width), F32), ((12, 1, width), F32))
    else:
        results = stacks
    scratch = [
        pltpu.VMEM((2, total, width), BF),
        pltpu.VMEM((width, 3 * width), BF),
        pltpu.VMEM((width, width), BF),
        pltpu.VMEM((ff // tall + (2 * DEDICATED if with_sums else 0), tall, width), BF),
        pltpu.VMEM((ff, width), BF),
        pltpu.VMEM((total, width), BF),
        pltpu.VMEM((MICRO, 2, keys, width), BF),
        pltpu.VMEM((MICRO, 8, keys), F32),
        pltpu.VMEM((total, width), BF),
        pltpu.VMEM((rows, width), BF),
        pltpu.VMEM((total, width), BF),
        pltpu.VMEM((total, width), BF),
        pltpu.VMEM((total, LANES), F32),
        pltpu.VMEM((total, LANES), F32),
        pltpu.VMEM((rows, width), F32),
        pltpu.VMEM((rows, width), F32),
        pltpu.VMEM((rows, width), BF),
        pltpu.VMEM((2, rows, width), F32),
        pltpu.VMEM((2, rows, width), BF),
        pltpu.VMEM((MICRO, 2, rows, width), BF),
        pltpu.VMEM((total, width), BF),
        dma((3 + 4 * (ff // width),)), dma((MICRO,)), dma((MICRO,)), dma((MICRO,)), dma((MICRO,)), dma((MICRO,)),
        dma((MICRO, 2)), dma((MICRO, 2)), dma((MICRO, 2)), dma((MICRO, 2)),
        dma((2, MICRO)), dma((2, MICRO)), dma((2, MICRO)),
    ]
    if with_sums:
        scratch += [pltpu.VMEM(dims, kind) for dims, kind in stacks]
        scratch += [
            pltpu.VMEM((2, 2, block, width), BF),
            pltpu.VMEM((Y_SLOTS, block, width), BF),
            pltpu.VMEM((jobs, count - 1, unit, width), BF),
            pltpu.VMEM((jobs, count - 1, unit, width), BF),
            pltpu.VMEM((len(Z_FIRST), unit, width), BF),
            pltpu.VMEM((len(Z_FIRST), unit, width), BF),
            pltpu.VMEM((3, 12, 1, width), F32),
            pltpu.VMEM((12, 1, width), F32),
            pltpu.VMEM((12, 1, width), F32),
            pltpu.VMEM((count - 1, 12, 1, width), F32),
            dma((CHUNKS, 2)), dma((CHUNKS, 2)), dma((CHUNKS,)), dma((CHUNKS,)),
            dma((jobs, count - 1)), dma((jobs, count - 1)),
            dma((jobs, count - 1)), dma((jobs, count - 1)),
            dma((len(Z_FIRST),)), dma((len(Z_FIRST),)), dma((2,)), dma((2,)),
            dma((count - 1,)), dma((count - 1,)),
        ]
    return pl.pallas_call(
        functools.partial(train_kernel, with_sums),
        name="train",
        out_shape=(shape((tables, span, width), BF), shape((tables, span, width), BF))
        + tuple(shape(dims, kind) for dims, kind in results),
        in_specs=[smem] + [any_spec] * 6 + [vmem] * 5,
        out_specs=(any_spec, any_spec) + (vmem,) * len(results),
        scratch_shapes=scratch,
        compiler_params=pltpu.CompilerParams(
            collective_id=0, has_side_effects=True, vmem_limit_bytes=VMEM_LIMIT
        ),
    )(lengths, inputs, cotangent, w_qkv, w_out, w_up, w_down,
      attn_bias, out_bias, bias_up, norm_gain, norm_bias)


def grads_by_scatter(lt, rt, bg, ff):
    width = lt.shape[1]
    parts = ff // width

    def scatter(full):
        return lax.psum_scatter(
            full.astype(BF), ("seq", "dp"), scatter_dimension=0, tiled=True
        ).astype(F32)

    left_f = lt[:parts].reshape(parts, 4, 4, width // 16, -1).transpose(1, 2, 0, 3, 4)
    down = scatter(dot_nn(left_f.reshape(ff, -1), rt[R_Z]))
    up = scatter(jnp.concatenate([dot_nn(lt[L_N], rt[R_U + j]) for j in range(parts)], axis=1))
    wout = scatter(dot_nn(lt[L_O], rt[R_A]))
    qkv = scatter(jnp.concatenate([dot_nn(lt[L_X], rt[R_P + j]) for j in range(3)], axis=1))
    return qkv, wout, up, down, lax.psum(bg, ("seq", "dp"))


def finish_kernel(
    sout, sgrad, grads, sums,
    sout_ref, sgrad_ref, qkv_ref, abias_ref, wout_ref, obias_ref, up_ref, bup_ref, down_ref,
    gain_ref, shift_ref, sem,
):
    copy = pltpu.make_async_copy(sout, sout_ref.at[0], sem)
    copy.start()
    width = grads.shape[2]
    unit = grads.shape[1]
    size = abias_ref.shape[1]
    index = lax.axis_index("seq") * lax.axis_size("dp") + lax.axis_index("dp")
    for k in range(CHUNKS):
        if k < 4:
            down_ref[0, k * unit:(k + 1) * unit, :] = grads[k]
        elif k < 8:
            up_ref[0, :, (k - 4) * width:(k - 3) * width] = grads[k]
        elif k == 8:
            wout_ref[0] = grads[k]
        else:
            qkv_ref[0, :, (k - 9) * width:(k - 8) * width] = grads[k]
    sgrad_ref[0] = sgrad[...].astype(F32)
    whole = width // size
    low = index < whole
    pairs = [jnp.where(low, sums[row], sums[row + 1]) for row in (0, 2, 8, 10)]
    block = jnp.concatenate(pairs + pairs, axis=0)
    block = pltpu.roll(block, (width - (index % whole) * size) % width, axis=1)
    for row, ref in enumerate((abias_ref, obias_ref, gain_ref, shift_ref)):
        ref[...] = block[row:row + 1, 0:size]
    wide = 2 * size
    per = width // wide
    rows = sums[4]
    for row in range(1, 4):
        rows = jnp.where(index // per == row, sums[4 + row], rows)
    rows = pltpu.roll(
        jnp.concatenate([rows] * 8, axis=0), (width - (index % per) * wide) % width, axis=1
    )
    bup_ref[...] = rows[0:1, 0:wide]
    copy.wait()


def run_finish(sout, sgrad, grads, sums):
    unit, width = grads.shape[1:]
    size = width // 8
    vmem = pl.BlockSpec(memory_space=pltpu.VMEM)
    any_spec = pl.BlockSpec(memory_space=pl.ANY)
    shape = jax.ShapeDtypeStruct
    return pl.pallas_call(
        finish_kernel,
        name="finish",
        out_shape=(
            shape((1,) + sout.shape, BF),
            shape((1,) + sgrad.shape, F32),
            shape((1, unit, 3 * width), F32),
            shape((1, size), F32),
            shape((1, unit, width), F32),
            shape((1, size), F32),
            shape((1, unit, 4 * width), F32),
            shape((1, 2 * size), F32),
            shape((1, 4 * unit, width), F32),
            shape((1, size), F32),
            shape((1, size), F32),
        ),
        in_specs=[any_spec] + [vmem] * 3,
        out_specs=(any_spec,) + (vmem,) * 10,
        scratch_shapes=[pltpu.SemaphoreType.DMA],
        compiler_params=pltpu.CompilerParams(vmem_limit_bytes=32 * 2 ** 20),
    )(sout, sgrad, grads, sums)


def local(*args):
    if lax.axis_size("dp") == 4:
        sout, sgrad, out, sums = run_train(args, True)
        return run_finish(sout, sgrad, out, sums)
    sout, sgrad, lt, rt, bg = run_train(args, False)
    width = lt.shape[1]
    ff = args[7].shape[2]
    index = lax.axis_index("seq") * lax.axis_size("dp") + lax.axis_index("dp")
    count = lax.axis_size("seq") * lax.axis_size("dp")
    qkv, wout, up, down, sums = grads_by_scatter(lt, rt, bg, ff)
    sums = sums.reshape(-1)

    def piece(start, rows):
        part = sums[start * width:(start + rows) * width]
        size = rows * width // count
        return lax.dynamic_slice_in_dim(part, index * size, size, 0)[None]

    return (
        sout[None],
        sgrad.astype(F32)[None],
        qkv[None],
        piece(0, 2),
        wout[None],
        piece(2, 2),
        up[None],
        piece(4, 4),
        down[None],
        piece(8, 2),
        piece(10, 2),
    )


def solution(mesh):
    return jax.shard_map(
        local,
        mesh=mesh,
        in_specs=(
            P("dp", "seq", None),
            P("dp", "seq", None),
            P("dp"),
            P("section", None, None),
            P("section", None),
            P("section", None, None),
            P("section", None),
            P("section", None, None),
            P("section", None),
            P("section", None, None),
            P("section", None),
            P("section", None),
        ),
        out_specs=(
            P("section", "dp", "seq", None),
            P("section", "dp", "seq", None),
            P("section", ("seq", "dp"), None),
            P("section", ("seq", "dp")),
            P("section", ("seq", "dp"), None),
            P("section", ("seq", "dp")),
            P("section", ("seq", "dp"), None),
            P("section", ("seq", "dp")),
            P("section", ("seq", "dp"), None),
            P("section", ("seq", "dp")),
            P("section", ("seq", "dp")),
        ),
        check_vma=False,
    )
```

```python
import functools

import jax
import jax.numpy as jnp
from jax import lax
from jax.experimental import pallas as pl
from jax.experimental.pallas import tpu as pltpu
from jax.sharding import PartitionSpec as P

H = 12
MICRO = 2
EPS = 1e-12
MESH = pl.DeviceIdType.MESH
BF = jnp.bfloat16
F32 = jnp.float32
LANES = 128
INV_SQRT_2PI = 0.3989422804014327
INV_SQRT_2 = 0.7071067811865476
L_F, L_N, L_O, L_X, L_COUNT = 0, 4, 5, 6, 7
R_P, R_A, R_U, R_Z, R_COUNT = 0, 3, 4, 8, 9
CHUNKS = 12
Z_FIRST = (1, 5)
EARLY = 6
DEDICATED = 6
Y_SLOTS = 10
STEPS = 19
VMEM_LIMIT = 63 * 2 ** 20


def dot_nn(a, b):
    return lax.dot_general(a, b, (((1,), (0,)), ((), ())), preferred_element_type=F32)


def dot_nt(a, b):
    return lax.dot_general(a, b, (((1,), (1,)), ((), ())), preferred_element_type=F32)


def dot_tn(a, b):
    return lax.dot_general(a, b, (((0,), (0,)), ((), ())), preferred_element_type=F32)


def train_kernel(with_sums, *refs):
    refs = iter(refs)

    def take(number):
        return [next(refs) for _ in range(number)]

    (len_ref, in_hbm, cot_hbm, wqkv_hbm, wout_hbm, wup_hbm, wdown_hbm,
     abias_ref, obias_ref, bup_ref, gain_ref, shift_ref) = take(12)
    sout_hbm, sgrad_hbm = take(2)
    if with_sums:
        out_hbm, bg_out = take(2)
    else:
        lt, rt, bg = take(3)
    (ab, wqkv, wout, pool, wdown, q_s, kv, lse, o_s, n_s, xh1, xh2, rs1, rs2, dr1, acc, do_s,
     dkv_own, dkv_send, dkv_recv, yb) = take(21)
    (w_sem, loc_sem, ex_send, ex_recv, hop_send, hop_recv, kv_ss, kv_rs, dk_ss, dk_rs,
     out_loc, out_ss, out_rs) = take(13)
    if with_sums:
        (lt, rt, bg, out, core_src, y_buf, up, down, turn_src, turn_buf,
         b_src, b_core, b_y, b_z) = take(14)
        (core_ss, core_rs, y_ss, y_rs, up_ss, up_rs, down_ss, down_rs, turn_ss, turn_rs,
         bc_ss, bc_rs, bz_ss, bz_rs, part_sem) = take(15)

    width = wqkv.shape[0]
    ff = wdown.shape[0]
    span = in_hbm.shape[1]
    rows = 2 * span
    keys = 2 * rows
    hd = width // H
    pairs = H // 2
    half_pairs = H // 4
    nff = ff // width
    quarter = 4
    unit = width // 16
    sec = lax.axis_index("section")
    seq = lax.axis_index("seq")
    z = lax.axis_index("dp")
    count = lax.axis_size("dp")
    hi = seq // 2
    lo = seq % 2
    core_dev = (sec, hi * 2 + 1 - lo, z)
    y_dev = (sec, (1 - hi) * 2 + lo, z)
    x_dev = (1 - sec, seq, z)

    def z_dev(index):
        return (sec, seq, index)

    def remote(src, dst, send, recv, dev):
        return pltpu.make_async_remote_copy(
            src_ref=src, dst_ref=dst, send_sem=send, recv_sem=recv,
            device_id=dev, device_id_type=MESH,
        )

    weight_copies = [
        pltpu.make_async_copy(src.at[0], dst, w_sem.at[i])
        for i, (src, dst) in enumerate(((wqkv_hbm, wqkv), (wout_hbm, wout), (wdown_hbm, wdown)))
    ]
    tall = width // 4
    for j in range(nff):
        for part in range(4):
            weight_copies.append(
                pltpu.make_async_copy(
                    wup_hbm.at[0, pl.ds(part * tall, tall), pl.ds(j * width, width)],
                    pool.at[j * 4 + part],
                    w_sem.at[3 + j * 4 + part],
                )
            )
    for copy in weight_copies:
        copy.start()

    partners = [core_dev, y_dev, x_dev]
    if with_sums:
        partners += [z_dev((z + by) % count) for by in range(1, count)]
    barrier = pltpu.get_barrier_semaphore()
    for dev in partners:
        pl.semaphore_signal(barrier, inc=1, device_id=dev, device_id_type=MESH)
    pl.semaphore_wait(barrier, len(partners))

    def mrows(m):
        return pl.ds(pl.multiple_of(m * rows, rows), rows)

    def own_copy(src, m):
        return pltpu.make_async_copy(
            src.at[2 * hi + m], ab.at[0, pl.ds(m * rows, span)], loc_sem.at[m]
        )

    def seq_copy(src, m):
        return remote(
            src.at[2 * (1 - hi) + m], ab.at[0, pl.ds(m * rows + span, span)],
            ex_send.at[m], ex_recv.at[m], y_dev,
        )

    for is_sec, src in ((0, in_hbm), (1, cot_hbm)):
        @pl.when(sec == is_sec)
        def _(src=src):
            for m in range(MICRO):
                seq_copy(src, m).start()
                own_copy(src, m).start()

    bg[...] = jnp.zeros_like(bg)

    def hop_copy(src, m):
        return remote(src.at[mrows(m)], ab.at[1, mrows(m)], hop_send.at[m], hop_recv.at[m], x_dev)

    def kv_copy(m, part):
        return remote(
            kv.at[m, part, pl.ds(0, rows)], kv.at[m, part, pl.ds(rows, rows)],
            kv_ss.at[m, part], kv_rs.at[m, part], core_dev,
        )

    def dkv_copy(m, group):
        return remote(
            dkv_send.at[group], dkv_recv.at[m, group],
            dk_ss.at[m, group], dk_rs.at[m, group], core_dev,
        )

    def out_copies(kind, src, dst, m):
        table = 2 * hi + m
        base = m * rows
        return (
            pltpu.make_async_copy(src.at[pl.ds(base, span)], dst.at[table], out_loc.at[kind, m]),
            remote(
                src.at[pl.ds(base + span, span)], dst.at[table],
                out_ss.at[kind, m], out_rs.at[kind, m], y_dev,
            ),
        )

    def wait_slot(which, m):
        @pl.when(which == 0)
        def _():
            own_copy(in_hbm, m).wait()
            seq_copy(in_hbm, m).wait_recv()

        @pl.when(which == 1)
        def _():
            hop_copy(yb, m).wait_recv()

    def positions(shape, dim):
        row = lax.broadcasted_iota(jnp.int32, shape, dim)
        block = row // span
        within = row % span
        half = jnp.where(block % 2 == 0, hi, 1 - hi)
        core = jnp.where(block < 2, lo, 1 - lo)
        return (half * 2 + core) * span + within

    def left_lanes():
        return lax.broadcasted_iota(jnp.int32, (1, LANES), 1) < hd

    def split_heads(value):
        left = left_lanes().astype(F32)
        return jnp.concatenate([value * left.astype(BF), value * (1.0 - left).astype(BF)], axis=0)

    def norm(resid, gain, shift):
        average = jnp.mean(resid, axis=-1, keepdims=True)
        centred = resid - average
        spread = jnp.mean(centred * centred, axis=-1, keepdims=True)
        scale = lax.rsqrt(spread + EPS)
        hat = centred * scale
        return hat, scale, hat * gain + shift

    def norm_back(grad, hat, scale, gain):
        dh = grad * gain
        return scale * (
            dh
            - jnp.mean(dh, axis=-1, keepdims=True)
            - hat * jnp.mean(dh * hat, axis=-1, keepdims=True)
        )

    def wup(j):
        return pool[4 * j:4 * j + 4].reshape(width, width)

    def vec(ref, part):
        return ref[0:1, part * width:(part + 1) * width].astype(F32)

    def add_bias_grad(row, value):
        bg[row] += jnp.sum(value, axis=0, keepdims=True)


    def project(step, m):
        r = mrows(m)
        wait_slot(sec, m)

        @pl.when(step == 0)
        def _():
            weight_copies[0].wait()

        x = ab[sec, r]
        kv[m, 0, pl.ds(0, rows)] = dot_nn(x, wqkv[:, width:2 * width]).astype(BF)
        kv_copy(m, 0).start()
        kv[m, 1, pl.ds(0, rows)] = (
            dot_nn(x, wqkv[:, 2 * width:3 * width]) + vec(abias_ref, 1)
        ).astype(BF)
        kv_copy(m, 1).start()
        queries = (dot_nn(x, wqkv[:, 0:width]) + vec(abias_ref, 0)).astype(BF)
        q_s[r] = queries * (hd ** -0.5)
        lt[L_X, :, r] = x.T

        @pl.when(step == 0)
        def _():
            for copy in weight_copies[1:]:
                copy.wait()

    def forward(m):
        r = mrows(m)
        kv_copy(m, 0).wait_recv()
        kv_copy(m, 1).wait_recv()
        key_bias = jnp.where(positions((1, keys), 1) < len_ref[2 * hi + m], 0.0, -1e30)
        lane = lax.broadcasted_iota(jnp.int32, (1, LANES), 1)
        stats = jnp.zeros((keys, LANES), F32)
        for p in range(pairs):
            cols = pl.ds(p * LANES, LANES)
            scores = dot_nt(split_heads(q_s[r, cols]), kv[m, 0, :, cols]) + key_bias
            top = jnp.max(scores, axis=1, keepdims=True)
            e = jnp.exp(scores - top)
            total = jnp.sum(e, axis=1, keepdims=True)
            stats = jnp.where(lane == p, top + jnp.log(total), stats)
            o = dot_nn(e.astype(BF), kv[m, 1, :, cols]) * (1.0 / total)
            o_s[r, cols] = jnp.where(left_lanes(), o[0:rows], o[rows:2 * rows]).astype(BF)
        lse[m] = stats.T[0:8]

        r1 = ab[sec, r].astype(F32) + dot_nn(o_s[r], wout[...]) + vec(obias_ref, 0)
        hat, scale, n1 = norm(r1, vec(gain_ref, 0), vec(shift_ref, 0))
        xh1[r] = hat.astype(BF)
        rs1[r] = jnp.broadcast_to(scale, (rows, LANES))
        n_s[...] = n1.astype(BF)
        acc[...] = n1 + vec(obias_ref, 1)
        for j in range(nff):
            cols = pl.ds(j * width, width)
            u = dot_nn(n_s[...], wup(j)) + bup_ref[0:1, cols].astype(F32)
            phi = 0.5 + 0.5 * lax.erf(u * INV_SQRT_2)
            f = (u * phi).astype(BF)
            f_t = f.T
            for owner in range(quarter):
                for part in range(nff):
                    at = (owner * nff + part) * unit
                    lt[part, pl.ds((j * quarter + owner) * unit, unit), r] = f_t[at:at + unit]
            rt[R_U + j, r] = (phi + u * (jnp.exp(-0.5 * u * u) * INV_SQRT_2PI)).astype(BF)
            acc[...] += dot_nn(f, wdown[cols, :])
        hat, scale, result = norm(acc[...], vec(gain_ref, 1), vec(shift_ref, 1))
        xh2[r] = hat.astype(BF)
        rs2[r] = jnp.broadcast_to(scale, (rows, LANES))
        yb[r] = result.astype(BF)

        @pl.when(sec == 0)
        def _():
            hop_copy(yb, m).start()

        for copy in out_copies(0, yb, sout_hbm, m):
            copy.start()
        lt[L_N, :, r] = n_s[...].T
        lt[L_O, :, r] = o_s[r].T

    def backward(m, serve):
        r = mrows(m)
        wait_slot(1 - sec, m)
        length = len_ref[2 * hi + m]
        row_scale = jnp.where((sec == 0) | (positions((rows, 1), 0) < length), 1.0, 0.0)
        dy = ab[1 - sec, r].astype(F32) * row_scale
        hat = xh2[r].astype(F32)
        add_bias_grad(9, dy * hat)
        add_bias_grad(11, dy)
        dr2 = norm_back(dy, hat, rs2[r, 0:1], vec(gain_ref, 1))
        dz = dr2.astype(BF)
        rt[R_Z, r] = dz
        add_bias_grad(3, dz.astype(F32))
        acc[...] = dr2
        serve(0, 3)
        for j in range(nff):
            cols = pl.ds(j * width, width)
            du = (dot_nt(rt[R_Z, r], wdown[cols, :]) * rt[R_U + j, r].astype(F32)).astype(BF)
            rt[R_U + j, r] = du
            bg[4 + j] += jnp.sum(du.astype(F32), axis=0, keepdims=True)
            acc[...] += dot_nt(du, wup(j))
        serve(3, 4)
        dn1 = acc[...]
        hat = xh1[r].astype(F32)
        add_bias_grad(8, dn1 * hat)
        add_bias_grad(10, dn1)
        grad1 = norm_back(dn1, hat, rs1[r, 0:1], vec(gain_ref, 0))
        dr1[...] = grad1
        da = grad1.astype(BF)
        rt[R_A, r] = da
        add_bias_grad(2, da.astype(F32))
        do_s[...] = dot_nt(da, wout[...]).astype(BF)
        serve(4, 5)
        key_bias = jnp.where(positions((keys, 1), 0) < length, 0.0, -1e30)

        def head_pair(group, index):
            p = group * half_pairs + index
            cols = pl.ds(p * LANES, LANES)
            kcols = pl.ds(index * LANES, LANES)
            vcols = pl.ds((half_pairs + index) * LANES, LANES)
            qq = split_heads(q_s[r, cols])
            dd = split_heads(do_s[:, cols])
            kp = kv[m, 0, :, cols]
            pt = jnp.exp(dot_nt(kp, qq) + key_bias - lse[m, p:p + 1])
            dv = dot_nn(pt.astype(BF), dd)
            dpt = dot_nt(kv[m, 1, :, cols], dd)
            sums = jnp.sum(pt * dpt, axis=0, keepdims=True)
            ds = (pt * (dpt - sums)).astype(BF)
            dk = dot_nn(ds, qq)
            dq_t = dot_tn(kp, ds)
            dq_pair = jnp.concatenate([dq_t[0:hd, 0:rows], dq_t[hd:2 * hd, rows:2 * rows]], axis=0)
            rt[R_P, r, cols] = (dq_pair.T * (hd ** -0.5)).astype(BF)
            dkv_own[group, :, kcols] = dk[0:rows]
            dkv_own[group, :, vcols] = dv[0:rows]
            dkv_send[group, :, kcols] = dk[rows:keys].astype(BF)
            dkv_send[group, :, vcols] = dv[rows:keys].astype(BF)

        for group in range(2):
            for index in range(half_pairs):
                head_pair(group, index)
            dkv_copy(m, group).start()
            if group == 0:
                serve(5, EARLY)
        dq = rt[R_P, r]
        add_bias_grad(0, dq.astype(F32))
        dr1[...] += dot_nt(dq, wqkv[:, 0:width])

    def input_grad(m):
        r = mrows(m)
        dx = dr1[...]
        part = width // 2
        for group in range(2):
            dkv_copy(m, group).wait_recv()
            both = (dkv_own[group] + dkv_recv[m, group].astype(F32)).astype(BF)
            for which in range(2):
                at = (1 + which) * width + group * part
                piece = both[:, which * part:(which + 1) * part]
                rt[R_P + 1 + which, r, group * part:(group + 1) * part] = piece
                dx = dx + dot_nt(piece, wqkv[:, at:at + part])
        local_out, remote_out = out_copies(0, yb, sout_hbm, m)
        local_out.wait()
        remote_out.wait_send()

        @pl.when(sec == 0)
        def _():
            hop_copy(yb, m).wait_send()

        yb[r] = dx.astype(BF)

        @pl.when(sec == 1)
        def _():
            hop_copy(yb, m).start()

        @pl.when(m == 0)
        def _():
            send_input_grad(m)

        for group in range(2):
            dkv_copy(m, group).wait_send()
        add_bias_grad(1, rt[R_P + 2, r].astype(F32))

    def send_input_grad(m):
        for copy in out_copies(1, yb, sgrad_hbm, m):
            copy.start()


    if with_sums:
        block = count * unit

        def slot_of(k, half):
            blocks = ff // tall
            return jnp.where(k < DEDICATED, blocks + 2 * k, 2 * (k - DEDICATED)) + half

        def core_copy(k, half):
            return remote(
                core_src.at[k % 2, half], pool.at[slot_of(k, half)],
                core_ss.at[k, half], core_rs.at[k, half], core_dev,
            )

        def y_copy(k, i):
            target = jnp.where(z < count // 2, count - 1 - i, i)
            rows_of = pl.ds(pl.multiple_of(target * unit, unit), unit)
            return target, remote(
                pool.at[slot_of(k, 1 - hi), rows_of], y_buf.at[k % Y_SLOTS, i],
                y_ss.at[k, i], y_rs.at[k, i], y_dev,
            )

        def turn_index(k):
            index = 0
            for i in range(1, len(Z_FIRST)):
                index = jnp.where(k == Z_FIRST[i], i, index)
            return index

        def turn_copy(k):
            i = turn_index(k)
            return remote(turn_src.at[i], turn_buf.at[i], turn_ss.at[i], turn_rs.at[i], y_dev)

        def piece(k, half, target):
            return pool.at[slot_of(k, half), pl.ds(pl.multiple_of(target * unit, unit), unit)]

        def up_copy(job, k, half, target):
            i = target - 1
            return remote(
                piece(k, half, target), up.at[job, i], up_ss.at[job, i], up_rs.at[job, i],
                z_dev(jnp.minimum(z + 1, count - 1)),
            )

        def down_copy(job, k, half, target):
            return remote(
                piece(k, half, target), down.at[job, target], down_ss.at[job, target],
                down_rs.at[job, target], z_dev(jnp.maximum(z - 1, 0)),
            )

        def add_piece(k, half, target, landed):
            ref = piece(k, half, target)
            ref[...] = (ref[...].astype(F32) + landed[...].astype(F32)).astype(BF)

        def hop(number, job, k, half):
            @pl.when(z == number - 1)
            def _():
                for target in range(count - 1, number - 1, -1):
                    if number > 1:
                        up_copy(job, k, half, target).wait_recv()
                        add_piece(k, half, target, up.at[job, target - 1])
                    up_copy(job, k, half, target).start()

            @pl.when(z == count - number)
            def _():
                for target in range(0, count - number):
                    if number > 1:
                        down_copy(job, k, half, target).wait_recv()
                        add_piece(k, half, target, down.at[job, target])
                    down_copy(job, k, half, target).start()

        def arrive(job, k, half):
            out[k] = piece(k, half, z)[...].astype(F32)

            @pl.when(z > 0)
            def _():
                up_copy(job, k, half, z).wait_recv()
                out[k] += up[job, jnp.maximum(z - 1, 0)].astype(F32)

            @pl.when(z < count - 1)
            def _():
                down_copy(job, k, half, z).wait_recv()
                out[k] += down[job, jnp.minimum(z, count - 2)].astype(F32)

        def along_z_first(k):
            hit = k == Z_FIRST[0]
            for other in Z_FIRST[1:]:
                hit = hit | (k == other)
            return hit

        def jobs_of(k):
            return ((k, hi), (CHUNKS + turn_index(k), 1 - hi))

        def product(k, half):
            left = jnp.where(k < 8, jnp.minimum(k, L_N), jnp.where(k == 8, L_O, L_X))
            right = jnp.where(k < 4, R_Z, jnp.where(k < 8, k, jnp.where(k == 8, R_A, k - 9)))
            base = pl.multiple_of(half * block, block)
            return dot_nn(lt[left, pl.ds(base, block), :], rt[right])

        def for_core(k):
            @pl.when(k >= 2)
            def _():
                for half in range(2):
                    core_copy(k - 2, half).wait_send()

            for half in range(2):
                core_src[k % 2, half] = product(k, half * 2 + 1 - lo).astype(BF)
                core_copy(k, half).start()

        def chip_sum(k):
            for half in range(2):
                core_copy(k, half).wait_recv()
                slot = slot_of(k, half)
                pool[slot] = (product(k, half * 2 + lo) + pool[slot].astype(F32)).astype(BF)

            @pl.when(along_z_first(k))
            def _():
                for job, half in jobs_of(k):
                    hop(1, job, k, half)

            @pl.when(jnp.logical_not(along_z_first(k)))
            def _():
                for i in range(count):
                    y_copy(k, i)[1].start()

        def part_copy(k):
            return pltpu.make_async_copy(out.at[k], out_hbm.at[k], part_sem.at[k])

        def bias_core():
            return remote(b_src.at[0], b_core, bc_ss.at[0], bc_rs.at[0], core_dev)

        def bias_y():
            return remote(b_src.at[1], b_y, bc_ss.at[1], bc_rs.at[1], y_dev)

        def bias_z(by):
            return remote(
                b_src.at[2], b_z.at[by - 1], bz_ss.at[by - 1], bz_rs.at[by - 1],
                z_dev((z + by) % count),
            )

        def sum_step(t):
            @pl.when(t < CHUNKS)
            def _():
                for_core(t)

            @pl.when((t >= 1) & (t <= CHUNKS))
            def _():
                chip_sum(t - 1)

            def y_first_at(lag, action):
                k = t - lag

                @pl.when((k >= 0) & (k < CHUNKS) & jnp.logical_not(along_z_first(k)))
                def _():
                    action(k)

            def z_first_at(lag, action):
                k = t - lag

                @pl.when(along_z_first(k))
                def _():
                    action(k)

            def from_y(k):
                for i in range(count):
                    target, copy = y_copy(k, i)
                    copy.wait_recv()
                    add_piece(k, hi, target, y_buf.at[k % Y_SLOTS, i])
                    if i < count - 1:
                        @pl.when(z == 0)
                        def _(target=count - 1 - i):
                            up_copy(k, k, hi, target).start()

                        @pl.when(z == count - 1)
                        def _(target=i):
                            down_copy(k, k, hi, target).start()

            y_first_at(4, from_y)
            for number in range(2, count):
                y_first_at(4 + number, lambda k, number=number: hop(number, k, k, hi))

                def both_halves(k, number=number):
                    for job, half in jobs_of(k):
                        hop(number, job, k, half)

                z_first_at(2 + 2 * number, both_halves)

            def turn(k):
                stays, goes = jobs_of(k)
                arrive(goes[0], k, goes[1])
                turn_src[turn_index(k)] = out[k].astype(BF)
                turn_copy(k).start()
                arrive(stays[0], k, stays[1])

            @pl.when(t == CHUNKS + 1)
            def _():
                send_input_grad(MICRO - 1)

            for i, k in enumerate(Z_FIRST):
                @pl.when(t == CHUNKS + 4 + i)
                def _(k=k):
                    turn(k)

            @pl.when(t == 7)
            def _():
                b_src[0] = bg[...]
                bias_core().start()

            @pl.when(t == 9)
            def _():
                bias_core().wait_recv()
                b_src[1] = b_src[0] + b_core[...]
                bias_y().start()

            @pl.when(t == 11)
            def _():
                bias_y().wait_recv()
                b_src[2] = b_src[1] + b_y[...]
                for by in range(1, count):
                    bias_z(by).start()

    def one_step(step, carry):
        first = sec == 0

        def among(*steps):
            hit = step == steps[0]
            for value in steps[1:]:
                hit = hit | (step == value)
            return hit

        late_forward = ((step == 3) & first) | ((step == 4) & jnp.logical_not(first))
        early_backward = ((step == 4) & first) | ((step == 3) & jnp.logical_not(first))
        m = jnp.where(among(2, 6, 7) | late_forward, 1, 0)

        def serve(start, stop):
            if with_sums:
                @pl.when((step == 6) & first)
                def _():
                    def body(t, c):
                        sum_step(t)
                        return c

                    lax.fori_loop(start, stop, body, 0)

        @pl.when(among(0, 2))
        def _():
            project(step, m)

        @pl.when((step == 1) | late_forward)
        def _():
            forward(m)

        @pl.when((step == 6) | early_backward)
        def _():
            backward(m, serve)

        @pl.when(among(5, 7))
        def _():
            input_grad(m)

        return carry

    lax.fori_loop(0, 8, one_step, 0)

    if not with_sums:
        send_input_grad(MICRO - 1)

    if with_sums:
        def rest(t, carry):
            sum_step(t)
            return carry

        lax.fori_loop(jnp.where(sec == 0, EARLY, 0), STEPS, rest, 0)

        def last_sum(k, carry):
            @pl.when(jnp.logical_not(along_z_first(k)))
            def _():
                arrive(k, k, hi)
                part_copy(k).start()

            return carry

        lax.fori_loop(0, CHUNKS, last_sum, 0)
        for k in Z_FIRST:
            turn_copy(k).wait_recv()
            out[k] += turn_buf[turn_index(k)].astype(F32)
            part_copy(k).start()

        total = b_src[2]
        for by in range(1, count):
            bias_z(by).wait_recv()
            total = total + b_z[by - 1]
        bg_out[...] = total
        bias_core().wait_send()
        bias_y().wait_send()
        for by in range(1, count):
            bias_z(by).wait_send()

        def sent(job, k, half):
            for target in range(count):
                if target > 0:
                    @pl.when(target > z)
                    def _(target=target):
                        up_copy(job, k, half, target).wait_send()

                if target < count - 1:
                    @pl.when(target < z)
                    def _(target=target):
                        down_copy(job, k, half, target).wait_send()

        def drain(k, carry):
            part_copy(k).wait()
            @pl.when(k >= CHUNKS - 2)
            def _():
                for half in range(2):
                    core_copy(k, half).wait_send()

            sent(k, k, hi)

            @pl.when(along_z_first(k))
            def _():
                turn_copy(k).wait_send()
                sent(CHUNKS + turn_index(k), k, 1 - hi)

            @pl.when(jnp.logical_not(along_z_first(k)))
            def _():
                for i in range(count):
                    y_copy(k, i)[1].wait_send()

            return carry

        lax.fori_loop(0, CHUNKS, drain, 0)

    for m in range(MICRO):
        seq_copy(in_hbm, m).wait_send()
        for part in range(2):
            kv_copy(m, part).wait_send()
        out_copies(0, yb, sout_hbm, m)[1].wait_recv()
        local_out, remote_out = out_copies(1, yb, sgrad_hbm, m)
        local_out.wait()
        remote_out.wait()

        @pl.when(sec == 1)
        def _():
            hop_copy(yb, m).wait_send()


def run_train(args, with_sums):
    (inputs, cotangent, lengths, w_qkv, attn_bias, w_out, out_bias, w_up, bias_up, w_down,
     norm_gain, norm_bias) = args
    tables, span, width = inputs.shape
    ff = w_up.shape[2]
    rows = 2 * span
    total = MICRO * rows
    keys = 2 * rows
    count = lax.axis_size("dp")
    unit = width // 16
    block = count * unit
    tall = width // 4
    jobs = CHUNKS + len(Z_FIRST)
    any_spec = pl.BlockSpec(memory_space=pl.ANY)
    vmem = pl.BlockSpec(memory_space=pltpu.VMEM)
    smem = pl.BlockSpec(memory_space=pltpu.SMEM)
    dma = pltpu.SemaphoreType.DMA
    shape = jax.ShapeDtypeStruct
    stacks = (
        ((L_COUNT, width, total), BF),
        ((R_COUNT, total, width), BF),
        ((12, 1, width), F32),
    )
    if with_sums:
        results = (((CHUNKS, unit, width), F32), ((12, 1, width), F32))
    else:
        results = stacks
    scratch = [
        pltpu.VMEM((2, total, width), BF),
        pltpu.VMEM((width, 3 * width), BF),
        pltpu.VMEM((width, width), BF),
        pltpu.VMEM((ff // tall + (2 * DEDICATED if with_sums else 0), tall, width), BF),
        pltpu.VMEM((ff, width), BF),
        pltpu.VMEM((total, width), BF),
        pltpu.VMEM((MICRO, 2, keys, width), BF),
        pltpu.VMEM((MICRO, 8, keys), F32),
        pltpu.VMEM((total, width), BF),
        pltpu.VMEM((rows, width), BF),
        pltpu.VMEM((total, width), BF),
        pltpu.VMEM((total, width), BF),
        pltpu.VMEM((total, LANES), F32),
        pltpu.VMEM((total, LANES), F32),
        pltpu.VMEM((rows, width), F32),
        pltpu.VMEM((rows, width), F32),
        pltpu.VMEM((rows, width), BF),
        pltpu.VMEM((2, rows, width), F32),
        pltpu.VMEM((2, rows, width), BF),
        pltpu.VMEM((MICRO, 2, rows, width), BF),
        pltpu.VMEM((total, width), BF),
        dma((3 + 4 * (ff // width),)), dma((MICRO,)), dma((MICRO,)), dma((MICRO,)), dma((MICRO,)), dma((MICRO,)),
        dma((MICRO, 2)), dma((MICRO, 2)), dma((MICRO, 2)), dma((MICRO, 2)),
        dma((2, MICRO)), dma((2, MICRO)), dma((2, MICRO)),
    ]
    if with_sums:
        scratch += [pltpu.VMEM(dims, kind) for dims, kind in stacks]
        scratch += [
            pltpu.VMEM((CHUNKS, unit, width), F32),
            pltpu.VMEM((2, 2, block, width), BF),
            pltpu.VMEM((Y_SLOTS, count, unit, width), BF),
            pltpu.VMEM((jobs, count - 1, unit, width), BF),
            pltpu.VMEM((jobs, count - 1, unit, width), BF),
            pltpu.VMEM((len(Z_FIRST), unit, width), BF),
            pltpu.VMEM((len(Z_FIRST), unit, width), BF),
            pltpu.VMEM((3, 12, 1, width), F32),
            pltpu.VMEM((12, 1, width), F32),
            pltpu.VMEM((12, 1, width), F32),
            pltpu.VMEM((count - 1, 12, 1, width), F32),
            dma((CHUNKS, 2)), dma((CHUNKS, 2)), dma((CHUNKS, count)), dma((CHUNKS, count)),
            dma((jobs, count - 1)), dma((jobs, count - 1)),
            dma((jobs, count - 1)), dma((jobs, count - 1)),
            dma((len(Z_FIRST),)), dma((len(Z_FIRST),)), dma((2,)), dma((2,)),
            dma((count - 1,)), dma((count - 1,)), dma((CHUNKS,)),
        ]
    return pl.pallas_call(
        functools.partial(train_kernel, with_sums),
        name="train",
        out_shape=(shape((tables, span, width), BF), shape((tables, span, width), BF))
        + tuple(shape(dims, kind) for dims, kind in results),
        in_specs=[smem] + [any_spec] * 6 + [vmem] * 5,
        out_specs=(any_spec, any_spec)
        + ((any_spec, vmem) if with_sums else (vmem,) * len(results)),
        scratch_shapes=scratch,
        compiler_params=pltpu.CompilerParams(
            collective_id=0, has_side_effects=True, vmem_limit_bytes=VMEM_LIMIT
        ),
    )(lengths, inputs, cotangent, w_qkv, w_out, w_up, w_down,
      attn_bias, out_bias, bias_up, norm_gain, norm_bias)


def grads_by_scatter(lt, rt, bg, ff):
    width = lt.shape[1]
    parts = ff // width

    def scatter(full):
        return lax.psum_scatter(
            full.astype(BF), ("seq", "dp"), scatter_dimension=0, tiled=True
        ).astype(F32)

    left_f = lt[:parts].reshape(parts, 4, 4, width // 16, -1).transpose(1, 2, 0, 3, 4)
    down = scatter(dot_nn(left_f.reshape(ff, -1), rt[R_Z]))
    up = scatter(jnp.concatenate([dot_nn(lt[L_N], rt[R_U + j]) for j in range(parts)], axis=1))
    wout = scatter(dot_nn(lt[L_O], rt[R_A]))
    qkv = scatter(jnp.concatenate([dot_nn(lt[L_X], rt[R_P + j]) for j in range(3)], axis=1))
    return qkv, wout, up, down, lax.psum(bg, ("seq", "dp"))


def finish_kernel(
    sout, sgrad, grads, sums_hbm,
    sout_ref, sgrad_ref, qkv_ref, abias_ref, wout_ref, obias_ref, up_ref, bup_ref, down_ref,
    gain_ref, shift_ref,
    kept, low, wide_grad, parts, sums, sem,
):
    unit, width = grads.shape[1:]
    size = abias_ref.shape[1]

    def copy(i, src, dst):
        started = pltpu.make_async_copy(src, dst, sem.at[i])
        started.start()
        return started

    sums_in = copy(0, sums_hbm, sums)
    grad_in = copy(1, sgrad, low)
    out_in = copy(2, sout, kept)
    parts_in = copy(3, grads, parts)
    grad_in.wait()
    wide_grad[...] = low[...].astype(F32)
    copies = [copy(4, wide_grad, sgrad_ref.at[0])]
    out_in.wait()
    copies.append(copy(5, kept, sout_ref.at[0]))
    parts_in.wait()
    for k in range(CHUNKS):
        if k < 4:
            dst = down_ref.at[0, pl.ds(k * unit, unit), :]
        elif k < 8:
            dst = up_ref.at[0, :, pl.ds((k - 4) * width, width)]
        elif k == 8:
            dst = wout_ref.at[0]
        else:
            dst = qkv_ref.at[0, :, pl.ds((k - 9) * width, width)]
        copies.append(copy(6 + k, parts.at[k], dst))
    sums_in.wait()
    index = lax.axis_index("seq") * lax.axis_size("dp") + lax.axis_index("dp")
    whole = width // size
    pairs = [jnp.where(index < whole, sums[row], sums[row + 1]) for row in (0, 2, 8, 10)]
    block = jnp.concatenate(pairs + pairs, axis=0)
    block = pltpu.roll(block, (width - (index % whole) * size) % width, axis=1)
    for row, ref in enumerate((abias_ref, obias_ref, gain_ref, shift_ref)):
        ref[...] = block[row:row + 1, 0:size]
    wide = 2 * size
    per = width // wide
    rows = sums[4]
    for row in range(1, 4):
        rows = jnp.where(index // per == row, sums[4 + row], rows)
    rows = pltpu.roll(
        jnp.concatenate([rows] * 8, axis=0), (width - (index % per) * wide) % width, axis=1
    )
    bup_ref[...] = rows[0:1, 0:wide]
    for started in copies:
        started.wait()


def run_finish(sout, sgrad, grads, sums):
    unit, width = grads.shape[1:]
    size = width // 8
    vmem = pl.BlockSpec(memory_space=pltpu.VMEM)
    any_spec = pl.BlockSpec(memory_space=pl.ANY)
    shape = jax.ShapeDtypeStruct
    return pl.pallas_call(
        finish_kernel,
        name="finish",
        out_shape=(
            shape((1,) + sout.shape, BF),
            shape((1,) + sgrad.shape, F32),
            shape((1, unit, 3 * width), F32),
            shape((1, size), F32),
            shape((1, unit, width), F32),
            shape((1, size), F32),
            shape((1, unit, 4 * width), F32),
            shape((1, 2 * size), F32),
            shape((1, 4 * unit, width), F32),
            shape((1, size), F32),
            shape((1, size), F32),
        ),
        in_specs=[any_spec] * 4,
        out_specs=(any_spec, any_spec, any_spec, vmem, any_spec, vmem, any_spec, vmem, any_spec,
                   vmem, vmem),
        scratch_shapes=[
            pltpu.VMEM(sout.shape, BF),
            pltpu.VMEM(sgrad.shape, BF),
            pltpu.VMEM(sgrad.shape, F32),
            pltpu.VMEM(grads.shape, F32),
            pltpu.VMEM(sums.shape, F32),
            pltpu.SemaphoreType.DMA((6 + CHUNKS,)),
        ],
        compiler_params=pltpu.CompilerParams(vmem_limit_bytes=VMEM_LIMIT),
    )(sout, sgrad, grads, sums)


def local(*args):
    if lax.axis_size("dp") == 4:
        sout, sgrad, out, sums = run_train(args, True)
        return run_finish(sout, sgrad, out, sums)
    sout, sgrad, lt, rt, bg = run_train(args, False)
    width = lt.shape[1]
    ff = args[7].shape[2]
    index = lax.axis_index("seq") * lax.axis_size("dp") + lax.axis_index("dp")
    count = lax.axis_size("seq") * lax.axis_size("dp")
    qkv, wout, up, down, sums = grads_by_scatter(lt, rt, bg, ff)
    sums = sums.reshape(-1)

    def piece(start, rows):
        part = sums[start * width:(start + rows) * width]
        size = rows * width // count
        return lax.dynamic_slice_in_dim(part, index * size, size, 0)[None]

    return (
        sout[None],
        sgrad.astype(F32)[None],
        qkv[None],
        piece(0, 2),
        wout[None],
        piece(2, 2),
        up[None],
        piece(4, 4),
        down[None],
        piece(8, 2),
        piece(10, 2),
    )


def solution(mesh):
    return jax.shard_map(
        local,
        mesh=mesh,
        in_specs=(
            P("dp", "seq", None),
            P("dp", "seq", None),
            P("dp"),
            P("section", None, None),
            P("section", None),
            P("section", None, None),
            P("section", None),
            P("section", None, None),
            P("section", None),
            P("section", None, None),
            P("section", None),
            P("section", None),
        ),
        out_specs=(
            P("section", "dp", "seq", None),
            P("section", "dp", "seq", None),
            P("section", ("seq", "dp"), None),
            P("section", ("seq", "dp")),
            P("section", ("seq", "dp"), None),
            P("section", ("seq", "dp")),
            P("section", ("seq", "dp"), None),
            P("section", ("seq", "dp")),
            P("section", ("seq", "dp"), None),
            P("section", ("seq", "dp")),
            P("section", ("seq", "dp")),
        ),
        check_vma=False,
    )
```

```python
import functools

import jax
import jax.numpy as jnp
from jax import lax
from jax.experimental import pallas as pl
from jax.experimental.pallas import tpu as pltpu
from jax.sharding import PartitionSpec as P

H = 12
MICRO = 2
EPS = 1e-12
MESH = pl.DeviceIdType.MESH
BF = jnp.bfloat16
F32 = jnp.float32
LANES = 128
INV_SQRT_2PI = 0.3989422804014327
INV_SQRT_2 = 0.7071067811865476
L_F, L_N, L_O, L_X, L_COUNT = 0, 4, 5, 6, 7
R_P, R_A, R_U, R_Z, R_COUNT = 0, 3, 4, 8, 9
CHUNKS = 12
OUT = 8
QKV = 9
EARLY = 5
FROM_Y = (
    {5: 1, 8: 2, 11: 4, 13: 6, 15: 8, 16: 9, 17: 10, 19: 11},
    {k + 4: k for k in range(1, CHUNKS)},
)
SECOND = (
    {8: 3, 10: 1, 11: 5, 12: 7, 13: 2, 14: 4, 15: 6, 17: 8, 18: 9, 19: 10, 20: 11},
    {k + 5: k for k in range(1, CHUNKS)},
)
THIRD = tuple(
    {t + lag: k for t, k in table.items()} for lag, table in zip((2, 1), SECOND)
)
STEPS = 23
LANDINGS = 5
VMEM_LIMIT = 63 * 2 ** 20


def dot_nn(a, b):
    return lax.dot_general(a, b, (((1,), (0,)), ((), ())), preferred_element_type=F32)


def dot_nt(a, b):
    return lax.dot_general(a, b, (((1,), (1,)), ((), ())), preferred_element_type=F32)


def dot_tn(a, b):
    return lax.dot_general(a, b, (((0,), (0,)), ((), ())), preferred_element_type=F32)


def train_kernel(with_sums, *refs):
    refs = iter(refs)

    def take(number):
        return [next(refs) for _ in range(number)]

    (len_ref, in_hbm, cot_hbm, wqkv_hbm, wout_hbm, wup_hbm, wdown_hbm,
     abias_ref, obias_ref, bup_ref, gain_ref, shift_ref) = take(12)
    sout_hbm, sgrad_hbm = take(2)
    if with_sums:
        out_hbm, bg_out = take(2)
    else:
        lt, rt, bg = take(3)
    (ab, wqkv, wout, pool, wdown, q_s, kv, lse, o_s, n_s, xh1, xh2, rs1, rs2, dr1, acc, do_s,
     dkv_own, dkv_send, dkv_recv, yb) = take(21)
    (w_sem, loc_sem, ex_send, ex_recv, hop_send, hop_recv, kv_ss, kv_rs, dk_ss, dk_rs,
     out_loc, out_ss, out_rs) = take(13)
    if with_sums:
        (lt, rt, bg, out, lt_y, dz_y, core_src, y_buf, land, turn_src, turn_buf,
         b_src, b_core, b_y, b_z) = take(15)
        (core_ss, core_rs, y_ss, y_rs, z_ss, z_rs, turn_ss, turn_rs,
         bc_ss, bc_rs, bz_ss, bz_rs, part_sem, lt_ss, lt_rs, dz_ss, dz_rs) = take(17)

    width = wqkv.shape[0]
    ff = wdown.shape[0]
    span = in_hbm.shape[1]
    rows = 2 * span
    keys = 2 * rows
    hd = width // H
    pairs = H // 2
    half_pairs = H // 4
    nff = ff // width
    quarter = 4
    unit = width // 16
    sec = lax.axis_index("section")
    seq = lax.axis_index("seq")
    z = lax.axis_index("dp")
    count = lax.axis_size("dp")
    hi = seq // 2
    lo = seq % 2
    core_dev = (sec, hi * 2 + 1 - lo, z)
    y_dev = (sec, (1 - hi) * 2 + lo, z)
    x_dev = (1 - sec, seq, z)

    def z_dev(index):
        return (sec, seq, index)

    def remote(src, dst, send, recv, dev):
        return pltpu.make_async_remote_copy(
            src_ref=src, dst_ref=dst, send_sem=send, recv_sem=recv,
            device_id=dev, device_id_type=MESH,
        )

    weight_copies = [
        pltpu.make_async_copy(src.at[0], dst, w_sem.at[i])
        for i, (src, dst) in enumerate(((wqkv_hbm, wqkv), (wout_hbm, wout), (wdown_hbm, wdown)))
    ]
    tall = width // 4
    for j in range(nff):
        for part in range(4):
            weight_copies.append(
                pltpu.make_async_copy(
                    wup_hbm.at[0, pl.ds(part * tall, tall), pl.ds(j * width, width)],
                    pool.at[j * 4 + part],
                    w_sem.at[3],
                )
            )
    for copy in weight_copies:
        copy.start()

    partners = [core_dev, y_dev, x_dev]
    if with_sums:
        partners += [z_dev((z + by) % count) for by in range(1, count)]
    barrier = pltpu.get_barrier_semaphore()
    for dev in partners:
        pl.semaphore_signal(barrier, inc=1, device_id=dev, device_id_type=MESH)
    pl.semaphore_wait(barrier, len(partners))

    def mrows(m):
        return pl.ds(pl.multiple_of(m * rows, rows), rows)

    def own_copy(src, m):
        return pltpu.make_async_copy(
            src.at[2 * hi + m], ab.at[0, pl.ds(m * rows, span)], loc_sem.at[m]
        )

    def seq_copy(src, m):
        return remote(
            src.at[2 * (1 - hi) + m], ab.at[0, pl.ds(m * rows + span, span)],
            ex_send.at[m], ex_recv.at[m], y_dev,
        )

    for is_sec, src in ((0, in_hbm), (1, cot_hbm)):
        @pl.when(sec == is_sec)
        def _(src=src):
            seq_copy(src, 0).start()
            for m in range(MICRO):
                own_copy(src, m).start()

    bg[...] = jnp.zeros_like(bg)

    def hop_copy(src, m):
        return remote(src.at[mrows(m)], ab.at[1, mrows(m)], hop_send.at[m], hop_recv.at[m], x_dev)

    def kv_copy(m, part):
        return remote(
            kv.at[m, part, pl.ds(0, rows)], kv.at[m, part, pl.ds(rows, rows)],
            kv_ss.at[m, part], kv_rs.at[m, part], core_dev,
        )

    def dkv_copy(m, group):
        return remote(
            dkv_send.at[group], dkv_recv.at[m, group],
            dk_ss.at[m, group], dk_rs.at[m, group], core_dev,
        )

    def out_copies(kind, src, dst, m):
        table = 2 * hi + m
        base = m * rows
        return (
            pltpu.make_async_copy(src.at[pl.ds(base, span)], dst.at[table], out_loc.at[kind, m]),
            remote(
                src.at[pl.ds(base + span, span)], dst.at[table],
                out_ss.at[kind, m], out_rs.at[kind, m], y_dev,
            ),
        )

    def wait_slot(which, m):
        @pl.when(which == 0)
        def _():
            own_copy(in_hbm, m).wait()
            seq_copy(in_hbm, m).wait_recv()

            for is_sec, src in ((0, in_hbm), (1, cot_hbm)):
                @pl.when((m == 0) & (sec == is_sec))
                def _(src=src):
                    seq_copy(src, 1).start()

        @pl.when(which == 1)
        def _():
            hop_copy(yb, m).wait_recv()

    def positions(shape, dim):
        row = lax.broadcasted_iota(jnp.int32, shape, dim)
        block = row // span
        within = row % span
        half = jnp.where(block % 2 == 0, hi, 1 - hi)
        core = jnp.where(block < 2, lo, 1 - lo)
        return (half * 2 + core) * span + within

    def left_lanes():
        return lax.broadcasted_iota(jnp.int32, (1, LANES), 1) < hd

    def split_heads(value):
        left = left_lanes().astype(F32)
        return jnp.concatenate([value * left.astype(BF), value * (1.0 - left).astype(BF)], axis=0)

    def norm(resid, gain, shift):
        average = jnp.mean(resid, axis=-1, keepdims=True)
        centred = resid - average
        spread = jnp.mean(centred * centred, axis=-1, keepdims=True)
        scale = lax.rsqrt(spread + EPS)
        hat = centred * scale
        return hat, scale, hat * gain + shift

    def norm_back(grad, hat, scale, gain):
        dh = grad * gain
        return scale * (
            dh
            - jnp.mean(dh, axis=-1, keepdims=True)
            - hat * jnp.mean(dh * hat, axis=-1, keepdims=True)
        )

    def wup(j):
        return pool[4 * j:4 * j + 4].reshape(width, width)

    def vec(ref, part):
        return ref[0:1, part * width:(part + 1) * width].astype(F32)

    def add_bias_grad(row, value):
        bg[row] += jnp.sum(value, axis=0, keepdims=True)

    def left_copy(m):
        tall_half = 2 * tall
        return remote(
            lt.at[pl.ds(L_F, nff), pl.ds((1 - hi) * tall_half, tall_half), mrows(m)],
            lt_y.at[:, :, mrows(m)], lt_ss.at[m], lt_rs.at[m], y_dev,
        )

    def right_copy(m):
        return remote(rt.at[R_Z, mrows(m)], dz_y.at[mrows(m)], dz_ss.at[m], dz_rs.at[m], y_dev)


    def project(step, m):
        r = mrows(m)
        wait_slot(sec, m)

        @pl.when(step == 0)
        def _():
            weight_copies[0].wait()

        x = ab[sec, r]
        kv[m, 0, pl.ds(0, rows)] = dot_nn(x, wqkv[:, width:2 * width]).astype(BF)
        kv_copy(m, 0).start()
        kv[m, 1, pl.ds(0, rows)] = (
            dot_nn(x, wqkv[:, 2 * width:3 * width]) + vec(abias_ref, 1)
        ).astype(BF)
        kv_copy(m, 1).start()
        queries = (dot_nn(x, wqkv[:, 0:width]) + vec(abias_ref, 0)).astype(BF)
        q_s[r] = queries * (hd ** -0.5)
        lt[L_X, :, r] = x.T

        @pl.when(step == 0)
        def _():
            for copy in weight_copies[1:3]:
                copy.wait()
            whole = pool.at[pl.ds(0, 4 * nff)]
            pltpu.make_async_copy(whole, whole, w_sem.at[3]).wait()

    def forward(m):
        r = mrows(m)
        kv_copy(m, 0).wait_recv()
        kv_copy(m, 1).wait_recv()
        key_bias = jnp.where(positions((1, keys), 1) < len_ref[2 * hi + m], 0.0, -1e30)
        lane = lax.broadcasted_iota(jnp.int32, (1, LANES), 1)
        stats = jnp.zeros((keys, LANES), F32)
        for p in range(pairs):
            cols = pl.ds(p * LANES, LANES)
            scores = dot_nt(split_heads(q_s[r, cols]), kv[m, 0, :, cols]) + key_bias
            top = jnp.max(scores, axis=1, keepdims=True)
            e = jnp.exp(scores - top)
            total = jnp.sum(e, axis=1, keepdims=True)
            stats = jnp.where(lane == p, top + jnp.log(total), stats)
            o = dot_nn(e.astype(BF), kv[m, 1, :, cols]) * (1.0 / total)
            o_s[r, cols] = jnp.where(left_lanes(), o[0:rows], o[rows:2 * rows]).astype(BF)
        lse[m] = stats.T[0:8]

        r1 = ab[sec, r].astype(F32) + dot_nn(o_s[r], wout[...]) + vec(obias_ref, 0)
        hat, scale, n1 = norm(r1, vec(gain_ref, 0), vec(shift_ref, 0))
        xh1[r] = hat.astype(BF)
        rs1[r] = jnp.broadcast_to(scale, (rows, LANES))
        n_s[...] = n1.astype(BF)
        acc[...] = n1 + vec(obias_ref, 1)
        for j in range(nff):
            cols = pl.ds(j * width, width)
            u = dot_nn(n_s[...], wup(j)) + bup_ref[0:1, cols].astype(F32)
            phi = 0.5 + 0.5 * lax.erf(u * INV_SQRT_2)
            f = (u * phi).astype(BF)
            f_t = f.T
            for owner in range(quarter):
                for part in range(nff):
                    at = (owner * nff + part) * unit
                    lt[part, pl.ds((j * quarter + owner) * unit, unit), r] = f_t[at:at + unit]
            rt[R_U + j, r] = (phi + u * (jnp.exp(-0.5 * u * u) * INV_SQRT_2PI)).astype(BF)
            acc[...] += dot_nn(f, wdown[cols, :])
        hat, scale, result = norm(acc[...], vec(gain_ref, 1), vec(shift_ref, 1))
        xh2[r] = hat.astype(BF)
        rs2[r] = jnp.broadcast_to(scale, (rows, LANES))
        yb[r] = result.astype(BF)

        @pl.when(sec == 0)
        def _():
            hop_copy(yb, m).start()

        for copy in out_copies(0, yb, sout_hbm, m):
            copy.start()
        if with_sums:
            @pl.when(sec == 0)
            def _():
                left_copy(m).start()

        lt[L_N, :, r] = n_s[...].T
        lt[L_O, :, r] = o_s[r].T

    def backward(m, serve):
        r = mrows(m)
        wait_slot(1 - sec, m)
        length = len_ref[2 * hi + m]
        row_scale = jnp.where((sec == 0) | (positions((rows, 1), 0) < length), 1.0, 0.0)
        dy = ab[1 - sec, r].astype(F32) * row_scale
        hat = xh2[r].astype(F32)
        add_bias_grad(9, dy * hat)
        add_bias_grad(11, dy)
        dr2 = norm_back(dy, hat, rs2[r, 0:1], vec(gain_ref, 1))
        dz = dr2.astype(BF)
        rt[R_Z, r] = dz
        if with_sums:
            @pl.when(sec == 0)
            def _():
                right_copy(m).start()

        add_bias_grad(3, dz.astype(F32))
        acc[...] = dr2
        serve(0, 1)
        for j in range(nff):
            cols = pl.ds(j * width, width)
            du = (dot_nt(rt[R_Z, r], wdown[cols, :]) * rt[R_U + j, r].astype(F32)).astype(BF)
            rt[R_U + j, r] = du
            bg[4 + j] += jnp.sum(du.astype(F32), axis=0, keepdims=True)
            acc[...] += dot_nt(du, wup(j))
        serve(1, 3)
        dn1 = acc[...]
        hat = xh1[r].astype(F32)
        add_bias_grad(8, dn1 * hat)
        add_bias_grad(10, dn1)
        grad1 = norm_back(dn1, hat, rs1[r, 0:1], vec(gain_ref, 0))
        dr1[...] = grad1
        da = grad1.astype(BF)
        rt[R_A, r] = da
        add_bias_grad(2, da.astype(F32))
        do_s[...] = dot_nt(da, wout[...]).astype(BF)
        key_bias = jnp.where(positions((keys, 1), 0) < length, 0.0, -1e30)

        def head_pair(group, index):
            p = group * half_pairs + index
            cols = pl.ds(p * LANES, LANES)
            kcols = pl.ds(index * LANES, LANES)
            vcols = pl.ds((half_pairs + index) * LANES, LANES)
            qq = split_heads(q_s[r, cols])
            dd = split_heads(do_s[:, cols])
            kp = kv[m, 0, :, cols]
            pt = jnp.exp(dot_nt(kp, qq) + key_bias - lse[m, p:p + 1])
            dv = dot_nn(pt.astype(BF), dd)
            dpt = dot_nt(kv[m, 1, :, cols], dd)
            sums = jnp.sum(pt * dpt, axis=0, keepdims=True)
            ds = (pt * (dpt - sums)).astype(BF)
            dk = dot_nn(ds, qq)
            dq_t = dot_tn(kp, ds)
            dq_pair = jnp.concatenate([dq_t[0:hd, 0:rows], dq_t[hd:2 * hd, rows:2 * rows]], axis=0)
            rt[R_P, r, cols] = (dq_pair.T * (hd ** -0.5)).astype(BF)
            dkv_own[group, :, kcols] = dk[0:rows]
            dkv_own[group, :, vcols] = dv[0:rows]
            dkv_send[group, :, kcols] = dk[rows:keys].astype(BF)
            dkv_send[group, :, vcols] = dv[rows:keys].astype(BF)

        for group in range(2):
            for index in range(half_pairs):
                head_pair(group, index)
            dkv_copy(m, group).start()
            if group == 0:
                serve(3, EARLY)
        dq = rt[R_P, r]
        add_bias_grad(0, dq.astype(F32))
        dr1[...] += dot_nt(dq, wqkv[:, 0:width])

    def input_grad(m):
        r = mrows(m)
        dx = dr1[...]
        part = width // 2
        for group in range(2):
            dkv_copy(m, group).wait_recv()
            both = (dkv_own[group] + dkv_recv[m, group].astype(F32)).astype(BF)
            for which in range(2):
                at = (1 + which) * width + group * part
                piece = both[:, which * part:(which + 1) * part]
                rt[R_P + 1 + which, r, group * part:(group + 1) * part] = piece
                dx = dx + dot_nt(piece, wqkv[:, at:at + part])
        local_out, remote_out = out_copies(0, yb, sout_hbm, m)
        local_out.wait()
        remote_out.wait_send()

        @pl.when(sec == 0)
        def _():
            hop_copy(yb, m).wait_send()

        yb[r] = dx.astype(BF)

        @pl.when(sec == 1)
        def _():
            hop_copy(yb, m).start()

        @pl.when(m == 0)
        def _():
            send_input_grad(m)

        for group in range(2):
            dkv_copy(m, group).wait_send()
        add_bias_grad(1, rt[R_P + 2, r].astype(F32))

    def send_input_grad(m):
        for copy in out_copies(1, yb, sgrad_hbm, m):
            copy.start()


    if with_sums:
        block = count * unit
        two = 2 * unit

        def of_down(k):
            return (k == 0) | ((k % 2 == 1) & (k >= 3) & (k < OUT))

        def is_down(k):
            return (sec == 0) & of_down(k) & (k > 0)

        def slot_of(k, half):
            return jnp.where(k < 4, 4 * nff + 2 * k, 2 * k - 8) + half

        def core_copy(k, i, half):
            return remote(
                core_src.at[k % 2, i], pool.at[slot_of(k, half)],
                core_ss.at[k % 2, i], core_rs.at[k % 4, i], core_dev,
            )

        def y_copy(k, i):
            rows_of = pl.ds(pl.multiple_of(jnp.where(z < count // 2, 1 - i, i) * two, two), two)
            slot = k - 1
            return rows_of, y_buf.at[slot, i], remote(
                pool.at[slot_of(k, 1 - hi), rows_of], y_buf.at[slot, i],
                y_ss.at[slot, i], y_rs.at[slot, i], y_dev,
            )

        def turn_copy():
            return remote(turn_src, turn_buf, turn_ss, turn_rs, y_dev)

        def piece(k, half, target):
            return pool.at[slot_of(k, half), pl.ds(pl.multiple_of(target * unit, unit), unit)]

        def up_copy(job, k, half, target):
            i = target - 1
            return remote(
                piece(k, half, target), land.at[job, i], z_ss.at[job, i], z_rs.at[job, i],
                z_dev(jnp.minimum(z + 1, count - 1)),
            )

        def down_copy(job, k, half, target):
            i = (target + count - 1) % LANDINGS
            return remote(
                piece(k, half, target), land.at[job, i], z_ss.at[job, target], z_rs.at[job, i],
                z_dev(jnp.maximum(z - 1, 0)),
            )

        def add_to(ref, landed):
            ref[...] = (ref[...].astype(F32) + landed[...].astype(F32)).astype(BF)

        def hop(number, job, k, half):
            @pl.when(z == number - 1)
            def _():
                for target in range(count - 1, number - 1, -1):
                    copy = up_copy(job, k, half, target)
                    if number > 1:
                        copy.wait_recv()
                        add_to(piece(k, half, target), land.at[job, target - 1])
                    copy.start()

            @pl.when(z == count - number)
            def _():
                for target in range(0, count - number):
                    copy = down_copy(job, k, half, target)
                    if number > 1:
                        copy.wait_recv()
                        add_to(piece(k, half, target), land.at[job, (target + count - 1) % LANDINGS])
                    copy.start()

        def arrive(job, k, half):
            out[k] = piece(k, half, z)[...].astype(F32)

            @pl.when(z > 0)
            def _():
                up_copy(job, k, half, jnp.maximum(z, 1)).wait_recv()
                out[k] += land[job, jnp.maximum(z, 1) - 1].astype(F32)

            @pl.when(z < count - 1)
            def _():
                down_copy(job, k, half, z).wait_recv()
                out[k] += land[job, (z + count - 1) % LANDINGS].astype(F32)

        def product(k, number):
            left = jnp.where(of_down(k), L_F + k // 2, L_N)
            left = jnp.where(k < OUT, left, jnp.where(k == OUT, L_O, L_X))
            right = jnp.where(of_down(k), R_Z, R_U + k // 2)
            right = jnp.where(k < OUT, right, jnp.where(k == OUT, R_A, R_P + k - QKV))
            base = pl.multiple_of(number * block, block)
            return dot_nn(lt[left, pl.ds(base, block), :], rt[right])

        def down_product(k, core):
            part = k // 2
            own_rows = pl.ds(pl.multiple_of((hi * 2 + core) * block, block), block)
            rows_y = pl.ds(pl.multiple_of(core * block, block), block)
            return dot_nn(lt[L_F + part, own_rows, :], rt[R_Z]) + dot_nn(
                lt_y[part, rows_y, :], dz_y[...]
            )

        def for_core(k):
            @pl.when((k >= 2) & is_down(k - 2))
            def _():
                core_copy(k - 2, 0, hi).wait_send()

            @pl.when((k >= 2) & jnp.logical_not(is_down(k - 2)))
            def _():
                for half in range(2):
                    core_copy(k - 2, half, half).wait_send()

            @pl.when((sec == 0) & (k == 3))
            def _():
                for m in range(MICRO):
                    left_copy(m).wait_recv()
                    right_copy(m).wait_recv()

            @pl.when(is_down(k))
            def _():
                core_src[k % 2, 0] = down_product(k, 1 - lo).astype(BF)
                core_copy(k, 0, hi).start()

            @pl.when(jnp.logical_not(is_down(k)))
            def _():
                for half in range(2):
                    core_src[k % 2, half] = product(k, half * 2 + 1 - lo).astype(BF)
                    core_copy(k, half, half).start()

        def chip_sum(k):
            @pl.when(is_down(k))
            def _():
                core_copy(k, 0, hi).wait_recv()
                slot = slot_of(k, hi)
                pool[slot] = (down_product(k, lo) + pool[slot].astype(F32)).astype(BF)
                hop(1, k, k, hi)

            @pl.when(jnp.logical_not(is_down(k)))
            def _():
                for half in range(2):
                    core_copy(k, half, half).wait_recv()
                    slot = slot_of(k, half)
                    pool[slot] = (product(k, half * 2 + lo) + pool[slot].astype(F32)).astype(BF)

                @pl.when(k == 0)
                def _():
                    for job, half in ((0, hi), (CHUNKS, 1 - hi)):
                        hop(1, job, 0, half)

                @pl.when(k > 0)
                def _():
                    for i in range(2):
                        y_copy(k, i)[2].start()

        def from_y(k):
            for i in range(2):
                rows_of, landed, copy = y_copy(k, i)
                copy.wait_recv()
                add_to(pool.at[slot_of(k, hi), rows_of], landed)

                @pl.when(z == 0)
                def _(i=i):
                    for target in ((3, 2), (1,))[i]:
                        up_copy(k, k, hi, target).start()

                @pl.when(z == count - 1)
                def _(i=i):
                    for target in ((0, 1), (2,))[i]:
                        down_copy(k, k, hi, target).start()

        def part_copy(k):
            return pltpu.make_async_copy(out.at[k], out_hbm.at[k], part_sem)

        def bias_core():
            return remote(b_src.at[0], b_core, bc_ss.at[0], bc_rs.at[0], core_dev)

        def bias_y():
            return remote(b_src.at[1], b_y, bc_ss.at[1], bc_rs.at[1], y_dev)

        def bias_z(by):
            return remote(
                b_src.at[2], b_z.at[by - 1], bz_ss.at[by - 1], bz_rs.at[by - 1],
                z_dev((z + by) % count),
            )

        def sum_step(t):
            @pl.when(t < CHUNKS)
            def _():
                for_core(t)

            @pl.when(((t >= 2) & (t <= CHUNKS)) | (t == 0))
            def _():
                chip_sum(jnp.maximum(t - 1, 0))

            def at(tables, action):
                k = -1
                for section, table in enumerate(tables):
                    for when, chunk in table.items():
                        k = jnp.where((sec == section) & (t == when), chunk, k)

                @pl.when(k >= 0)
                def _():
                    action(k)

            def both_halves(number):
                for job, half in ((0, hi), (CHUNKS, 1 - hi)):
                    hop(number, job, 0, half)

            at(FROM_Y, from_y)
            at(THIRD, lambda k: hop(3, k, k, hi))
            at(SECOND, lambda k: hop(2, k, k, hi))

            @pl.when(t == 6)
            def _():
                both_halves(2)

            @pl.when(t == 10)
            def _():
                both_halves(3)

            @pl.when(t == CHUNKS + 1)
            def _():
                send_input_grad(MICRO - 1)

            @pl.when(t == CHUNKS + 1)
            def _():
                arrive(CHUNKS, 0, 1 - hi)
                turn_src[...] = out[0].astype(BF)
                turn_copy().start()
                arrive(0, 0, hi)

            @pl.when(t == 5)
            def _():
                b_src[0] = bg[...]
                bias_core().start()

            @pl.when(t == 6)
            def _():
                bias_core().wait_recv()
                b_src[1] = b_src[0] + b_core[...]
                bias_y().start()

            @pl.when(t == 16)
            def _():
                bias_y().wait_recv()
                b_src[2] = b_src[1] + b_y[...]
                for by in range(1, count):
                    bias_z(by).start()

    def one_step(step, carry):
        first = sec == 0

        def among(*steps):
            hit = step == steps[0]
            for value in steps[1:]:
                hit = hit | (step == value)
            return hit

        late_forward = ((step == 3) & first) | ((step == 4) & jnp.logical_not(first))
        early_backward = ((step == 4) & first) | ((step == 3) & jnp.logical_not(first))
        m = jnp.where(among(2, 6, 7) | late_forward, 1, 0)

        def serve(start, stop):
            if with_sums:
                @pl.when((step == 6) & first)
                def _():
                    def body(t, c):
                        sum_step(t)
                        return c

                    lax.fori_loop(start, stop, body, 0)

        @pl.when(among(0, 2))
        def _():
            project(step, m)

        @pl.when((step == 1) | late_forward)
        def _():
            forward(m)

        @pl.when((step == 6) | early_backward)
        def _():
            backward(m, serve)

        @pl.when(among(5, 7))
        def _():
            input_grad(m)

        return carry

    lax.fori_loop(0, 8, one_step, 0)

    if not with_sums:
        send_input_grad(MICRO - 1)

    if with_sums:
        def rest(t, carry):
            sum_step(t)
            return carry

        lax.fori_loop(jnp.where(sec == 0, EARLY, 0), STEPS, rest, 0)

        def last_sum(k, carry):
            arrive(k, k, hi)
            part_copy(k).start()
            return carry

        lax.fori_loop(1, CHUNKS, last_sum, 0)
        turn_copy().wait_recv()
        out[0] += turn_buf[...].astype(F32)
        part_copy(0).start()

        total = b_src[2]
        for by in range(1, count):
            bias_z(by).wait_recv()
            total = total + b_z[by - 1]
        bg_out[...] = total
        bias_core().wait_send()
        bias_y().wait_send()
        for by in range(1, count):
            bias_z(by).wait_send()

        def sent(job, k, half):
            for target in range(count):
                if target > 0:
                    @pl.when(target > z)
                    def _(target=target):
                        up_copy(job, k, half, target).wait_send()

                if target < count - 1:
                    @pl.when(target < z)
                    def _(target=target):
                        down_copy(job, k, half, target).wait_send()

        def drain(k, carry):
            sent(k, k, hi)

            @pl.when((k > 0) & jnp.logical_not(is_down(k)))
            def _():
                for i in range(2):
                    y_copy(k, i)[2].wait_send()

            return carry

        lax.fori_loop(0, CHUNKS, drain, 0)
        pltpu.make_async_copy(out, out_hbm, part_sem).wait()
        sent(CHUNKS, 0, 1 - hi)
        turn_copy().wait_send()
        for k in (CHUNKS - 2, CHUNKS - 1):
            for half in range(2):
                core_copy(k, half, half).wait_send()

        @pl.when(sec == 0)
        def _():
            for m in range(MICRO):
                left_copy(m).wait_send()
                right_copy(m).wait_send()

    for m in range(MICRO):
        seq_copy(in_hbm, m).wait_send()
        for part in range(2):
            kv_copy(m, part).wait_send()
        out_copies(0, yb, sout_hbm, m)[1].wait_recv()
        local_out, remote_out = out_copies(1, yb, sgrad_hbm, m)
        local_out.wait()
        remote_out.wait()

        @pl.when(sec == 1)
        def _():
            hop_copy(yb, m).wait_send()


def run_train(args, with_sums):
    (inputs, cotangent, lengths, w_qkv, attn_bias, w_out, out_bias, w_up, bias_up, w_down,
     norm_gain, norm_bias) = args
    tables, span, width = inputs.shape
    ff = w_up.shape[2]
    rows = 2 * span
    total = MICRO * rows
    keys = 2 * rows
    count = lax.axis_size("dp")
    unit = width // 16
    block = count * unit
    tall = width // 4
    any_spec = pl.BlockSpec(memory_space=pl.ANY)
    vmem = pl.BlockSpec(memory_space=pltpu.VMEM)
    smem = pl.BlockSpec(memory_space=pltpu.SMEM)
    dma = pltpu.SemaphoreType.DMA
    shape = jax.ShapeDtypeStruct
    stacks = (
        ((L_COUNT, width, total), BF),
        ((R_COUNT, total, width), BF),
        ((12, 1, width), F32),
    )
    if with_sums:
        results = (((CHUNKS, unit, width), F32), ((12, 1, width), F32))
    else:
        results = stacks
    scratch = [
        pltpu.VMEM((2, total, width), BF),
        pltpu.VMEM((width, 3 * width), BF),
        pltpu.VMEM((width, width), BF),
        pltpu.VMEM((ff // tall + (8 if with_sums else 0), tall, width), BF),
        pltpu.VMEM((ff, width), BF),
        pltpu.VMEM((total, width), BF),
        pltpu.VMEM((MICRO, 2, keys, width), BF),
        pltpu.VMEM((MICRO, 8, keys), F32),
        pltpu.VMEM((total, width), BF),
        pltpu.VMEM((rows, width), BF),
        pltpu.VMEM((total, width), BF),
        pltpu.VMEM((total, width), BF),
        pltpu.VMEM((total, LANES), F32),
        pltpu.VMEM((total, LANES), F32),
        pltpu.VMEM((rows, width), F32),
        pltpu.VMEM((rows, width), F32),
        pltpu.VMEM((rows, width), BF),
        pltpu.VMEM((2, rows, width), F32),
        pltpu.VMEM((2, rows, width), BF),
        pltpu.VMEM((MICRO, 2, rows, width), BF),
        pltpu.VMEM((total, width), BF),
        dma((4,)), dma((MICRO,)), dma((MICRO,)), dma((MICRO,)), dma((MICRO,)), dma((MICRO,)),
        dma((MICRO, 2)), dma((MICRO, 2)), dma((MICRO, 2)), dma((MICRO, 2)),
        dma((2, MICRO)), dma((2, MICRO)), dma((2, MICRO)),
    ]
    if with_sums:
        scratch += [pltpu.VMEM(dims, kind) for dims, kind in stacks]
        scratch += [
            pltpu.VMEM((CHUNKS, unit, width), F32),
            pltpu.VMEM((ff // width, 2 * block, total), BF),
            pltpu.VMEM((total, width), BF),
            pltpu.VMEM((2, 2, block, width), BF),
            pltpu.VMEM((CHUNKS - 1, 2, 2 * unit, width), BF),
            pltpu.VMEM((CHUNKS + 1, LANDINGS, unit, width), BF),
            pltpu.VMEM((unit, width), BF),
            pltpu.VMEM((unit, width), BF),
            pltpu.VMEM((3, 12, 1, width), F32),
            pltpu.VMEM((12, 1, width), F32),
            pltpu.VMEM((12, 1, width), F32),
            pltpu.VMEM((count - 1, 12, 1, width), F32),
            dma((2, 2)), dma((4, 2)), dma((CHUNKS - 1, 2)), dma((CHUNKS - 1, 2)),
            dma((CHUNKS + 1, count - 1)), dma((CHUNKS + 1, LANDINGS)), dma, dma,
            dma((2,)), dma((2,)), dma((count - 1,)), dma((count - 1,)), dma,
            dma((MICRO,)), dma((MICRO,)), dma((MICRO,)), dma((MICRO,)),
        ]
    return pl.pallas_call(
        functools.partial(train_kernel, with_sums),
        name="train",
        out_shape=(shape((tables, span, width), BF), shape((tables, span, width), BF))
        + tuple(shape(dims, kind) for dims, kind in results),
        in_specs=[smem] + [any_spec] * 6 + [vmem] * 5,
        out_specs=(any_spec, any_spec)
        + ((any_spec, vmem) if with_sums else (vmem,) * len(results)),
        scratch_shapes=scratch,
        compiler_params=pltpu.CompilerParams(
            collective_id=0, has_side_effects=True, vmem_limit_bytes=VMEM_LIMIT
        ),
    )(lengths, inputs, cotangent, w_qkv, w_out, w_up, w_down,
      attn_bias, out_bias, bias_up, norm_gain, norm_bias)


def grads_by_scatter(lt, rt, bg, ff):
    width = lt.shape[1]
    parts = ff // width

    def scatter(full):
        return lax.psum_scatter(
            full.astype(BF), ("seq", "dp"), scatter_dimension=0, tiled=True
        ).astype(F32)

    left_f = lt[:parts].reshape(parts, 4, 4, width // 16, -1).transpose(1, 2, 0, 3, 4)
    down = scatter(dot_nn(left_f.reshape(ff, -1), rt[R_Z]))
    up = scatter(jnp.concatenate([dot_nn(lt[L_N], rt[R_U + j]) for j in range(parts)], axis=1))
    wout = scatter(dot_nn(lt[L_O], rt[R_A]))
    qkv = scatter(jnp.concatenate([dot_nn(lt[L_X], rt[R_P + j]) for j in range(3)], axis=1))
    return qkv, wout, up, down, lax.psum(bg, ("seq", "dp"))


def finish_kernel(
    sout, sgrad, grads, sums_hbm,
    sout_ref, sgrad_ref, qkv_ref, abias_ref, wout_ref, obias_ref, up_ref, bup_ref, down_ref,
    gain_ref, shift_ref,
    kept, low, wide_grad, parts, sums, sem,
):
    unit, width = grads.shape[1:]
    size = abias_ref.shape[1]

    def copy(i, src, dst):
        started = pltpu.make_async_copy(src, dst, sem.at[i])
        started.start()
        return started

    sums_in = copy(0, sums_hbm, sums)
    grad_in = copy(1, sgrad, low)
    out_in = copy(2, sout, kept)
    parts_in = copy(3, grads, parts)
    grad_in.wait()
    wide_grad[...] = low[...].astype(F32)
    copies = [copy(4, wide_grad, sgrad_ref.at[0])]
    out_in.wait()
    copies.append(copy(5, kept, sout_ref.at[0]))
    parts_in.wait()
    for k in range(CHUNKS):
        if k in (0, 3, 5, 7):
            dst = down_ref.at[0, pl.ds(k // 2 * unit, unit), :]
        elif k < OUT:
            dst = up_ref.at[0, :, pl.ds(k // 2 * width, width)]
        elif k == OUT:
            dst = wout_ref.at[0]
        else:
            dst = qkv_ref.at[0, :, pl.ds((k - QKV) * width, width)]
        copies.append(copy(6 + k, parts.at[k], dst))
    sums_in.wait()
    index = lax.axis_index("seq") * lax.axis_size("dp") + lax.axis_index("dp")
    whole = width // size
    pairs = [jnp.where(index < whole, sums[row], sums[row + 1]) for row in (0, 2, 8, 10)]
    block = jnp.concatenate(pairs + pairs, axis=0)
    block = pltpu.roll(block, (width - (index % whole) * size) % width, axis=1)
    for row, ref in enumerate((abias_ref, obias_ref, gain_ref, shift_ref)):
        ref[...] = block[row:row + 1, 0:size]
    wide = 2 * size
    per = width // wide
    rows = sums[4]
    for row in range(1, 4):
        rows = jnp.where(index // per == row, sums[4 + row], rows)
    rows = pltpu.roll(
        jnp.concatenate([rows] * 8, axis=0), (width - (index % per) * wide) % width, axis=1
    )
    bup_ref[...] = rows[0:1, 0:wide]
    for started in copies:
        started.wait()


def run_finish(sout, sgrad, grads, sums):
    unit, width = grads.shape[1:]
    size = width // 8
    vmem = pl.BlockSpec(memory_space=pltpu.VMEM)
    any_spec = pl.BlockSpec(memory_space=pl.ANY)
    shape = jax.ShapeDtypeStruct
    return pl.pallas_call(
        finish_kernel,
        name="finish",
        out_shape=(
            shape((1,) + sout.shape, BF),
            shape((1,) + sgrad.shape, F32),
            shape((1, unit, 3 * width), F32),
            shape((1, size), F32),
            shape((1, unit, width), F32),
            shape((1, size), F32),
            shape((1, unit, 4 * width), F32),
            shape((1, 2 * size), F32),
            shape((1, 4 * unit, width), F32),
            shape((1, size), F32),
            shape((1, size), F32),
        ),
        in_specs=[any_spec] * 4,
        out_specs=(any_spec, any_spec, any_spec, vmem, any_spec, vmem, any_spec, vmem, any_spec,
                   vmem, vmem),
        scratch_shapes=[
            pltpu.VMEM(sout.shape, BF),
            pltpu.VMEM(sgrad.shape, BF),
            pltpu.VMEM(sgrad.shape, F32),
            pltpu.VMEM(grads.shape, F32),
            pltpu.VMEM(sums.shape, F32),
            pltpu.SemaphoreType.DMA((6 + CHUNKS,)),
        ],
        compiler_params=pltpu.CompilerParams(vmem_limit_bytes=VMEM_LIMIT),
    )(sout, sgrad, grads, sums)


def local(*args):
    if lax.axis_size("dp") == 4:
        sout, sgrad, out, sums = run_train(args, True)
        return run_finish(sout, sgrad, out, sums)
    sout, sgrad, lt, rt, bg = run_train(args, False)
    width = lt.shape[1]
    ff = args[7].shape[2]
    index = lax.axis_index("seq") * lax.axis_size("dp") + lax.axis_index("dp")
    count = lax.axis_size("seq") * lax.axis_size("dp")
    qkv, wout, up, down, sums = grads_by_scatter(lt, rt, bg, ff)
    sums = sums.reshape(-1)

    def piece(start, rows):
        part = sums[start * width:(start + rows) * width]
        size = rows * width // count
        return lax.dynamic_slice_in_dim(part, index * size, size, 0)[None]

    return (
        sout[None],
        sgrad.astype(F32)[None],
        qkv[None],
        piece(0, 2),
        wout[None],
        piece(2, 2),
        up[None],
        piece(4, 4),
        down[None],
        piece(8, 2),
        piece(10, 2),
    )


def solution(mesh):
    return jax.shard_map(
        local,
        mesh=mesh,
        in_specs=(
            P("dp", "seq", None),
            P("dp", "seq", None),
            P("dp"),
            P("section", None, None),
            P("section", None),
            P("section", None, None),
            P("section", None),
            P("section", None, None),
            P("section", None),
            P("section", None, None),
            P("section", None),
            P("section", None),
        ),
        out_specs=(
            P("section", "dp", "seq", None),
            P("section", "dp", "seq", None),
            P("section", ("seq", "dp"), None),
            P("section", ("seq", "dp")),
            P("section", ("seq", "dp"), None),
            P("section", ("seq", "dp")),
            P("section", ("seq", "dp"), None),
            P("section", ("seq", "dp")),
            P("section", ("seq", "dp"), None),
            P("section", ("seq", "dp")),
            P("section", ("seq", "dp")),
        ),
        check_vma=False,
    )
```

```python
import functools

import jax
import jax.numpy as jnp
from jax import lax
from jax.experimental import pallas as pl
from jax.experimental.pallas import tpu as pltpu
from jax.sharding import PartitionSpec as P

H = 12
MICRO = 2
EPS = 1e-12
MESH = pl.DeviceIdType.MESH
BF = jnp.bfloat16
F32 = jnp.float32
LANES = 128
INV_SQRT_2PI = 0.3989422804014327
INV_SQRT_2 = 0.7071067811865476
L_F, L_N, L_O, L_X, L_COUNT = 0, 4, 5, 6, 7
R_P, R_A, R_U, R_Z, R_COUNT = 0, 3, 4, 8, 9
CHUNKS = 12
OUT = 8
QKV = 9
EARLY = 6
FROM_Y = (
    {5: 1, 7: 2, 10: 4, 13: 6, 15: 8, 16: 9, 17: 10, 19: 11},
    {5: 1, 6: 2, 7: 3, 9: 5, 10: 6, 11: 7, 12: 8, 13: 9, 14: 10, 15: 11},
)
SECOND = (
    {8: 3, 10: 1, 11: 5, 12: 7, 13: 2, 14: 4, 15: 6, 17: 8, 18: 9, 19: 10, 20: 11},
    {7: 1, 8: 2, 9: 3, 10: 5, 11: 6, 12: 7, 13: 8, 14: 9, 15: 10, 16: 11},
)
THIRD = tuple(
    {t + lag: k for t, k in table.items()} for lag, table in zip((2, 1), SECOND)
)
ARRIVE = (
    {14: 3, 15: 1, 16: 5, 17: 7, 18: 2, 19: 4, 20: 6, 21: 8},
    {11: 1, 12: 2, 13: 3, 15: 5, 16: 6, 17: 7, 18: 8},
)
Z_FIRST = 2
Z_SECOND = ({5: 0}, {6: 0, 9: 4})
Z_THIRD = ({9: 0}, {8: 0, 11: 4})
TURN = ({14: 0}, {13: 0, 14: 4})
LAST = QKV
STEPS = 23
LANDINGS = 5
Y_SLOTS = 10
VMEM_LIMIT = 127 * 2 ** 19


def dot_nn(a, b):
    return lax.dot_general(a, b, (((1,), (0,)), ((), ())), preferred_element_type=F32)


def dot_nt(a, b):
    return lax.dot_general(a, b, (((1,), (1,)), ((), ())), preferred_element_type=F32)


def dot_tn(a, b):
    return lax.dot_general(a, b, (((0,), (0,)), ((), ())), preferred_element_type=F32)


def train_kernel(with_sums, *refs):
    refs = iter(refs)

    def take(number):
        return [next(refs) for _ in range(number)]

    (len_ref, in_hbm, cot_hbm, wqkv_hbm, wout_hbm, wup_hbm, wdown_hbm,
     abias_ref, obias_ref, bup_ref, gain_ref, shift_ref) = take(12)
    sout_hbm, sgrad_hbm = take(2)
    if with_sums:
        out_hbm, bg_out = take(2)
    else:
        lt, rt, bg = take(3)
    (ab, wqkv, wout, pool, wdown, q_s, kv, lse, o_s, n_s, xh1, xh2, rs, dr1, acc, do_s,
     dkv_own, dkv_send, dkv_recv, yb) = take(20)
    (w_sem, loc_sem, ex_send, ex_recv, hop_send, hop_recv, kv_ss, kv_rs, dk_ss, dk_rs,
     out_loc, out_ss, out_rs) = take(13)
    if with_sums:
        (lt, rt, bg, out, lt_y, dz_y, core_src, y_buf, land, turn_src, turn_buf,
         b_src, b_core, b_y, b_z) = take(15)
        (core_ss, core_rs, y_ss, y_rs, z_ss, z_rs, turn_ss, turn_rs,
         bc_ss, bc_rs, bz_ss, bz_rs, part_sem, lt_ss, lt_rs, dz_ss, dz_rs) = take(17)

    width = wqkv.shape[0]
    ff = wdown.shape[0]
    span = in_hbm.shape[1]
    rows = 2 * span
    keys = 2 * rows
    hd = width // H
    pairs = H // 2
    half_pairs = H // 4
    nff = ff // width
    quarter = 4
    unit = width // 16
    sec = lax.axis_index("section")
    seq = lax.axis_index("seq")
    z = lax.axis_index("dp")
    count = lax.axis_size("dp")
    hi = seq // 2
    lo = seq % 2
    core_dev = (sec, hi * 2 + 1 - lo, z)
    y_dev = (sec, (1 - hi) * 2 + lo, z)
    x_dev = (1 - sec, seq, z)

    def z_dev(index):
        return (sec, seq, index)

    def remote(src, dst, send, recv, dev):
        return pltpu.make_async_remote_copy(
            src_ref=src, dst_ref=dst, send_sem=send, recv_sem=recv,
            device_id=dev, device_id_type=MESH,
        )

    weight_copies = [
        pltpu.make_async_copy(src.at[0], dst, w_sem.at[i])
        for i, (src, dst) in enumerate(((wqkv_hbm, wqkv), (wout_hbm, wout), (wdown_hbm, wdown)))
    ]
    tall = width // 4
    for j in range(nff):
        for part in range(4):
            weight_copies.append(
                pltpu.make_async_copy(
                    wup_hbm.at[0, pl.ds(part * tall, tall), pl.ds(j * width, width)],
                    pool.at[j * 4 + part],
                    w_sem.at[3],
                )
            )
    for copy in weight_copies:
        copy.start()

    partners = [core_dev, y_dev, x_dev]
    if with_sums:
        partners += [z_dev((z + by) % count) for by in range(1, count)]
    barrier = pltpu.get_barrier_semaphore()
    for dev in partners:
        pl.semaphore_signal(barrier, inc=1, device_id=dev, device_id_type=MESH)
    pl.semaphore_wait(barrier, len(partners))

    def mrows(m):
        return pl.ds(pl.multiple_of(m * rows, rows), rows)

    def own_copy(src, m):
        return pltpu.make_async_copy(
            src.at[2 * hi + m], ab.at[0, pl.ds(m * rows, span)], loc_sem.at[m]
        )

    def seq_copy(src, m):
        return remote(
            src.at[2 * (1 - hi) + m], ab.at[0, pl.ds(m * rows + span, span)],
            ex_send.at[m], ex_recv.at[m], y_dev,
        )

    for is_sec, src in ((0, in_hbm), (1, cot_hbm)):
        @pl.when(sec == is_sec)
        def _(src=src):
            seq_copy(src, 0).start()
            for m in range(MICRO):
                own_copy(src, m).start()

    bg[...] = jnp.zeros_like(bg)

    def hop_copy(src, m):
        return remote(src.at[mrows(m)], ab.at[1, mrows(m)], hop_send.at[m], hop_recv.at[m], x_dev)

    def kv_copy(m, part):
        return remote(
            kv.at[m, part, pl.ds(0, rows)], kv.at[m, part, pl.ds(rows, rows)],
            kv_ss.at[m, part], kv_rs.at[m, part], core_dev,
        )

    def dkv_copy(m, group):
        return remote(
            dkv_send.at[group], dkv_recv.at[m, group],
            dk_ss.at[m, group], dk_rs.at[m, group], core_dev,
        )

    def out_copies(kind, src, dst, m):
        table = 2 * hi + m
        base = m * rows
        return (
            pltpu.make_async_copy(src.at[pl.ds(base, span)], dst.at[table], out_loc.at[kind, m]),
            remote(
                src.at[pl.ds(base + span, span)], dst.at[table],
                out_ss.at[kind, m], out_rs.at[kind, m], y_dev,
            ),
        )

    def wait_slot(which, m):
        @pl.when(which == 0)
        def _():
            own_copy(in_hbm, m).wait()
            seq_copy(in_hbm, m).wait_recv()

            for is_sec, src in ((0, in_hbm), (1, cot_hbm)):
                @pl.when((m == 0) & (sec == is_sec))
                def _(src=src):
                    seq_copy(src, 1).start()

        @pl.when(which == 1)
        def _():
            hop_copy(yb, m).wait_recv()

    def positions(shape, dim):
        row = lax.broadcasted_iota(jnp.int32, shape, dim)
        block = row // span
        within = row % span
        half = jnp.where(block % 2 == 0, hi, 1 - hi)
        core = jnp.where(block < 2, lo, 1 - lo)
        return (half * 2 + core) * span + within

    def left_lanes():
        return lax.broadcasted_iota(jnp.int32, (1, LANES), 1) < hd

    def split_heads(value):
        left = left_lanes().astype(F32)
        return jnp.concatenate([value * left.astype(BF), value * (1.0 - left).astype(BF)], axis=0)

    def norm(resid, gain, shift):
        average = jnp.mean(resid, axis=-1, keepdims=True)
        centred = resid - average
        spread = jnp.mean(centred * centred, axis=-1, keepdims=True)
        scale = lax.rsqrt(spread + EPS)
        hat = centred * scale
        return hat, scale, hat * gain + shift

    def norm_back(grad, hat, scale, gain):
        dh = grad * gain
        return scale * (
            dh
            - jnp.mean(dh, axis=-1, keepdims=True)
            - hat * jnp.mean(dh * hat, axis=-1, keepdims=True)
        )

    def wup(j):
        return pool[4 * j:4 * j + 4].reshape(width, width)

    def vec(ref, part):
        return ref[0:1, part * width:(part + 1) * width].astype(F32)

    def add_bias_grad(row, value):
        bg[row] += jnp.sum(value, axis=0, keepdims=True)

    def turn_left_sides(m):
        r = mrows(m)
        lt[L_X, :, r] = ab[sec, r].T
        lt[L_N, :, r] = n_s[r].T
        lt[L_O, :, r] = o_s[r].T

    def left_copy(m):
        tall_half = 2 * tall
        return remote(
            lt.at[pl.ds(L_F, nff), pl.ds((1 - hi) * tall_half, tall_half), mrows(m)],
            lt_y.at[:, :, mrows(m)], lt_ss.at[m], lt_rs.at[m], y_dev,
        )

    def right_copy(m):
        return remote(rt.at[R_Z, mrows(m)], dz_y.at[mrows(m)], dz_ss.at[m], dz_rs.at[m], y_dev)


    def project(step, m):
        r = mrows(m)
        wait_slot(sec, m)

        @pl.when(step == 0)
        def _():
            weight_copies[0].wait()

        x = ab[sec, r]
        kv[m, 0, pl.ds(0, rows)] = dot_nn(x, wqkv[:, width:2 * width]).astype(BF)
        kv_copy(m, 0).start()
        kv[m, 1, pl.ds(0, rows)] = (
            dot_nn(x, wqkv[:, 2 * width:3 * width]) + vec(abias_ref, 1)
        ).astype(BF)
        kv_copy(m, 1).start()
        queries = (dot_nn(x, wqkv[:, 0:width]) + vec(abias_ref, 0)).astype(BF)
        q_s[r] = queries * (hd ** -0.5)

        @pl.when(step == 0)
        def _():
            for copy in weight_copies[1:3]:
                copy.wait()
            whole = pool.at[pl.ds(0, 4 * nff)]
            pltpu.make_async_copy(whole, whole, w_sem.at[3]).wait()

    def forward(m):
        r = mrows(m)
        kv_copy(m, 0).wait_recv()
        kv_copy(m, 1).wait_recv()
        key_bias = jnp.where(positions((1, keys), 1) < len_ref[2 * hi + m], 0.0, -1e30)
        lane = lax.broadcasted_iota(jnp.int32, (1, LANES), 1)
        stats = jnp.zeros((keys, LANES), F32)
        for p in range(pairs):
            cols = pl.ds(p * LANES, LANES)
            scores = dot_nt(split_heads(q_s[r, cols]), kv[m, 0, :, cols]) + key_bias
            top = jnp.max(scores, axis=1, keepdims=True)
            e = jnp.exp(scores - top)
            total = jnp.sum(e, axis=1, keepdims=True)
            stats = jnp.where(lane == p, top + jnp.log(total), stats)
            o = dot_nn(e.astype(BF), kv[m, 1, :, cols]) * (1.0 / total)
            o_s[r, cols] = jnp.where(left_lanes(), o[0:rows], o[rows:2 * rows]).astype(BF)
        lse[m] = stats.T[0:8]

        r1 = ab[sec, r].astype(F32) + dot_nn(o_s[r], wout[...]) + vec(obias_ref, 0)
        hat, scale, n1 = norm(r1, vec(gain_ref, 0), vec(shift_ref, 0))
        xh1[r] = hat.astype(BF)
        rs[r] = jnp.broadcast_to(scale, (rows, LANES))
        n_s[r] = n1.astype(BF)
        acc[...] = n1 + vec(obias_ref, 1)
        for j in range(nff):
            cols = pl.ds(j * width, width)
            u = dot_nn(n_s[r], wup(j)) + bup_ref[0:1, cols].astype(F32)
            phi = 0.5 + 0.5 * lax.erf(u * INV_SQRT_2)
            f = (u * phi).astype(BF)
            f_t = f.T
            for owner in range(quarter):
                for part in range(nff):
                    at = (owner * nff + part) * unit
                    lt[part, pl.ds((j * quarter + owner) * unit, unit), r] = f_t[at:at + unit]
            rt[R_U + j, r] = (phi + u * (jnp.exp(-0.5 * u * u) * INV_SQRT_2PI)).astype(BF)
            acc[...] += dot_nn(f, wdown[cols, :])
        hat, scale, result = norm(acc[...], vec(gain_ref, 1), vec(shift_ref, 1))
        xh2[r] = hat.astype(BF)
        rs[r] = jnp.where(left_lanes(), rs[r], scale)
        yb[r] = result.astype(BF)

        @pl.when(sec == 0)
        def _():
            hop_copy(yb, m).start()

        for copy in out_copies(0, yb, sout_hbm, m):
            copy.start()
        if with_sums:
            @pl.when(sec == 0)
            def _():
                left_copy(m).start()


        @pl.when(sec == 0)
        def _():
            turn_left_sides(m)


    def backward(m, serve):
        r = mrows(m)
        wait_slot(1 - sec, m)
        length = len_ref[2 * hi + m]
        row_scale = jnp.where((sec == 0) | (positions((rows, 1), 0) < length), 1.0, 0.0)
        dy = ab[1 - sec, r].astype(F32) * row_scale
        hat = xh2[r].astype(F32)
        add_bias_grad(9, dy * hat)
        add_bias_grad(11, dy)
        dr2 = norm_back(dy, hat, rs[r, hd:hd + 1], vec(gain_ref, 1))
        dz = dr2.astype(BF)
        rt[R_Z, r] = dz
        if with_sums:
            @pl.when(sec == 0)
            def _():
                right_copy(m).start()

        add_bias_grad(3, dz.astype(F32))
        acc[...] = dr2
        serve(0, 1)
        for j in range(nff):
            cols = pl.ds(j * width, width)
            du = (dot_nt(rt[R_Z, r], wdown[cols, :]) * rt[R_U + j, r].astype(F32)).astype(BF)
            rt[R_U + j, r] = du
            bg[4 + j] += jnp.sum(du.astype(F32), axis=0, keepdims=True)
            acc[...] += dot_nt(du, wup(j))
        serve(1, 3)
        dn1 = acc[...]
        hat = xh1[r].astype(F32)
        add_bias_grad(8, dn1 * hat)
        add_bias_grad(10, dn1)
        grad1 = norm_back(dn1, hat, rs[r, 0:1], vec(gain_ref, 0))
        dr1[...] = grad1
        da = grad1.astype(BF)
        rt[R_A, r] = da
        add_bias_grad(2, da.astype(F32))
        do_s[...] = dot_nt(da, wout[...]).astype(BF)
        serve(3, 5)
        key_bias = jnp.where(positions((keys, 1), 0) < length, 0.0, -1e30)

        def head_pair(group, index):
            p = group * half_pairs + index
            cols = pl.ds(p * LANES, LANES)
            kcols = pl.ds(index * LANES, LANES)
            vcols = pl.ds((half_pairs + index) * LANES, LANES)
            qq = split_heads(q_s[r, cols])
            dd = split_heads(do_s[:, cols])
            kp = kv[m, 0, :, cols]
            pt = jnp.exp(dot_nt(kp, qq) + key_bias - lse[m, p:p + 1])
            dv = dot_nn(pt.astype(BF), dd)
            dpt = dot_nt(kv[m, 1, :, cols], dd)
            sums = jnp.sum(pt * dpt, axis=0, keepdims=True)
            ds = (pt * (dpt - sums)).astype(BF)
            dk = dot_nn(ds, qq)
            dq_t = dot_tn(kp, ds)
            dq_pair = jnp.concatenate([dq_t[0:hd, 0:rows], dq_t[hd:2 * hd, rows:2 * rows]], axis=0)
            rt[R_P, r, cols] = (dq_pair.T * (hd ** -0.5)).astype(BF)
            dkv_own[group, :, kcols] = dk[0:rows]
            dkv_own[group, :, vcols] = dv[0:rows]
            dkv_send[group, :, kcols] = dk[rows:keys].astype(BF)
            dkv_send[group, :, vcols] = dv[rows:keys].astype(BF)

        for group in range(2):
            for index in range(half_pairs):
                head_pair(group, index)
            dkv_copy(m, group).start()
            if group == 0:
                serve(5, EARLY)
        dq = rt[R_P, r]
        add_bias_grad(0, dq.astype(F32))
        dr1[...] += dot_nt(dq, wqkv[:, 0:width])

    def input_grad(m):
        r = mrows(m)
        dx = dr1[...]
        part = width // 2
        for group in range(2):
            dkv_copy(m, group).wait_recv()
            both = (dkv_own[group] + dkv_recv[m, group].astype(F32)).astype(BF)
            for which in range(2):
                at = (1 + which) * width + group * part
                piece = both[:, which * part:(which + 1) * part]
                rt[R_P + 1 + which, r, group * part:(group + 1) * part] = piece
                dx = dx + dot_nt(piece, wqkv[:, at:at + part])
        local_out, remote_out = out_copies(0, yb, sout_hbm, m)
        local_out.wait()
        remote_out.wait_send()

        @pl.when(sec == 0)
        def _():
            hop_copy(yb, m).wait_send()

        yb[r] = dx.astype(BF)

        @pl.when(sec == 1)
        def _():
            hop_copy(yb, m).start()

        @pl.when((m == 0) & (sec == 1))
        def _():
            send_input_grad(m)

        for group in range(2):
            dkv_copy(m, group).wait_send()
        add_bias_grad(1, rt[R_P + 2, r].astype(F32))

    def send_input_grad(m):
        for copy in out_copies(1, yb, sgrad_hbm, m):
            copy.start()

    def send_late_grads():
        @pl.when(sec == 0)
        def _():
            send_input_grad(0)

        send_input_grad(1)


    if with_sums:
        block = count * unit
        two = 2 * unit

        other_z = 4

        def of_down(k):
            return (k == 0) | ((k % 2 == 1) & (k >= 3) & (k < OUT))

        def is_z_first(k):
            return (k == 0) | ((sec == 1) & (k == other_z))

        def is_down(k):
            return (sec == 0) & of_down(k) & (k > 0)

        def slot_of(k, half):
            return jnp.where(k < 4, 4 * nff + 2 * k, 2 * k - 8) + half

        def core_copy(k, i, half):
            return remote(
                core_src.at[k % 2, i], pool.at[slot_of(k, half)],
                core_ss.at[k % 2, i], core_rs.at[k % 4, i], core_dev,
            )

        def y_copy(k, i):
            rows_of = pl.ds(pl.multiple_of(jnp.where(z < count // 2, 1 - i, i) * two, two), two)
            first = jnp.where(k < 4, k - 1, jnp.where(k < QKV, k // 2, k - 4))
            second = k - 1 - jnp.where(k > 4, 1, 0)
            slot = jnp.where(sec == 0, first, second)
            return rows_of, y_buf.at[slot, i], remote(
                pool.at[slot_of(k, 1 - hi), rows_of], y_buf.at[slot, i],
                y_ss.at[slot, i], y_rs.at[slot, i], y_dev,
            )

        def turn_copy(k):
            i = jnp.where(k == 0, 0, 1)
            return remote(turn_src.at[i], turn_buf.at[i], turn_ss.at[i], turn_rs.at[i], y_dev)

        def z_first_jobs(k):
            return ((k, hi), (CHUNKS + jnp.where(k == 0, 0, 1), 1 - hi))

        def piece(k, half, target):
            return pool.at[slot_of(k, half), pl.ds(pl.multiple_of(target * unit, unit), unit)]

        def up_copy(job, k, half, target):
            i = target - 1
            return remote(
                piece(k, half, target), land.at[job, i], z_ss.at[job, i], z_rs.at[job, i],
                z_dev(jnp.minimum(z + 1, count - 1)),
            )

        def down_copy(job, k, half, target):
            i = (target + count - 1) % LANDINGS
            return remote(
                piece(k, half, target), land.at[job, i], z_ss.at[job, target], z_rs.at[job, i],
                z_dev(jnp.maximum(z - 1, 0)),
            )

        def add_to(ref, landed):
            ref[...] = (ref[...].astype(F32) + landed[...].astype(F32)).astype(BF)

        def hop(number, job, k, half):
            @pl.when(z == number - 1)
            def _():
                for target in range(count - 1, number - 1, -1):
                    copy = up_copy(job, k, half, target)
                    if number > 1:
                        copy.wait_recv()
                        add_to(piece(k, half, target), land.at[job, target - 1])
                    copy.start()

            @pl.when(z == count - number)
            def _():
                for target in range(0, count - number):
                    copy = down_copy(job, k, half, target)
                    if number > 1:
                        copy.wait_recv()
                        add_to(piece(k, half, target), land.at[job, (target + count - 1) % LANDINGS])
                    copy.start()

        def arrive(job, k, half):
            out[k] = piece(k, half, z)[...].astype(F32)

            @pl.when(z > 0)
            def _():
                up_copy(job, k, half, jnp.maximum(z, 1)).wait_recv()
                out[k] += land[job, jnp.maximum(z, 1) - 1].astype(F32)

            @pl.when(z < count - 1)
            def _():
                down_copy(job, k, half, z).wait_recv()
                out[k] += land[job, (z + count - 1) % LANDINGS].astype(F32)

        def product(k, number):
            left = jnp.where(of_down(k), L_F + k // 2, L_N)
            left = jnp.where(k < OUT, left, jnp.where(k == OUT, L_O, L_X))
            right = jnp.where(of_down(k), R_Z, R_U + k // 2)
            right = jnp.where(k < OUT, right, jnp.where(k == OUT, R_A, R_P + k - QKV))
            base = pl.multiple_of(number * block, block)
            return dot_nn(lt[left, pl.ds(base, block), :], rt[right])

        def down_product(k, core):
            part = k // 2
            own_rows = pl.ds(pl.multiple_of((hi * 2 + core) * block, block), block)
            rows_y = pl.ds(pl.multiple_of(core * block, block), block)
            return dot_nn(lt[L_F + part, own_rows, :], rt[R_Z]) + dot_nn(
                lt_y[part, rows_y, :], dz_y[...]
            )

        def for_core(k):
            @pl.when((k >= 2) & is_down(k - 2))
            def _():
                core_copy(k - 2, 0, hi).wait_send()

            @pl.when((k >= 2) & jnp.logical_not(is_down(k - 2)))
            def _():
                for half in range(2):
                    core_copy(k - 2, half, half).wait_send()

            @pl.when((sec == 0) & (k == 3))
            def _():
                for m in range(MICRO):
                    left_copy(m).wait_recv()
                    right_copy(m).wait_recv()

            @pl.when(is_down(k))
            def _():
                core_src[k % 2, 0] = down_product(k, 1 - lo).astype(BF)
                core_copy(k, 0, hi).start()

            @pl.when(jnp.logical_not(is_down(k)))
            def _():
                for half in range(2):
                    core_src[k % 2, half] = product(k, half * 2 + 1 - lo).astype(BF)
                    core_copy(k, half, half).start()

        def chip_sum(k):
            @pl.when(is_down(k))
            def _():
                core_copy(k, 0, hi).wait_recv()
                slot = slot_of(k, hi)
                pool[slot] = (down_product(k, lo) + pool[slot].astype(F32)).astype(BF)
                hop(1, k, k, hi)

            @pl.when(jnp.logical_not(is_down(k)))
            def _():
                for half in range(2):
                    core_copy(k, half, half).wait_recv()
                    slot = slot_of(k, half)
                    pool[slot] = (product(k, half * 2 + lo) + pool[slot].astype(F32)).astype(BF)

                @pl.when(is_z_first(k))
                def _():
                    for job, half in z_first_jobs(k):
                        hop(1, job, k, half)

                @pl.when(jnp.logical_not(is_z_first(k)))
                def _():
                    for i in range(2):
                        y_copy(k, i)[2].start()

        def from_y(k):
            for i in range(2):
                rows_of, landed, copy = y_copy(k, i)
                copy.wait_recv()
                add_to(pool.at[slot_of(k, hi), rows_of], landed)

                @pl.when(z == 0)
                def _(i=i):
                    for target in ((3, 2), (1,))[i]:
                        up_copy(k, k, hi, target).start()

                @pl.when(z == count - 1)
                def _(i=i):
                    for target in ((0, 1), (2,))[i]:
                        down_copy(k, k, hi, target).start()

        def finished(k):
            arrive(k, k, hi)
            part_copy(k).start()

        def sent(job, k, half):
            for target in range(count):
                if target > 0:
                    @pl.when(target > z)
                    def _(target=target):
                        up_copy(job, k, half, target).wait_send()

                if target < count - 1:
                    @pl.when(target < z)
                    def _(target=target):
                        down_copy(job, k, half, target).wait_send()

        def drain(k):
            sent(k, k, hi)

            @pl.when(jnp.logical_not(is_z_first(k) | is_down(k)))
            def _():
                for i in range(2):
                    y_copy(k, i)[2].wait_send()

        def part_copy(k):
            return pltpu.make_async_copy(out.at[k], out_hbm.at[k], part_sem)

        def bias_core():
            return remote(b_src.at[0], b_core, bc_ss.at[0], bc_rs.at[0], core_dev)

        def bias_y():
            return remote(b_src.at[1], b_y, bc_ss.at[1], bc_rs.at[1], y_dev)

        def bias_z(by):
            return remote(
                b_src.at[2], b_z.at[by - 1], bz_ss.at[by - 1], bz_rs.at[by - 1],
                z_dev((z + by) % count),
            )

        def sum_step(t):
            @pl.when(t < CHUNKS)
            def _():
                for_core(t)

            @pl.when(((t >= 2) & (t <= CHUNKS)) | (t == 0))
            def _():
                chip_sum(jnp.maximum(t - 1, 0))

            def at(tables, action):
                k = -1
                for section, table in enumerate(tables):
                    for when, chunk in table.items():
                        k = jnp.where((sec == section) & (t == when), chunk, k)

                @pl.when(k >= 0)
                def _():
                    action(k)

            def both_halves(number, k):
                for job, half in z_first_jobs(k):
                    hop(number, job, k, half)

            def turn(k):
                stays, goes = z_first_jobs(k)
                arrive(goes[0], k, goes[1])
                turn_src[jnp.where(k == 0, 0, 1)] = out[k].astype(BF)
                turn_copy(k).start()
                arrive(stays[0], k, stays[1])

            at(FROM_Y, from_y)
            at(THIRD, lambda k: hop(3, k, k, hi))
            at(SECOND, lambda k: hop(2, k, k, hi))

            at(Z_THIRD, lambda k: both_halves(3, k))
            at(Z_SECOND, lambda k: both_halves(2, k))

            at(ARRIVE, finished)

            @pl.when((t >= 14) & (t < 14 + LAST))
            def _():
                drain(t - 14)

            @pl.when(t == CHUNKS + 1)
            def _():
                send_late_grads()

            at(TURN, turn)

            @pl.when(t == EARLY)
            def _():
                b_src[0] = bg[...]
                bias_core().start()

            @pl.when(t == EARLY + 1)
            def _():
                bias_core().wait_recv()
                b_src[1] = b_src[0] + b_core[...]
                bias_y().start()

            @pl.when(t == 16)
            def _():
                bias_y().wait_recv()
                b_src[2] = b_src[1] + b_y[...]
                for by in range(1, count):
                    bias_z(by).start()

    def one_step(step, carry):
        first = sec == 0

        def among(*steps):
            hit = step == steps[0]
            for value in steps[1:]:
                hit = hit | (step == value)
            return hit

        late_forward = ((step == 3) & first) | ((step == 4) & jnp.logical_not(first))
        early_backward = ((step == 4) & first) | ((step == 3) & jnp.logical_not(first))
        m = jnp.where(among(2, 6, 7) | late_forward, 1, 0)

        def serve(start, stop):
            if with_sums:
                @pl.when((step == 6) & first)
                def _():
                    def body(t, c):
                        sum_step(t)
                        return c

                    lax.fori_loop(start, stop, body, 0)

        @pl.when(among(0, 2))
        def _():
            project(step, m)

        @pl.when((step == 1) | late_forward)
        def _():
            forward(m)

        @pl.when((step == 6) | early_backward)
        def _():
            backward(m, serve)

        @pl.when(among(5, 7))
        def _():
            input_grad(m)

        return carry

    lax.fori_loop(0, 8, one_step, 0)

    @pl.when(sec == 1)
    def _():
        for m in range(MICRO):
            turn_left_sides(m)

    if not with_sums:
        send_late_grads()

    if with_sums:
        def rest(t, carry):
            sum_step(t)
            return carry

        lax.fori_loop(jnp.where(sec == 0, EARLY, 0), STEPS, rest, 0)

        for k in range(LAST, CHUNKS):
            finished(k)
        for i, k in enumerate((0, other_z)):
            @pl.when((sec == 1) | (i == 0))
            def _(i=i, k=k):
                turn_copy(k).wait_recv()
                out[k] += turn_buf[i].astype(F32)
                part_copy(k).start()

        total = b_src[2]
        for by in range(1, count):
            bias_z(by).wait_recv()
            total = total + b_z[by - 1]
        bg_out[...] = total
        bias_core().wait_send()
        bias_y().wait_send()
        for by in range(1, count):
            bias_z(by).wait_send()

        for k in range(LAST, CHUNKS):
            drain(k)
        pltpu.make_async_copy(out, out_hbm, part_sem).wait()
        for i, k in enumerate((0, other_z)):
            @pl.when((sec == 1) | (i == 0))
            def _(i=i, k=k):
                sent(CHUNKS + i, k, 1 - hi)
                turn_copy(k).wait_send()
        for k in (CHUNKS - 2, CHUNKS - 1):
            for half in range(2):
                core_copy(k, half, half).wait_send()

        @pl.when(sec == 0)
        def _():
            for m in range(MICRO):
                left_copy(m).wait_send()
                right_copy(m).wait_send()

    for m in range(MICRO):
        seq_copy(in_hbm, m).wait_send()
        for part in range(2):
            kv_copy(m, part).wait_send()
        out_copies(0, yb, sout_hbm, m)[1].wait_recv()
        local_out, remote_out = out_copies(1, yb, sgrad_hbm, m)
        local_out.wait()
        remote_out.wait()

        @pl.when(sec == 1)
        def _():
            hop_copy(yb, m).wait_send()


def run_train(args, with_sums):
    (inputs, cotangent, lengths, w_qkv, attn_bias, w_out, out_bias, w_up, bias_up, w_down,
     norm_gain, norm_bias) = args
    tables, span, width = inputs.shape
    ff = w_up.shape[2]
    rows = 2 * span
    total = MICRO * rows
    keys = 2 * rows
    count = lax.axis_size("dp")
    unit = width // 16
    block = count * unit
    tall = width // 4
    any_spec = pl.BlockSpec(memory_space=pl.ANY)
    vmem = pl.BlockSpec(memory_space=pltpu.VMEM)
    smem = pl.BlockSpec(memory_space=pltpu.SMEM)
    dma = pltpu.SemaphoreType.DMA
    shape = jax.ShapeDtypeStruct
    stacks = (
        ((L_COUNT, width, total), BF),
        ((R_COUNT, total, width), BF),
        ((12, 1, width), F32),
    )
    if with_sums:
        results = (((CHUNKS, unit, width), F32), ((12, 1, width), F32))
    else:
        results = stacks
    scratch = [
        pltpu.VMEM((2, total, width), BF),
        pltpu.VMEM((width, 3 * width), BF),
        pltpu.VMEM((width, width), BF),
        pltpu.VMEM((ff // tall + (8 if with_sums else 0), tall, width), BF),
        pltpu.VMEM((ff, width), BF),
        pltpu.VMEM((total, width), BF),
        pltpu.VMEM((MICRO, 2, keys, width), BF),
        pltpu.VMEM((MICRO, 8, keys), F32),
        pltpu.VMEM((total, width), BF),
        pltpu.VMEM((total, width), BF),
        pltpu.VMEM((total, width), BF),
        pltpu.VMEM((total, width), BF),
        pltpu.VMEM((total, LANES), F32),
        pltpu.VMEM((rows, width), F32),
        pltpu.VMEM((rows, width), F32),
        pltpu.VMEM((rows, width), BF),
        pltpu.VMEM((2, rows, width), F32),
        pltpu.VMEM((2, rows, width), BF),
        pltpu.VMEM((MICRO, 2, rows, width), BF),
        pltpu.VMEM((total, width), BF),
        dma((4,)), dma((MICRO,)), dma((MICRO,)), dma((MICRO,)), dma((MICRO,)), dma((MICRO,)),
        dma((MICRO, 2)), dma((MICRO, 2)), dma((MICRO, 2)), dma((MICRO, 2)),
        dma((2, MICRO)), dma((2, MICRO)), dma((2, MICRO)),
    ]
    if with_sums:
        scratch += [pltpu.VMEM(dims, kind) for dims, kind in stacks]
        scratch += [
            pltpu.VMEM((CHUNKS, unit, width), F32),
            pltpu.VMEM((ff // width, 2 * block, total), BF),
            pltpu.VMEM((total, width), BF),
            pltpu.VMEM((2, 2, block, width), BF),
            pltpu.VMEM((Y_SLOTS, 2, 2 * unit, width), BF),
            pltpu.VMEM((CHUNKS + Z_FIRST, LANDINGS, unit, width), BF),
            pltpu.VMEM((Z_FIRST, unit, width), BF),
            pltpu.VMEM((Z_FIRST, unit, width), BF),
            pltpu.VMEM((3, 12, 1, width), F32),
            pltpu.VMEM((12, 1, width), F32),
            pltpu.VMEM((12, 1, width), F32),
            pltpu.VMEM((count - 1, 12, 1, width), F32),
            dma((2, 2)), dma((4, 2)), dma((Y_SLOTS, 2)), dma((Y_SLOTS, 2)),
            dma((CHUNKS + Z_FIRST, count - 1)), dma((CHUNKS + Z_FIRST, LANDINGS)),
            dma((Z_FIRST,)), dma((Z_FIRST,)),
            dma((2,)), dma((2,)), dma((count - 1,)), dma((count - 1,)), dma,
            dma((MICRO,)), dma((MICRO,)), dma((MICRO,)), dma((MICRO,)),
        ]
    return pl.pallas_call(
        functools.partial(train_kernel, with_sums),
        name="train",
        out_shape=(shape((tables, span, width), BF), shape((tables, span, width), BF))
        + tuple(shape(dims, kind) for dims, kind in results),
        in_specs=[smem] + [any_spec] * 6 + [vmem] * 5,
        out_specs=(any_spec, any_spec)
        + ((any_spec, vmem) if with_sums else (vmem,) * len(results)),
        scratch_shapes=scratch,
        compiler_params=pltpu.CompilerParams(
            collective_id=0, has_side_effects=True, vmem_limit_bytes=VMEM_LIMIT
        ),
    )(lengths, inputs, cotangent, w_qkv, w_out, w_up, w_down,
      attn_bias, out_bias, bias_up, norm_gain, norm_bias)


def grads_by_scatter(lt, rt, bg, ff):
    width = lt.shape[1]
    parts = ff // width

    def scatter(full):
        return lax.psum_scatter(
            full.astype(BF), ("seq", "dp"), scatter_dimension=0, tiled=True
        ).astype(F32)

    left_f = lt[:parts].reshape(parts, 4, 4, width // 16, -1).transpose(1, 2, 0, 3, 4)
    down = scatter(dot_nn(left_f.reshape(ff, -1), rt[R_Z]))
    up = scatter(jnp.concatenate([dot_nn(lt[L_N], rt[R_U + j]) for j in range(parts)], axis=1))
    wout = scatter(dot_nn(lt[L_O], rt[R_A]))
    qkv = scatter(jnp.concatenate([dot_nn(lt[L_X], rt[R_P + j]) for j in range(3)], axis=1))
    return qkv, wout, up, down, lax.psum(bg, ("seq", "dp"))


def finish_kernel(
    sout, sgrad, grads, sums_hbm,
    sout_ref, sgrad_ref, qkv_ref, abias_ref, wout_ref, obias_ref, up_ref, bup_ref, down_ref,
    gain_ref, shift_ref,
    kept, low, wide_grad, parts, sums, sem,
):
    unit, width = grads.shape[1:]
    size = abias_ref.shape[1]

    def copy(i, src, dst):
        started = pltpu.make_async_copy(src, dst, sem.at[i])
        started.start()
        return started

    sums_in = copy(0, sums_hbm, sums)
    grad_in = copy(1, sgrad, low)
    out_in = copy(2, sout, kept)
    parts_in = [copy(6 + CHUNKS + k, grads.at[k], parts.at[k]) for k in range(CHUNKS)]
    grad_in.wait()
    wide_grad[...] = low[...].astype(F32)
    copies = [copy(4, wide_grad, sgrad_ref.at[0])]
    out_in.wait()
    copies.append(copy(5, kept, sout_ref.at[0]))
    for k in range(CHUNKS):
        parts_in[k].wait()
        if k in (0, 3, 5, 7):
            dst = down_ref.at[0, pl.ds(k // 2 * unit, unit), :]
        elif k < OUT:
            dst = up_ref.at[0, :, pl.ds(k // 2 * width, width)]
        elif k == OUT:
            dst = wout_ref.at[0]
        else:
            dst = qkv_ref.at[0, :, pl.ds((k - QKV) * width, width)]
        copies.append(copy(6 + k, parts.at[k], dst))
    sums_in.wait()
    index = lax.axis_index("seq") * lax.axis_size("dp") + lax.axis_index("dp")
    whole = width // size
    pairs = [jnp.where(index < whole, sums[row], sums[row + 1]) for row in (0, 2, 8, 10)]
    block = jnp.concatenate(pairs + pairs, axis=0)
    block = pltpu.roll(block, (width - (index % whole) * size) % width, axis=1)
    for row, ref in enumerate((abias_ref, obias_ref, gain_ref, shift_ref)):
        ref[...] = block[row:row + 1, 0:size]
    wide = 2 * size
    per = width // wide
    rows = sums[4]
    for row in range(1, 4):
        rows = jnp.where(index // per == row, sums[4 + row], rows)
    rows = pltpu.roll(
        jnp.concatenate([rows] * 8, axis=0), (width - (index % per) * wide) % width, axis=1
    )
    bup_ref[...] = rows[0:1, 0:wide]
    for started in copies:
        started.wait()


def run_finish(sout, sgrad, grads, sums):
    unit, width = grads.shape[1:]
    size = width // 8
    vmem = pl.BlockSpec(memory_space=pltpu.VMEM)
    any_spec = pl.BlockSpec(memory_space=pl.ANY)
    shape = jax.ShapeDtypeStruct
    return pl.pallas_call(
        finish_kernel,
        name="finish",
        out_shape=(
            shape((1,) + sout.shape, BF),
            shape((1,) + sgrad.shape, F32),
            shape((1, unit, 3 * width), F32),
            shape((1, size), F32),
            shape((1, unit, width), F32),
            shape((1, size), F32),
            shape((1, unit, 4 * width), F32),
            shape((1, 2 * size), F32),
            shape((1, 4 * unit, width), F32),
            shape((1, size), F32),
            shape((1, size), F32),
        ),
        in_specs=[any_spec] * 4,
        out_specs=(any_spec, any_spec, any_spec, vmem, any_spec, vmem, any_spec, vmem, any_spec,
                   vmem, vmem),
        scratch_shapes=[
            pltpu.VMEM(sout.shape, BF),
            pltpu.VMEM(sgrad.shape, BF),
            pltpu.VMEM(sgrad.shape, F32),
            pltpu.VMEM(grads.shape, F32),
            pltpu.VMEM(sums.shape, F32),
            pltpu.SemaphoreType.DMA((6 + 2 * CHUNKS,)),
        ],
        compiler_params=pltpu.CompilerParams(vmem_limit_bytes=VMEM_LIMIT),
    )(sout, sgrad, grads, sums)


def local(*args):
    if lax.axis_size("dp") == 4:
        sout, sgrad, out, sums = run_train(args, True)
        return run_finish(sout, sgrad, out, sums)
    sout, sgrad, lt, rt, bg = run_train(args, False)
    width = lt.shape[1]
    ff = args[7].shape[2]
    index = lax.axis_index("seq") * lax.axis_size("dp") + lax.axis_index("dp")
    count = lax.axis_size("seq") * lax.axis_size("dp")
    qkv, wout, up, down, sums = grads_by_scatter(lt, rt, bg, ff)
    sums = sums.reshape(-1)

    def piece(start, rows):
        part = sums[start * width:(start + rows) * width]
        size = rows * width // count
        return lax.dynamic_slice_in_dim(part, index * size, size, 0)[None]

    return (
        sout[None],
        sgrad.astype(F32)[None],
        qkv[None],
        piece(0, 2),
        wout[None],
        piece(2, 2),
        up[None],
        piece(4, 4),
        down[None],
        piece(8, 2),
        piece(10, 2),
    )


def solution(mesh):
    return jax.shard_map(
        local,
        mesh=mesh,
        in_specs=(
            P("dp", "seq", None),
            P("dp", "seq", None),
            P("dp"),
            P("section", None, None),
            P("section", None),
            P("section", None, None),
            P("section", None),
            P("section", None, None),
            P("section", None),
            P("section", None, None),
            P("section", None),
            P("section", None),
        ),
        out_specs=(
            P("section", "dp", "seq", None),
            P("section", "dp", "seq", None),
            P("section", ("seq", "dp"), None),
            P("section", ("seq", "dp")),
            P("section", ("seq", "dp"), None),
            P("section", ("seq", "dp")),
            P("section", ("seq", "dp"), None),
            P("section", ("seq", "dp")),
            P("section", ("seq", "dp"), None),
            P("section", ("seq", "dp")),
            P("section", ("seq", "dp")),
        ),
        check_vma=False,
    )
```

```python
import functools

import jax
import jax.numpy as jnp
from jax import lax
from jax.experimental import pallas as pl
from jax.experimental.pallas import tpu as pltpu
from jax.sharding import PartitionSpec as P

H = 12
MICRO = 2
EPS = 1e-12
MESH = pl.DeviceIdType.MESH
BF = jnp.bfloat16
F32 = jnp.float32
LANES = 128
INV_SQRT_2PI = 0.3989422804014327
INV_SQRT_2 = 0.7071067811865476
L_F, L_N, L_O, L_X, L_COUNT = 0, 4, 5, 6, 7
R_P, R_A, R_U, R_Z, R_COUNT = 0, 3, 4, 8, 9
CHUNKS = 12
OUT = 8
QKV = 9
EARLY = 6
FROM_Y = (
    {5: 1, 7: 2, 10: 4, 13: 6, 15: 8, 16: 9, 17: 10, 19: 11},
    {5: 1, 6: 2, 7: 3, 9: 5, 10: 6, 11: 7, 12: 8, 13: 9, 14: 10, 15: 11},
)
SECOND = (
    {8: 3, 10: 1, 11: 5, 12: 7, 13: 2, 14: 4, 15: 6, 17: 8, 18: 9, 19: 10, 20: 11},
    {7: 1, 8: 2, 9: 3, 10: 5, 11: 6, 12: 7, 13: 8, 14: 9, 15: 10, 16: 11},
)
THIRD = tuple(
    {t + lag: k for t, k in table.items()} for lag, table in zip((2, 1), SECOND)
)
ARRIVE = (
    {14: 3, 15: 1, 16: 5, 17: 7, 18: 2, 19: 4, 20: 6, 21: 8},
    {11: 1, 12: 2, 13: 3, 15: 5, 16: 6, 17: 7, 18: 8},
)
Z_FIRST = 2
Z_SECOND = ({5: 0}, {6: 0, 9: 4})
Z_THIRD = ({9: 0}, {8: 0, 11: 4})
TURN = ({14: 0}, {13: 0, 14: 4})
LAST = QKV
STEPS = 23
LANDINGS = 5
Y_SLOTS = 10
VMEM_LIMIT = 127 * 2 ** 19


def dot_nn(a, b):
    return lax.dot_general(a, b, (((1,), (0,)), ((), ())), preferred_element_type=F32)


def dot_nt(a, b):
    return lax.dot_general(a, b, (((1,), (1,)), ((), ())), preferred_element_type=F32)


def dot_tn(a, b):
    return lax.dot_general(a, b, (((0,), (0,)), ((), ())), preferred_element_type=F32)


def train_kernel(with_sums, *refs):
    refs = iter(refs)

    def take(number):
        return [next(refs) for _ in range(number)]

    (len_ref, in_hbm, cot_hbm, wqkv_hbm, wout_hbm, wup_hbm, wdown_hbm,
     abias_ref, obias_ref, bup_ref, gain_ref, shift_ref) = take(12)
    sout_hbm, sgrad_hbm = take(2)
    if with_sums:
        out_hbm, bg_out = take(2)
    else:
        lt, rt, bg = take(3)
    (ab, wqkv, wout, pool, wdown, q_s, kv, lse, o_s, n_s, xh1, xh2, rs, dr1, acc, do_s,
     dkv_own, dkv_send, dkv_recv, yb) = take(20)
    (w_sem, loc_sem, ex_send, ex_recv, hop_send, hop_recv, kv_ss, kv_rs, dk_ss, dk_rs,
     out_loc, out_ss, out_rs) = take(13)
    if with_sums:
        (lt, rt, bg, out, lt_y, dz_y, core_src, y_buf, land, turn_src, turn_buf,
         b_src, b_core, b_y, b_z) = take(15)
        (core_ss, core_rs, y_ss, y_rs, z_ss, z_rs, turn_ss, turn_rs,
         bc_ss, bc_rs, bz_ss, bz_rs, part_sem, lt_ss, lt_rs, dz_ss, dz_rs) = take(17)

    width = wqkv.shape[0]
    ff = wdown.shape[0]
    span = in_hbm.shape[1]
    rows = 2 * span
    keys = 2 * rows
    hd = width // H
    pairs = H // 2
    half_pairs = H // 4
    nff = ff // width
    quarter = 4
    unit = width // 16
    sec = lax.axis_index("section")
    seq = lax.axis_index("seq")
    z = lax.axis_index("dp")
    count = lax.axis_size("dp")
    hi = seq // 2
    lo = seq % 2
    core_dev = (sec, hi * 2 + 1 - lo, z)
    y_dev = (sec, (1 - hi) * 2 + lo, z)
    x_dev = (1 - sec, seq, z)

    def z_dev(index):
        return (sec, seq, index)

    def remote(src, dst, send, recv, dev):
        return pltpu.make_async_remote_copy(
            src_ref=src, dst_ref=dst, send_sem=send, recv_sem=recv,
            device_id=dev, device_id_type=MESH,
        )

    weight_copies = [
        pltpu.make_async_copy(src.at[0], dst, w_sem.at[i])
        for i, (src, dst) in enumerate(((wqkv_hbm, wqkv), (wout_hbm, wout), (wdown_hbm, wdown)))
    ]
    tall = width // 4
    for j in range(nff):
        for part in range(4):
            weight_copies.append(
                pltpu.make_async_copy(
                    wup_hbm.at[0, pl.ds(part * tall, tall), pl.ds(j * width, width)],
                    pool.at[j * 4 + part],
                    w_sem.at[3],
                )
            )
    for copy in weight_copies:
        copy.start()

    partners = [core_dev, y_dev, x_dev]
    if with_sums:
        partners += [z_dev((z + by) % count) for by in range(1, count)]
    barrier = pltpu.get_barrier_semaphore()
    for dev in partners:
        pl.semaphore_signal(barrier, inc=1, device_id=dev, device_id_type=MESH)
    pl.semaphore_wait(barrier, len(partners))

    def mrows(m):
        return pl.ds(pl.multiple_of(m * rows, rows), rows)

    def own_copy(src, m):
        return pltpu.make_async_copy(
            src.at[2 * hi + m], ab.at[0, pl.ds(m * rows, span)], loc_sem.at[m]
        )

    def seq_copy(src, m):
        return remote(
            src.at[2 * (1 - hi) + m], ab.at[0, pl.ds(m * rows + span, span)],
            ex_send.at[m], ex_recv.at[m], y_dev,
        )

    for is_sec, src in ((0, in_hbm), (1, cot_hbm)):
        @pl.when(sec == is_sec)
        def _(src=src):
            seq_copy(src, 0).start()
            for m in range(MICRO):
                own_copy(src, m).start()

    bg[...] = jnp.zeros_like(bg)

    def part_rows(m, base, size):
        return pl.ds(pl.multiple_of(m * rows + base, size), size)

    def hop_copy(m, part):
        place = part_rows(m, part * span, span)
        return remote(
            yb.at[place], ab.at[1, place], hop_send.at[m, part], hop_recv.at[m, part], x_dev
        )

    def kv_copy(m, part):
        return remote(
            kv.at[m, part, pl.ds(0, rows)], kv.at[m, part, pl.ds(rows, rows)],
            kv_ss.at[m, part], kv_rs.at[m, part], core_dev,
        )

    def dkv_copy(m, group):
        return remote(
            dkv_send.at[group], dkv_recv.at[m, group],
            dk_ss.at[m, group], dk_rs.at[m, group], core_dev,
        )

    def out_copies(kind, src, dst, m):
        table = 2 * hi + m
        base = m * rows
        return (
            pltpu.make_async_copy(src.at[pl.ds(base, span)], dst.at[table], out_loc.at[kind, m]),
            remote(
                src.at[pl.ds(base + span, span)], dst.at[table],
                out_ss.at[kind, m], out_rs.at[kind, m], y_dev,
            ),
        )

    def wait_slot(which, m):
        @pl.when(which == 0)
        def _():
            own_copy(in_hbm, m).wait()
            seq_copy(in_hbm, m).wait_recv()

            for is_sec, src in ((0, in_hbm), (1, cot_hbm)):
                @pl.when((m == 0) & (sec == is_sec))
                def _(src=src):
                    seq_copy(src, 1).start()

        @pl.when(which == 1)
        def _():
            for part in range(2):
                hop_copy(m, part).wait_recv()

    def positions(shape, dim):
        row = lax.broadcasted_iota(jnp.int32, shape, dim)
        block = row // span
        within = row % span
        half = jnp.where(block % 2 == 0, hi, 1 - hi)
        core = jnp.where(block < 2, lo, 1 - lo)
        return (half * 2 + core) * span + within

    def left_lanes():
        return lax.broadcasted_iota(jnp.int32, (1, LANES), 1) < hd

    def split_heads(value):
        left = left_lanes().astype(F32)
        return jnp.concatenate([value * left.astype(BF), value * (1.0 - left).astype(BF)], axis=0)

    def norm(resid, gain, shift):
        average = jnp.mean(resid, axis=-1, keepdims=True)
        centred = resid - average
        spread = jnp.mean(centred * centred, axis=-1, keepdims=True)
        scale = lax.rsqrt(spread + EPS)
        hat = centred * scale
        return hat, scale, hat * gain + shift

    def norm_back(grad, hat, scale, gain):
        dh = grad * gain
        return scale * (
            dh
            - jnp.mean(dh, axis=-1, keepdims=True)
            - hat * jnp.mean(dh * hat, axis=-1, keepdims=True)
        )

    def wup(j):
        return pool[4 * j:4 * j + 4].reshape(width, width)

    def vec(ref, part):
        return ref[0:1, part * width:(part + 1) * width].astype(F32)

    def add_bias_grad(row, value):
        bg[row] += jnp.sum(value, axis=0, keepdims=True)

    def turn_left_sides(m):
        r = mrows(m)
        lt[L_X, :, r] = ab[sec, r].T
        lt[L_N, :, r] = n_s[r].T
        lt[L_O, :, r] = o_s[r].T

    def left_copy(m):
        tall_half = 2 * tall
        return remote(
            lt.at[pl.ds(L_F, nff), pl.ds((1 - hi) * tall_half, tall_half), mrows(m)],
            lt_y.at[:, :, mrows(m)], lt_ss.at[m], lt_rs.at[m], y_dev,
        )

    def right_copy(m):
        return remote(rt.at[R_Z, mrows(m)], dz_y.at[mrows(m)], dz_ss.at[m], dz_rs.at[m], y_dev)


    def project(step, m):
        r = mrows(m)
        wait_slot(sec, m)

        @pl.when(step == 0)
        def _():
            weight_copies[0].wait()

        x = ab[sec, r]
        kv[m, 0, pl.ds(0, rows)] = dot_nn(x, wqkv[:, width:2 * width]).astype(BF)
        kv_copy(m, 0).start()
        kv[m, 1, pl.ds(0, rows)] = (
            dot_nn(x, wqkv[:, 2 * width:3 * width]) + vec(abias_ref, 1)
        ).astype(BF)
        kv_copy(m, 1).start()
        queries = (dot_nn(x, wqkv[:, 0:width]) + vec(abias_ref, 0)).astype(BF)
        q_s[r] = queries * (hd ** -0.5)

        @pl.when(step == 0)
        def _():
            for copy in weight_copies[1:3]:
                copy.wait()
            whole = pool.at[pl.ds(0, 4 * nff)]
            pltpu.make_async_copy(whole, whole, w_sem.at[3]).wait()

    def forward(m):
        r = mrows(m)
        kv_copy(m, 0).wait_recv()
        kv_copy(m, 1).wait_recv()
        key_bias = jnp.where(positions((1, keys), 1) < len_ref[2 * hi + m], 0.0, -1e30)
        lane = lax.broadcasted_iota(jnp.int32, (1, LANES), 1)
        stats = jnp.zeros((keys, LANES), F32)
        for p in range(pairs):
            cols = pl.ds(p * LANES, LANES)
            scores = dot_nt(split_heads(q_s[r, cols]), kv[m, 0, :, cols]) + key_bias
            top = jnp.max(scores, axis=1, keepdims=True)
            e = jnp.exp(scores - top)
            total = jnp.sum(e, axis=1, keepdims=True)
            stats = jnp.where(lane == p, top + jnp.log(total), stats)
            o = dot_nn(e.astype(BF), kv[m, 1, :, cols]) * (1.0 / total)
            o_s[r, cols] = jnp.where(left_lanes(), o[0:rows], o[rows:2 * rows]).astype(BF)
        lse[m] = stats.T[0:8]

        r1 = ab[sec, r].astype(F32) + dot_nn(o_s[r], wout[...]) + vec(obias_ref, 0)
        hat, scale, n1 = norm(r1, vec(gain_ref, 0), vec(shift_ref, 0))
        xh1[r] = hat.astype(BF)
        rs[r] = jnp.broadcast_to(scale, (rows, LANES))
        n_s[r] = n1.astype(BF)
        acc[...] = n1 + vec(obias_ref, 1)

        def feed_forward(base, size):
            place = part_rows(m, base, size)
            for j in range(nff):
                cols = pl.ds(j * width, width)
                u = dot_nn(n_s[place], wup(j)) + bup_ref[0:1, cols].astype(F32)
                phi = 0.5 + 0.5 * lax.erf(u * INV_SQRT_2)
                f = (u * phi).astype(BF)
                f_t = f.T
                for owner in range(quarter):
                    for part in range(nff):
                        at = (owner * nff + part) * unit
                        lt[part, pl.ds((j * quarter + owner) * unit, unit), place] = (
                            f_t[at:at + unit]
                        )
                rt[R_U + j, place] = (
                    phi + u * (jnp.exp(-0.5 * u * u) * INV_SQRT_2PI)
                ).astype(BF)
                acc[base:base + size] += dot_nn(f, wdown[cols, :])
            hat, scale, result = norm(acc[base:base + size], vec(gain_ref, 1), vec(shift_ref, 1))
            xh2[place] = hat.astype(BF)
            rs[place] = jnp.where(left_lanes(), rs[place], scale)
            yb[place] = result.astype(BF)

        @pl.when(sec == 0)
        def _():
            for part in range(2):
                feed_forward(part * span, span)
                hop_copy(m, part).start()

        @pl.when(sec == 1)
        def _():
            feed_forward(0, rows)

        for copy in out_copies(0, yb, sout_hbm, m):
            copy.start()
        if with_sums:
            @pl.when(sec == 0)
            def _():
                left_copy(m).start()


        @pl.when(sec == 0)
        def _():
            turn_left_sides(m)


    def backward(m, serve):
        r = mrows(m)
        wait_slot(1 - sec, m)
        length = len_ref[2 * hi + m]
        row_scale = jnp.where((sec == 0) | (positions((rows, 1), 0) < length), 1.0, 0.0)
        dy = ab[1 - sec, r].astype(F32) * row_scale
        hat = xh2[r].astype(F32)
        add_bias_grad(9, dy * hat)
        add_bias_grad(11, dy)
        dr2 = norm_back(dy, hat, rs[r, hd:hd + 1], vec(gain_ref, 1))
        dz = dr2.astype(BF)
        rt[R_Z, r] = dz
        if with_sums:
            @pl.when(sec == 0)
            def _():
                right_copy(m).start()

        add_bias_grad(3, dz.astype(F32))
        acc[...] = dr2
        serve(0, 1)
        for j in range(nff):
            cols = pl.ds(j * width, width)
            du = (dot_nt(rt[R_Z, r], wdown[cols, :]) * rt[R_U + j, r].astype(F32)).astype(BF)
            rt[R_U + j, r] = du
            bg[4 + j] += jnp.sum(du.astype(F32), axis=0, keepdims=True)
            acc[...] += dot_nt(du, wup(j))
        serve(1, 3)
        dn1 = acc[...]
        hat = xh1[r].astype(F32)
        add_bias_grad(8, dn1 * hat)
        add_bias_grad(10, dn1)
        grad1 = norm_back(dn1, hat, rs[r, 0:1], vec(gain_ref, 0))
        dr1[...] = grad1
        da = grad1.astype(BF)
        rt[R_A, r] = da
        add_bias_grad(2, da.astype(F32))
        do_s[...] = dot_nt(da, wout[...]).astype(BF)
        serve(3, 5)
        key_bias = jnp.where(positions((keys, 1), 0) < length, 0.0, -1e30)

        def head_pair(group, index):
            p = group * half_pairs + index
            cols = pl.ds(p * LANES, LANES)
            kcols = pl.ds(index * LANES, LANES)
            vcols = pl.ds((half_pairs + index) * LANES, LANES)
            qq = split_heads(q_s[r, cols])
            dd = split_heads(do_s[:, cols])
            kp = kv[m, 0, :, cols]
            pt = jnp.exp(dot_nt(kp, qq) + key_bias - lse[m, p:p + 1])
            dv = dot_nn(pt.astype(BF), dd)
            dpt = dot_nt(kv[m, 1, :, cols], dd)
            sums = jnp.sum(pt * dpt, axis=0, keepdims=True)
            ds = (pt * (dpt - sums)).astype(BF)
            dk = dot_nn(ds, qq)
            dq_t = dot_tn(kp, ds)
            dq_pair = jnp.concatenate([dq_t[0:hd, 0:rows], dq_t[hd:2 * hd, rows:2 * rows]], axis=0)
            rt[R_P, r, cols] = (dq_pair.T * (hd ** -0.5)).astype(BF)
            dkv_own[group, :, kcols] = dk[0:rows]
            dkv_own[group, :, vcols] = dv[0:rows]
            dkv_send[group, :, kcols] = dk[rows:keys].astype(BF)
            dkv_send[group, :, vcols] = dv[rows:keys].astype(BF)

        for group in range(2):
            for index in range(half_pairs):
                head_pair(group, index)
            dkv_copy(m, group).start()
            if group == 0:
                serve(5, EARLY)
        dq = rt[R_P, r]
        add_bias_grad(0, dq.astype(F32))
        dr1[...] += dot_nt(dq, wqkv[:, 0:width])

    def input_grad(m):
        r = mrows(m)
        part = width // 2
        for group in range(2):
            dkv_copy(m, group).wait_recv()
            both = (dkv_own[group] + dkv_recv[m, group].astype(F32)).astype(BF)
            for which in range(2):
                rt[R_P + 1 + which, r, group * part:(group + 1) * part] = (
                    both[:, which * part:(which + 1) * part]
                )
        local_out, remote_out = out_copies(0, yb, sout_hbm, m)
        local_out.wait()
        remote_out.wait_send()

        @pl.when(sec == 0)
        def _():
            for piece_of in range(2):
                hop_copy(m, piece_of).wait_send()

        dx = dr1[...]
        for which in range(1, 3):
            dx = dx + dot_nt(rt[R_P + which, r], wqkv[:, which * width:(which + 1) * width])
        yb[r] = dx.astype(BF)

        @pl.when(sec == 1)
        def _():
            for piece_of in range(2):
                hop_copy(m, piece_of).start()

        @pl.when((m == 0) & (sec == 1))
        def _():
            send_input_grad(m)

        for group in range(2):
            dkv_copy(m, group).wait_send()
        add_bias_grad(1, rt[R_P + 2, r].astype(F32))

    def send_input_grad(m):
        for copy in out_copies(1, yb, sgrad_hbm, m):
            copy.start()

    def send_late_grads():
        @pl.when(sec == 0)
        def _():
            send_input_grad(0)

        send_input_grad(1)


    if with_sums:
        block = count * unit
        two = 2 * unit

        other_z = 4

        def of_down(k):
            return (k == 0) | ((k % 2 == 1) & (k >= 3) & (k < OUT))

        def is_z_first(k):
            return (k == 0) | ((sec == 1) & (k == other_z))

        def is_down(k):
            return (sec == 0) & of_down(k) & (k > 0)

        def slot_of(k, half):
            return jnp.where(k < 4, 4 * nff + 2 * k, 2 * k - 8) + half

        def core_copy(k, i, half):
            return remote(
                core_src.at[k % 2, i], pool.at[slot_of(k, half)],
                core_ss.at[k % 2, i], core_rs.at[k % 4, i], core_dev,
            )

        def y_copy(k, i):
            rows_of = pl.ds(pl.multiple_of(jnp.where(z < count // 2, 1 - i, i) * two, two), two)
            first = jnp.where(k < 4, k - 1, jnp.where(k < QKV, k // 2, k - 4))
            second = k - 1 - jnp.where(k > 4, 1, 0)
            slot = jnp.where(sec == 0, first, second)
            return rows_of, y_buf.at[slot, i], remote(
                pool.at[slot_of(k, 1 - hi), rows_of], y_buf.at[slot, i],
                y_ss.at[slot, i], y_rs.at[slot, i], y_dev,
            )

        def turn_copy(k):
            i = jnp.where(k == 0, 0, 1)
            return remote(turn_src.at[i], turn_buf.at[i], turn_ss.at[i], turn_rs.at[i], y_dev)

        def z_first_jobs(k):
            return ((k, hi), (CHUNKS + jnp.where(k == 0, 0, 1), 1 - hi))

        def piece(k, half, target):
            return pool.at[slot_of(k, half), pl.ds(pl.multiple_of(target * unit, unit), unit)]

        def up_copy(job, k, half, target):
            i = target - 1
            return remote(
                piece(k, half, target), land.at[job, i], z_ss.at[job], z_rs.at[job, i],
                z_dev(jnp.minimum(z + 1, count - 1)),
            )

        def down_copy(job, k, half, target):
            i = (target + count - 1) % LANDINGS
            return remote(
                piece(k, half, target), land.at[job, i], z_ss.at[job], z_rs.at[job, i],
                z_dev(jnp.maximum(z - 1, 0)),
            )

        def add_to(ref, landed):
            ref[...] = (ref[...].astype(F32) + landed[...].astype(F32)).astype(BF)

        def hop(number, job, k, half):
            @pl.when(z == number - 1)
            def _():
                for target in range(count - 1, number - 1, -1):
                    copy = up_copy(job, k, half, target)
                    if number > 1:
                        copy.wait_recv()
                        add_to(piece(k, half, target), land.at[job, target - 1])
                    copy.start()

            @pl.when(z == count - number)
            def _():
                for target in range(0, count - number):
                    copy = down_copy(job, k, half, target)
                    if number > 1:
                        copy.wait_recv()
                        add_to(piece(k, half, target), land.at[job, (target + count - 1) % LANDINGS])
                    copy.start()

        def arrive(job, k, half):
            out[k] = piece(k, half, z)[...].astype(F32)

            @pl.when(z > 0)
            def _():
                up_copy(job, k, half, jnp.maximum(z, 1)).wait_recv()
                out[k] += land[job, jnp.maximum(z, 1) - 1].astype(F32)

            @pl.when(z < count - 1)
            def _():
                down_copy(job, k, half, z).wait_recv()
                out[k] += land[job, (z + count - 1) % LANDINGS].astype(F32)

        def product(k, number):
            left = jnp.where(of_down(k), L_F + k // 2, L_N)
            left = jnp.where(k < OUT, left, jnp.where(k == OUT, L_O, L_X))
            right = jnp.where(of_down(k), R_Z, R_U + k // 2)
            right = jnp.where(k < OUT, right, jnp.where(k == OUT, R_A, R_P + k - QKV))
            base = pl.multiple_of(number * block, block)
            return dot_nn(lt[left, pl.ds(base, block), :], rt[right])

        def down_product(k, core):
            part = k // 2
            own_rows = pl.ds(pl.multiple_of((hi * 2 + core) * block, block), block)
            rows_y = pl.ds(pl.multiple_of(core * block, block), block)
            return dot_nn(lt[L_F + part, own_rows, :], rt[R_Z]) + dot_nn(
                lt_y[part, rows_y, :], dz_y[...]
            )

        def for_core(k):
            @pl.when((k >= 2) & is_down(k - 2))
            def _():
                core_copy(k - 2, 0, hi).wait_send()

            @pl.when((k >= 2) & jnp.logical_not(is_down(k - 2)))
            def _():
                for half in range(2):
                    core_copy(k - 2, half, half).wait_send()

            @pl.when((sec == 0) & (k == 3))
            def _():
                for m in range(MICRO):
                    left_copy(m).wait_recv()
                    right_copy(m).wait_recv()

            @pl.when(is_down(k))
            def _():
                core_src[k % 2, 0] = down_product(k, 1 - lo).astype(BF)
                core_copy(k, 0, hi).start()

            @pl.when(jnp.logical_not(is_down(k)))
            def _():
                for half in range(2):
                    core_src[k % 2, half] = product(k, half * 2 + 1 - lo).astype(BF)
                    core_copy(k, half, half).start()

        def chip_sum(k):
            @pl.when(is_down(k))
            def _():
                core_copy(k, 0, hi).wait_recv()
                slot = slot_of(k, hi)
                pool[slot] = (down_product(k, lo) + pool[slot].astype(F32)).astype(BF)
                hop(1, k, k, hi)

            @pl.when(jnp.logical_not(is_down(k)))
            def _():
                for half in range(2):
                    core_copy(k, half, half).wait_recv()
                    slot = slot_of(k, half)
                    pool[slot] = (product(k, half * 2 + lo) + pool[slot].astype(F32)).astype(BF)

                @pl.when(is_z_first(k))
                def _():
                    for job, half in z_first_jobs(k):
                        hop(1, job, k, half)

                @pl.when(jnp.logical_not(is_z_first(k)))
                def _():
                    for i in range(2):
                        y_copy(k, i)[2].start()

        def from_y(k):
            for i in range(2):
                rows_of, landed, copy = y_copy(k, i)
                copy.wait_recv()
                add_to(pool.at[slot_of(k, hi), rows_of], landed)

                @pl.when(z == 0)
                def _(i=i):
                    for target in ((3, 2), (1,))[i]:
                        up_copy(k, k, hi, target).start()

                @pl.when(z == count - 1)
                def _(i=i):
                    for target in ((0, 1), (2,))[i]:
                        down_copy(k, k, hi, target).start()

        def finished(k):
            arrive(k, k, hi)
            part_copy(k).start()

        def sent(job):
            others = land.at[job, pl.ds(0, count - 1)]
            pltpu.make_async_copy(others, others, z_ss.at[job]).wait()

        def drain(k):
            sent(k)

            @pl.when(jnp.logical_not(is_z_first(k) | is_down(k)))
            def _():
                for i in range(2):
                    y_copy(k, i)[2].wait_send()

        def part_copy(k):
            return pltpu.make_async_copy(out.at[k], out_hbm.at[k], part_sem)

        def bias_core():
            return remote(b_src.at[0], b_core, bc_ss.at[0], bc_rs.at[0], core_dev)

        def bias_y():
            return remote(b_src.at[1], b_y, bc_ss.at[1], bc_rs.at[1], y_dev)

        def bias_z(by):
            return remote(
                b_src.at[2], b_z.at[by - 1], bz_ss.at[by - 1], bz_rs.at[by - 1],
                z_dev((z + by) % count),
            )

        def sum_step(t):
            @pl.when(t < CHUNKS)
            def _():
                for_core(t)

            @pl.when(((t >= 2) & (t <= CHUNKS)) | (t == 0))
            def _():
                chip_sum(jnp.maximum(t - 1, 0))

            def at(tables, action):
                k = -1
                for section, table in enumerate(tables):
                    for when, chunk in table.items():
                        k = jnp.where((sec == section) & (t == when), chunk, k)

                @pl.when(k >= 0)
                def _():
                    action(k)

            def both_halves(number, k):
                for job, half in z_first_jobs(k):
                    hop(number, job, k, half)

            def turn(k):
                stays, goes = z_first_jobs(k)
                arrive(goes[0], k, goes[1])
                turn_src[jnp.where(k == 0, 0, 1)] = out[k].astype(BF)
                turn_copy(k).start()
                arrive(stays[0], k, stays[1])

            at(FROM_Y, from_y)
            at(THIRD, lambda k: hop(3, k, k, hi))
            at(SECOND, lambda k: hop(2, k, k, hi))

            at(Z_THIRD, lambda k: both_halves(3, k))
            at(Z_SECOND, lambda k: both_halves(2, k))

            at(ARRIVE, finished)

            @pl.when((t >= 14) & (t < 14 + LAST))
            def _():
                drain(t - 14)

            @pl.when(t == CHUNKS + 1)
            def _():
                send_late_grads()

            at(TURN, turn)

            @pl.when(t == EARLY)
            def _():
                b_src[0] = bg[...]
                bias_core().start()

            @pl.when(t == EARLY + 1)
            def _():
                bias_core().wait_recv()
                b_src[1] = b_src[0] + b_core[...]
                bias_y().start()

            @pl.when(t == 16)
            def _():
                bias_y().wait_recv()
                b_src[2] = b_src[1] + b_y[...]
                for by in range(1, count):
                    bias_z(by).start()

    def one_step(step, carry):
        first = sec == 0

        def among(*steps):
            hit = step == steps[0]
            for value in steps[1:]:
                hit = hit | (step == value)
            return hit

        late_forward = ((step == 3) & first) | ((step == 4) & jnp.logical_not(first))
        early_backward = ((step == 4) & first) | ((step == 3) & jnp.logical_not(first))
        m = jnp.where(among(2, 6, 7) | late_forward, 1, 0)

        def serve(start, stop):
            if with_sums:
                @pl.when((step == 6) & first)
                def _():
                    def body(t, c):
                        sum_step(t)
                        return c

                    lax.fori_loop(start, stop, body, 0)

        @pl.when(among(0, 2))
        def _():
            project(step, m)

        @pl.when((step == 1) | late_forward)
        def _():
            forward(m)

        @pl.when((step == 6) | early_backward)
        def _():
            backward(m, serve)

        @pl.when(among(5, 7))
        def _():
            input_grad(m)

        return carry

    lax.fori_loop(0, 8, one_step, 0)

    @pl.when(sec == 1)
    def _():
        for m in range(MICRO):
            turn_left_sides(m)

    if not with_sums:
        send_late_grads()

    if with_sums:
        def rest(t, carry):
            sum_step(t)
            return carry

        lax.fori_loop(jnp.where(sec == 0, EARLY, 0), STEPS, rest, 0)

        for k in range(LAST, CHUNKS):
            finished(k)
        for i, k in enumerate((0, other_z)):
            @pl.when((sec == 1) | (i == 0))
            def _(i=i, k=k):
                turn_copy(k).wait_recv()
                out[k] += turn_buf[i].astype(F32)
                part_copy(k).start()

        total = b_src[2]
        for by in range(1, count):
            bias_z(by).wait_recv()
            total = total + b_z[by - 1]
        bg_out[...] = total
        bias_core().wait_send()
        bias_y().wait_send()
        for by in range(1, count):
            bias_z(by).wait_send()

        for k in range(LAST, CHUNKS):
            drain(k)
        pltpu.make_async_copy(out, out_hbm, part_sem).wait()
        for i, k in enumerate((0, other_z)):
            @pl.when((sec == 1) | (i == 0))
            def _(i=i, k=k):
                sent(CHUNKS + i)
                turn_copy(k).wait_send()
        for k in (CHUNKS - 2, CHUNKS - 1):
            for half in range(2):
                core_copy(k, half, half).wait_send()

        @pl.when(sec == 0)
        def _():
            for m in range(MICRO):
                left_copy(m).wait_send()
                right_copy(m).wait_send()

    for m in range(MICRO):
        seq_copy(in_hbm, m).wait_send()
        for part in range(2):
            kv_copy(m, part).wait_send()
        out_copies(0, yb, sout_hbm, m)[1].wait_recv()
        local_out, remote_out = out_copies(1, yb, sgrad_hbm, m)
        local_out.wait()
        remote_out.wait()

        @pl.when(sec == 1)
        def _():
            for part in range(2):
                hop_copy(m, part).wait_send()


def run_train(args, with_sums):
    (inputs, cotangent, lengths, w_qkv, attn_bias, w_out, out_bias, w_up, bias_up, w_down,
     norm_gain, norm_bias) = args
    tables, span, width = inputs.shape
    ff = w_up.shape[2]
    rows = 2 * span
    total = MICRO * rows
    keys = 2 * rows
    count = lax.axis_size("dp")
    unit = width // 16
    block = count * unit
    tall = width // 4
    any_spec = pl.BlockSpec(memory_space=pl.ANY)
    vmem = pl.BlockSpec(memory_space=pltpu.VMEM)
    smem = pl.BlockSpec(memory_space=pltpu.SMEM)
    dma = pltpu.SemaphoreType.DMA
    shape = jax.ShapeDtypeStruct
    stacks = (
        ((L_COUNT, width, total), BF),
        ((R_COUNT, total, width), BF),
        ((12, 1, width), F32),
    )
    if with_sums:
        results = (((CHUNKS, unit, width), F32), ((12, 1, width), F32))
    else:
        results = stacks
    scratch = [
        pltpu.VMEM((2, total, width), BF),
        pltpu.VMEM((width, 3 * width), BF),
        pltpu.VMEM((width, width), BF),
        pltpu.VMEM((ff // tall + (8 if with_sums else 0), tall, width), BF),
        pltpu.VMEM((ff, width), BF),
        pltpu.VMEM((total, width), BF),
        pltpu.VMEM((MICRO, 2, keys, width), BF),
        pltpu.VMEM((MICRO, 8, keys), F32),
        pltpu.VMEM((total, width), BF),
        pltpu.VMEM((total, width), BF),
        pltpu.VMEM((total, width), BF),
        pltpu.VMEM((total, width), BF),
        pltpu.VMEM((total, LANES), F32),
        pltpu.VMEM((rows, width), F32),
        pltpu.VMEM((rows, width), F32),
        pltpu.VMEM((rows, width), BF),
        pltpu.VMEM((2, rows, width), F32),
        pltpu.VMEM((2, rows, width), BF),
        pltpu.VMEM((MICRO, 2, rows, width), BF),
        pltpu.VMEM((total, width), BF),
        dma((4,)), dma((MICRO,)), dma((MICRO,)), dma((MICRO,)), dma((MICRO, 2)), dma((MICRO, 2)),
        dma((MICRO, 2)), dma((MICRO, 2)), dma((MICRO, 2)), dma((MICRO, 2)),
        dma((2, MICRO)), dma((2, MICRO)), dma((2, MICRO)),
    ]
    if with_sums:
        scratch += [pltpu.VMEM(dims, kind) for dims, kind in stacks]
        scratch += [
            pltpu.VMEM((CHUNKS, unit, width), F32),
            pltpu.VMEM((ff // width, 2 * block, total), BF),
            pltpu.VMEM((total, width), BF),
            pltpu.VMEM((2, 2, block, width), BF),
            pltpu.VMEM((Y_SLOTS, 2, 2 * unit, width), BF),
            pltpu.VMEM((CHUNKS + Z_FIRST, LANDINGS, unit, width), BF),
            pltpu.VMEM((Z_FIRST, unit, width), BF),
            pltpu.VMEM((Z_FIRST, unit, width), BF),
            pltpu.VMEM((3, 12, 1, width), F32),
            pltpu.VMEM((12, 1, width), F32),
            pltpu.VMEM((12, 1, width), F32),
            pltpu.VMEM((count - 1, 12, 1, width), F32),
            dma((2, 2)), dma((4, 2)), dma((Y_SLOTS, 2)), dma((Y_SLOTS, 2)),
            dma((CHUNKS + Z_FIRST,)), dma((CHUNKS + Z_FIRST, LANDINGS)),
            dma((Z_FIRST,)), dma((Z_FIRST,)),
            dma((2,)), dma((2,)), dma((count - 1,)), dma((count - 1,)), dma,
            dma((MICRO,)), dma((MICRO,)), dma((MICRO,)), dma((MICRO,)),
        ]
    return pl.pallas_call(
        functools.partial(train_kernel, with_sums),
        name="train",
        out_shape=(shape((tables, span, width), BF), shape((tables, span, width), BF))
        + tuple(shape(dims, kind) for dims, kind in results),
        in_specs=[smem] + [any_spec] * 6 + [vmem] * 5,
        out_specs=(any_spec, any_spec)
        + ((any_spec, vmem) if with_sums else (vmem,) * len(results)),
        scratch_shapes=scratch,
        compiler_params=pltpu.CompilerParams(
            collective_id=0, has_side_effects=True, vmem_limit_bytes=VMEM_LIMIT
        ),
    )(lengths, inputs, cotangent, w_qkv, w_out, w_up, w_down,
      attn_bias, out_bias, bias_up, norm_gain, norm_bias)


def grads_by_scatter(lt, rt, bg, ff):
    width = lt.shape[1]
    parts = ff // width

    def scatter(full):
        return lax.psum_scatter(
            full.astype(BF), ("seq", "dp"), scatter_dimension=0, tiled=True
        ).astype(F32)

    left_f = lt[:parts].reshape(parts, 4, 4, width // 16, -1).transpose(1, 2, 0, 3, 4)
    down = scatter(dot_nn(left_f.reshape(ff, -1), rt[R_Z]))
    up = scatter(jnp.concatenate([dot_nn(lt[L_N], rt[R_U + j]) for j in range(parts)], axis=1))
    wout = scatter(dot_nn(lt[L_O], rt[R_A]))
    qkv = scatter(jnp.concatenate([dot_nn(lt[L_X], rt[R_P + j]) for j in range(3)], axis=1))
    return qkv, wout, up, down, lax.psum(bg, ("seq", "dp"))


def finish_kernel(
    sout, sgrad, grads, sums_hbm,
    sout_ref, sgrad_ref, qkv_ref, abias_ref, wout_ref, obias_ref, up_ref, bup_ref, down_ref,
    gain_ref, shift_ref,
    kept, low, wide_grad, parts, sums, sem,
):
    unit, width = grads.shape[1:]
    size = abias_ref.shape[1]

    def copy(i, src, dst):
        started = pltpu.make_async_copy(src, dst, sem.at[i])
        started.start()
        return started

    sums_in = copy(0, sums_hbm, sums)
    grad_in = copy(1, sgrad, low)
    out_in = copy(2, sout, kept)
    parts_in = [copy(6 + CHUNKS + k, grads.at[k], parts.at[k]) for k in range(CHUNKS)]
    grad_in.wait()
    wide_grad[...] = low[...].astype(F32)
    copies = [copy(4, wide_grad, sgrad_ref.at[0])]
    out_in.wait()
    copies.append(copy(5, kept, sout_ref.at[0]))
    for k in range(CHUNKS):
        parts_in[k].wait()
        if k in (0, 3, 5, 7):
            dst = down_ref.at[0, pl.ds(k // 2 * unit, unit), :]
        elif k < OUT:
            dst = up_ref.at[0, :, pl.ds(k // 2 * width, width)]
        elif k == OUT:
            dst = wout_ref.at[0]
        else:
            dst = qkv_ref.at[0, :, pl.ds((k - QKV) * width, width)]
        copies.append(copy(6 + k, parts.at[k], dst))
    sums_in.wait()
    index = lax.axis_index("seq") * lax.axis_size("dp") + lax.axis_index("dp")
    whole = width // size
    pairs = [jnp.where(index < whole, sums[row], sums[row + 1]) for row in (0, 2, 8, 10)]
    block = jnp.concatenate(pairs + pairs, axis=0)
    block = pltpu.roll(block, (width - (index % whole) * size) % width, axis=1)
    for row, ref in enumerate((abias_ref, obias_ref, gain_ref, shift_ref)):
        ref[...] = block[row:row + 1, 0:size]
    wide = 2 * size
    per = width // wide
    rows = sums[4]
    for row in range(1, 4):
        rows = jnp.where(index // per == row, sums[4 + row], rows)
    rows = pltpu.roll(
        jnp.concatenate([rows] * 8, axis=0), (width - (index % per) * wide) % width, axis=1
    )
    bup_ref[...] = rows[0:1, 0:wide]
    for started in copies:
        started.wait()


def run_finish(sout, sgrad, grads, sums):
    unit, width = grads.shape[1:]
    size = width // 8
    vmem = pl.BlockSpec(memory_space=pltpu.VMEM)
    any_spec = pl.BlockSpec(memory_space=pl.ANY)
    shape = jax.ShapeDtypeStruct
    return pl.pallas_call(
        finish_kernel,
        name="finish",
        out_shape=(
            shape((1,) + sout.shape, BF),
            shape((1,) + sgrad.shape, F32),
            shape((1, unit, 3 * width), F32),
            shape((1, size), F32),
            shape((1, unit, width), F32),
            shape((1, size), F32),
            shape((1, unit, 4 * width), F32),
            shape((1, 2 * size), F32),
            shape((1, 4 * unit, width), F32),
            shape((1, size), F32),
            shape((1, size), F32),
        ),
        in_specs=[any_spec] * 4,
        out_specs=(any_spec, any_spec, any_spec, vmem, any_spec, vmem, any_spec, vmem, any_spec,
                   vmem, vmem),
        scratch_shapes=[
            pltpu.VMEM(sout.shape, BF),
            pltpu.VMEM(sgrad.shape, BF),
            pltpu.VMEM(sgrad.shape, F32),
            pltpu.VMEM(grads.shape, F32),
            pltpu.VMEM(sums.shape, F32),
            pltpu.SemaphoreType.DMA((6 + 2 * CHUNKS,)),
        ],
        compiler_params=pltpu.CompilerParams(vmem_limit_bytes=VMEM_LIMIT),
    )(sout, sgrad, grads, sums)


def local(*args):
    if lax.axis_size("dp") == 4:
        sout, sgrad, out, sums = run_train(args, True)
        return run_finish(sout, sgrad, out, sums)
    sout, sgrad, lt, rt, bg = run_train(args, False)
    width = lt.shape[1]
    ff = args[7].shape[2]
    index = lax.axis_index("seq") * lax.axis_size("dp") + lax.axis_index("dp")
    count = lax.axis_size("seq") * lax.axis_size("dp")
    qkv, wout, up, down, sums = grads_by_scatter(lt, rt, bg, ff)
    sums = sums.reshape(-1)

    def piece(start, rows):
        part = sums[start * width:(start + rows) * width]
        size = rows * width // count
        return lax.dynamic_slice_in_dim(part, index * size, size, 0)[None]

    return (
        sout[None],
        sgrad.astype(F32)[None],
        qkv[None],
        piece(0, 2),
        wout[None],
        piece(2, 2),
        up[None],
        piece(4, 4),
        down[None],
        piece(8, 2),
        piece(10, 2),
    )


def solution(mesh):
    return jax.shard_map(
        local,
        mesh=mesh,
        in_specs=(
            P("dp", "seq", None),
            P("dp", "seq", None),
            P("dp"),
            P("section", None, None),
            P("section", None),
            P("section", None, None),
            P("section", None),
            P("section", None, None),
            P("section", None),
            P("section", None, None),
            P("section", None),
            P("section", None),
        ),
        out_specs=(
            P("section", "dp", "seq", None),
            P("section", "dp", "seq", None),
            P("section", ("seq", "dp"), None),
            P("section", ("seq", "dp")),
            P("section", ("seq", "dp"), None),
            P("section", ("seq", "dp")),
            P("section", ("seq", "dp"), None),
            P("section", ("seq", "dp")),
            P("section", ("seq", "dp"), None),
            P("section", ("seq", "dp")),
            P("section", ("seq", "dp")),
        ),
        check_vma=False,
    )
```
